32 devices in a mesh: parts: 2 (over x), wide: 4 (over y, core), narrow: 4 (over z).
Axes of the slice: x: 2, y: 2, z: 4, core: 2. Of those that a mesh axis runs over, the one named last changes fastest.
Arguments:
- hidden: bfloat16 [512, 2560], P(('parts', 'wide'), 'narrow'), parts along dimension 0, may hold values from -64 to 64
- input_norm_gain: float32 [2560], replicated, may hold values from 0.25 to 1.75
- query_projection_weight: bfloat16 [2560, 4096], P(None, 'narrow'), may hold values from -0.125 to 0.125
- key_projection_weight: bfloat16 [2560, 1024], P(None, 'narrow'), may hold values from -0.125 to 0.125
- value_projection_weight: bfloat16 [2560, 1024], P(None, 'narrow'), may hold values from -0.125 to 0.125
- query_norm_gain: float32 [128], replicated, may hold values from 0.25 to 1.75
- key_norm_gain: float32 [128], replicated, may hold values from 0.25 to 1.75
- output_projection_weight: bfloat16 [4096, 2560], P('narrow'), may hold values from -0.09375 to 0.09375
- stacked_down_factors: bfloat16 [64, 192, 2560], P(('parts', 'wide'), None, 'narrow'), parts along dimension 0, may hold values from -0.125 to 0.125
- query_up_factor: bfloat16 [64, 64, 4096], P(('parts', 'wide'), None, 'narrow'), parts along dimension 0, may hold values from -0.75 to 0.75
- key_up_factor: bfloat16 [64, 64, 1024], P(('parts', 'wide'), None, 'narrow'), parts along dimension 0, may hold values from -0.75 to 0.75
- value_up_factor: bfloat16 [64, 64, 1024], P(('parts', 'wide'), None, 'narrow'), parts along dimension 0, may hold values from -0.75 to 0.75
- output_down_factor: bfloat16 [64, 64, 4096], P(('parts', 'wide'), None, 'narrow'), parts along dimension 0, may hold values from -0.09375 to 0.09375
- output_up_factor: bfloat16 [64, 64, 2560], P(('parts', 'wide'), None, 'narrow'), parts along dimension 0, may hold values from -0.75 to 0.75
- cached_key_rows: bfloat16 [512, 8, 24, 128], P(('parts', 'wide'), 'narrow'), parts along dimension 0, may hold values from -170 to 170
- cached_value_rows: bfloat16 [512, 8, 24, 128], P(('parts', 'wide'), 'narrow'), parts along dimension 0, may hold values from -5 to 5
- cached_length_rows: int32 [512], P(('parts', 'wide')), parts along dimension 0, may hold values from 1 to 24, as said below
- domain_of_row: int32 [512], P('parts'), parts along dimension 0, may hold values from 0 to 31, as said below
- slot_of_domain: int32 [64], P('parts'), parts along dimension 0, may hold values from 0 to 31, as said below
Outputs:
- final_state: bfloat16 [512, 2560], P(('parts', 'wide'), 'narrow'), parts along dimension 0
The draws below stay inside these ranges and needn't reach their ends.
There are 2 independent parts, one for each index of `parts`. The reference program is written for one: setup_inputs(seed, part) draws one part's arguments, and reference() takes and returns one part's arrays. A program takes and returns all parts, laid end to end along the dimension named above; an argument that names none is the same for every part. Nothing has to cross between parts.
Inputs may be any that keep to these rules, and one draw needn't show every extreme that they name: Domain d's adapter sits at slot slot_of_domain[d]; slots g * 8 to (g + 1) * 8 - 1 belong to serving group g. Each slot holds one domain. `domain_of_row`: in each aligned block of 64 rows (the rows of one serving group), at most 16 rows have domains whose slots belong to any one serving group; in every draw one serving group receives exactly 16 rows from every block. `cached_length_rows`: each aligned block of 64 rows holds a row with 24 valid positions.
All inputs are finite; a program needn't handle non-finite values.
Results may differ from the reference program's by a relative error of at most 0.024.
Values may be sent and summed in bfloat16 or wider, within the bound.
No kernel may reach another device: no remote copies, remote signals or barrier semaphores. Data moves between devices by JAX's collectives and lax.ppermute only.
A program may use at most 128 MiB of HBM per device.

```python
import jax
import jax.numpy as jnp
from jax import lax

MODEL_WIDTH = 2560
QUERY_HEAD_COUNT = 32
KEY_VALUE_HEADS = 8
HEAD_SIZE = 128
ADAPTER_RANK = 64
STEPS = 4
ROW_GROUP = 64
CTX = 24
DOM_GROUP = 8
CAP = 16
ROWS = 256
DOMAIN_COUNT = 32
N_NARROW = 4


def route_tables(key):
    slot_seed, hot_seed, block_seed = jax.random.split(key, 3)
    groups = DOMAIN_COUNT // DOM_GROUP
    slot_of = jax.random.permutation(slot_seed, DOMAIN_COUNT).astype(jnp.int32)
    domain_at = jnp.zeros((DOMAIN_COUNT,), jnp.int32).at[slot_of].set(jnp.arange(DOMAIN_COUNT, dtype=jnp.int32))
    hottest = jax.random.randint(hot_seed, (), 0, groups).astype(jnp.int32)

    def one_block(index):
        block_key = jax.random.fold_in(block_seed, index)
        pick_seed, order_seed, local_seed = jax.random.split(block_key, 3)
        others = jax.random.permutation(pick_seed, (groups - 1) * CAP)[:ROW_GROUP - CAP] // CAP
        targets = jnp.concatenate([jnp.full((CAP,), hottest, jnp.int32), ((hottest + 1 + others) % groups).astype(jnp.int32)])
        targets = jax.random.permutation(order_seed, targets)
        local_pick = jax.random.randint(local_seed, (ROW_GROUP,), 0, DOM_GROUP).astype(jnp.int32)
        return domain_at[targets * DOM_GROUP + local_pick]
    blocks = jax.vmap(one_block)(jnp.arange(ROWS // ROW_GROUP))
    return (slot_of, blocks.reshape(ROWS).astype(jnp.int32))


def draw_slot_of_domain(key, part):
    return route_tables(key)[0]


def draw_domain_of_row(key, part):
    return route_tables(key)[1]


def draw_cached_length_rows(key, part):
    key = jax.random.fold_in(key, 5)
    length_seed, pick_seed = jax.random.split(key, 2)
    lengths = jax.random.randint(length_seed, (ROWS,), 1, CTX + 1)
    forced = jax.random.randint(pick_seed, (ROWS // ROW_GROUP,), 0, ROW_GROUP)
    index = jnp.arange(ROWS)
    chosen = index % ROW_GROUP == jnp.repeat(forced, ROW_GROUP)
    return jnp.where(chosen, CTX, lengths).astype(jnp.int32)


def draw_hidden(key, part):
    key = jax.random.fold_in(key, 7)
    base_seed, row_seed = jax.random.split(key, 2)
    columns = jnp.arange(MODEL_WIDTH, dtype=jnp.float32) / MODEL_WIDTH
    column_scale = 10.0 ** (columns - 0.5)
    base = jnp.clip(jax.random.normal(base_seed, (ROWS, MODEL_WIDTH), jnp.float32), -4.0, 4.0)
    row_scale = 10.0 ** jax.random.uniform(row_seed, (ROWS, 1), jnp.float32, -0.5, 0.5)
    return (base * row_scale * column_scale).astype(jnp.bfloat16)


def draw_cached_key_rows(key, part):
    key = jax.random.fold_in(key, 11)
    base_seed = jax.random.fold_in(key, 0)
    array_shape = (ROWS, KEY_VALUE_HEADS, CTX, HEAD_SIZE)
    base = jnp.clip(jax.random.normal(base_seed, array_shape, jnp.float32), -4.0, 4.0)
    return base.astype(jnp.bfloat16)


def block_levels(rng, dims, cuts, smallest, top_value):
    def one(axis_at, shards_of):
        heights = jax.random.uniform(jax.random.fold_in(jax.random.fold_in(rng, 6), axis_at), (shards_of,), jnp.float32, smallest / len(cuts), top_value / len(cuts))
        return jnp.repeat(jnp.exp(heights), dims[axis_at] // shards_of).reshape((-1,) + (1,) * (len(dims) - axis_at - 1))

    level = one(*cuts[0])
    for cut in cuts[1:]:
        level = level * one(*cut)
    return level


def scatter_about(rng, shape, deviation, reach, cuts=(), kind=jnp.bfloat16):
    level = block_levels(rng, shape, cuts, -0.22, 0.18) if cuts else 1.0
    result = jax.random.normal(rng, shape, jnp.float32) * deviation * level
    return jnp.minimum(jnp.maximum(result, -reach), reach).astype(kind)


def setup_inputs(seed: int = 0, part: int = 0) -> dict:
    key_list = jax.random.split(jax.random.key(seed), 20)
    own_keys = jax.random.split(jax.random.fold_in(key_list[19], part), 20)
    hidden = draw_hidden(jax.random.fold_in(jax.random.fold_in(key_list[19], part), 71), part)
    input_norm_gain = jnp.clip(1.0 + 0.15 * jax.random.normal(key_list[1], (MODEL_WIDTH,), jnp.float32), 0.25, 1.75)
    query_projection_weight = scatter_about(key_list[2], (MODEL_WIDTH, QUERY_HEAD_COUNT * HEAD_SIZE), MODEL_WIDTH ** -0.5, 0.125, ((1, 4),))
    key_projection_weight = scatter_about(key_list[3], (MODEL_WIDTH, KEY_VALUE_HEADS * HEAD_SIZE), MODEL_WIDTH ** -0.5, 0.125, ((1, 4),))
    value_projection_weight = scatter_about(key_list[4], (MODEL_WIDTH, KEY_VALUE_HEADS * HEAD_SIZE), MODEL_WIDTH ** -0.5, 0.125, ((1, 4),))
    query_norm_gain = jnp.clip(1.0 + 0.15 * jax.random.normal(key_list[5], (HEAD_SIZE,), jnp.float32), 0.25, 1.75)
    key_norm_gain = jnp.clip(1.0 + 0.15 * jax.random.normal(key_list[6], (HEAD_SIZE,), jnp.float32), 0.25, 1.75)
    output_projection_weight = scatter_about(key_list[7], (QUERY_HEAD_COUNT * HEAD_SIZE, MODEL_WIDTH), (QUERY_HEAD_COUNT * HEAD_SIZE) ** -0.5, 0.09375, ((0, 4),))
    stacked_down_factors = scatter_about(own_keys[8], (DOMAIN_COUNT, 3 * ADAPTER_RANK, MODEL_WIDTH), MODEL_WIDTH ** -0.5, 0.125, ((0, 4), (2, 4)))
    query_up_factor = scatter_about(own_keys[9], (DOMAIN_COUNT, ADAPTER_RANK, QUERY_HEAD_COUNT * HEAD_SIZE), ADAPTER_RANK ** -0.5, 0.75, ((0, 4), (2, 4)))
    key_up_factor = scatter_about(own_keys[10], (DOMAIN_COUNT, ADAPTER_RANK, KEY_VALUE_HEADS * HEAD_SIZE), ADAPTER_RANK ** -0.5, 0.75, ((0, 4), (2, 4)))
    value_up_factor = scatter_about(own_keys[11], (DOMAIN_COUNT, ADAPTER_RANK, KEY_VALUE_HEADS * HEAD_SIZE), ADAPTER_RANK ** -0.5, 0.75, ((0, 4), (2, 4)))
    output_down_factor = scatter_about(own_keys[12], (DOMAIN_COUNT, ADAPTER_RANK, QUERY_HEAD_COUNT * HEAD_SIZE), (QUERY_HEAD_COUNT * HEAD_SIZE) ** -0.5, 0.09375, ((0, 4), (2, 4)))
    output_up_factor = scatter_about(own_keys[13], (DOMAIN_COUNT, ADAPTER_RANK, MODEL_WIDTH), ADAPTER_RANK ** -0.5, 0.75, ((0, 4), (2, 4)))
    cached_key_rows = draw_cached_key_rows(jax.random.fold_in(jax.random.fold_in(key_list[19], part), 71), part)
    cached_value_rows = scatter_about(own_keys[15], (ROWS, KEY_VALUE_HEADS, CTX, HEAD_SIZE), 1.0, 5.0, ((0, 4), (1, 4)))
    cached_length_rows = draw_cached_length_rows(jax.random.fold_in(jax.random.fold_in(key_list[19], part), 71), part)
    domain_of_row = draw_domain_of_row(jax.random.fold_in(jax.random.fold_in(key_list[19], part), 71), part)
    slot_of_domain = draw_slot_of_domain(jax.random.fold_in(jax.random.fold_in(key_list[19], part), 71), part)
    return dict(hidden=hidden, input_norm_gain=input_norm_gain, query_projection_weight=query_projection_weight, key_projection_weight=key_projection_weight, value_projection_weight=value_projection_weight, query_norm_gain=query_norm_gain, key_norm_gain=key_norm_gain, output_projection_weight=output_projection_weight, stacked_down_factors=stacked_down_factors, query_up_factor=query_up_factor, key_up_factor=key_up_factor, value_up_factor=value_up_factor, output_down_factor=output_down_factor, output_up_factor=output_up_factor, cached_key_rows=cached_key_rows, cached_value_rows=cached_value_rows, cached_length_rows=cached_length_rows, domain_of_row=domain_of_row, slot_of_domain=slot_of_domain)


epsilon = 1e-06
rope_base = 1000000.0

def head_norm(values, gain):
    return values * lax.rsqrt(lax.optimization_barrier(jnp.mean(values * values, axis=-1, keepdims=True)) + epsilon) * gain

def rotate(values, positions):
    half = values.shape[-1] // 2
    frequency = rope_base ** (-(jnp.arange(half, dtype=jnp.float32) * 2.0) / values.shape[-1])
    angles = positions[:, None, None] * frequency
    cosine = jnp.cos(angles)
    sine = jnp.sin(angles)
    first = values[..., :half]
    second = values[..., half:]
    return jnp.concatenate([first * cosine - second * sine, second * cosine + first * sine], axis=-1)

def attend(query, keys_cached, values_cached, keys_fresh, values_fresh, lengths, step):
    scale = query.shape[-1] ** (-0.5)
    cached = jnp.einsum('rkgd,rkjd->rkgj', query.astype(jnp.float32), keys_cached.astype(jnp.float32)) * scale
    fresh = jnp.einsum('rkgd,rkjd->rkgj', query.astype(jnp.float32), keys_fresh.astype(jnp.float32)) * scale
    valid_cache = (jnp.arange(keys_cached.shape[2])[None, :] < lengths[:, None])[:, None, None, :]
    valid_fresh = (jnp.arange(keys_fresh.shape[2]) <= step)[None, None, None, :]
    cached = jnp.where(valid_cache, cached, -1e+30)
    fresh = jnp.where(valid_fresh, fresh, -1e+30)
    largest = jnp.maximum(lax.optimization_barrier(jnp.max(cached, axis=-1, keepdims=True)), lax.optimization_barrier(jnp.max(fresh, axis=-1, keepdims=True)))
    cached = jnp.where(valid_cache, jnp.exp(cached - largest), 0.0)
    fresh = jnp.where(valid_fresh, jnp.exp(fresh - largest), 0.0)
    total = lax.optimization_barrier(jnp.sum(cached, axis=-1, keepdims=True)) + lax.optimization_barrier(jnp.sum(fresh, axis=-1, keepdims=True))
    cached = (cached / total).astype(jnp.bfloat16)
    fresh = (fresh / total).astype(jnp.bfloat16)
    mixed = jnp.einsum('rkgj,rkjd->rkgd', cached.astype(jnp.float32), values_cached.astype(jnp.float32))
    mixed = mixed + jnp.einsum('rkgj,rkjd->rkgd', fresh.astype(jnp.float32), values_fresh.astype(jnp.float32))
    return mixed.astype(jnp.bfloat16).reshape(query.shape[0], -1)

def adapter_of_row(row, slot, down, ups):
    matrix = lax.dynamic_index_in_dim(down, slot, 0, keepdims=False)
    reduced = jnp.dot(matrix, row, preferred_element_type=jnp.float32).astype(jnp.bfloat16)
    rank = ups[0].shape[1]
    pieces = []
    for index, upper in enumerate(ups):
        factor = reduced[index * rank:(index + 1) * rank]
        table = lax.dynamic_index_in_dim(upper, slot, 0, keepdims=False)
        pieces.append(jnp.dot(factor, table, preferred_element_type=jnp.float32).astype(jnp.bfloat16))
    return jnp.concatenate(pieces)

def reference(hidden, input_norm_gain, query_projection_weight, key_projection_weight, value_projection_weight, query_norm_gain, key_norm_gain, output_projection_weight, stacked_down_factors, query_up_factor, key_up_factor, value_up_factor, output_down_factor, output_up_factor, cached_key_rows, cached_value_rows, cached_length_rows, domain_of_row, slot_of_domain):
    adapter_slots = jnp.take(slot_of_domain, domain_of_row).astype(jnp.int32)
    blocks = ROWS // ROW_GROUP
    per_kv = QUERY_HEAD_COUNT // KEY_VALUE_HEADS
    query_width = QUERY_HEAD_COUNT * HEAD_SIZE
    key_width = KEY_VALUE_HEADS * HEAD_SIZE
    share = query_width // N_NARROW
    keys_fresh = jnp.zeros((ROWS, KEY_VALUE_HEADS, STEPS, HEAD_SIZE), jnp.bfloat16)
    values_fresh = jnp.zeros((ROWS, KEY_VALUE_HEADS, STEPS, HEAD_SIZE), jnp.bfloat16)
    positions_base = cached_length_rows.astype(jnp.float32)
    state = hidden
    for step in range(STEPS):
        flat = state.astype(jnp.float32)
        normed_input = (flat * lax.rsqrt(lax.optimization_barrier(jnp.mean(flat * flat, axis=1, keepdims=True)) + epsilon) * input_norm_gain).astype(jnp.bfloat16)
        adapter_delta = lax.map(lambda slot_pair: adapter_of_row(slot_pair[0], slot_pair[1], stacked_down_factors, (query_up_factor, key_up_factor, value_up_factor)), (normed_input, adapter_slots))
        query_now = jnp.dot(normed_input, query_projection_weight, preferred_element_type=jnp.float32) + adapter_delta[:, :query_width].astype(jnp.float32)
        key_now = jnp.dot(normed_input, key_projection_weight, preferred_element_type=jnp.float32) + adapter_delta[:, query_width:query_width + key_width].astype(jnp.float32)
        value_now = (jnp.dot(normed_input, value_projection_weight, preferred_element_type=jnp.float32) + adapter_delta[:, query_width + key_width:].astype(jnp.float32)).astype(jnp.bfloat16)
        positions = positions_base + step
        query_heads = rotate(head_norm(query_now.reshape(ROWS, QUERY_HEAD_COUNT, HEAD_SIZE), query_norm_gain), positions).astype(jnp.bfloat16)
        key_heads = rotate(head_norm(key_now.reshape(ROWS, KEY_VALUE_HEADS, HEAD_SIZE), key_norm_gain), positions).astype(jnp.bfloat16)
        keys_fresh = keys_fresh.at[:, :, step].set(key_heads)
        values_fresh = values_fresh.at[:, :, step].set(value_now.reshape(ROWS, KEY_VALUE_HEADS, HEAD_SIZE))

        def block_attend(parts):
            return attend(parts[0], parts[1], parts[2], parts[3], parts[4], parts[5], step)
        attended_output = lax.map(block_attend, (query_heads.reshape(blocks, ROW_GROUP, KEY_VALUE_HEADS, per_kv, HEAD_SIZE), cached_key_rows.reshape(blocks, ROW_GROUP, KEY_VALUE_HEADS, CTX, HEAD_SIZE), cached_value_rows.reshape(blocks, ROW_GROUP, KEY_VALUE_HEADS, CTX, HEAD_SIZE), keys_fresh.reshape(blocks, ROW_GROUP, KEY_VALUE_HEADS, STEPS, HEAD_SIZE), values_fresh.reshape(blocks, ROW_GROUP, KEY_VALUE_HEADS, STEPS, HEAD_SIZE), cached_length_rows.reshape(blocks, ROW_GROUP))).reshape(ROWS, query_width)
        output_delta = lax.map(lambda slot_pair: adapter_of_row(slot_pair[0], slot_pair[1], output_down_factor, (output_up_factor,)), (attended_output, adapter_slots))
        projected = jnp.zeros((ROWS, MODEL_WIDTH), jnp.float32)
        for piece in range(N_NARROW):
            term = jnp.dot(attended_output[:, piece * share:(piece + 1) * share], output_projection_weight[piece * share:(piece + 1) * share], preferred_element_type=jnp.float32).astype(jnp.bfloat16)
            projected = projected + lax.optimization_barrier(term).astype(jnp.float32)
        state = (flat + projected + output_delta.astype(jnp.float32)).astype(jnp.bfloat16)
    return state
```

```python
import functools

import jax
import jax.numpy as jnp
from jax import lax
from jax.experimental import pallas as pl
from jax.experimental.pallas import tpu as pltpu
from jax.sharding import PartitionSpec as P

STEPS = 4

epsilon = 1e-06
rope_base = 1000000.0
blocked = -1e30
f32 = jnp.float32
bf16 = jnp.bfloat16

NT = (((1,), (1,)), ((), ()))


def vmem_specs(count):
    return [pl.BlockSpec(memory_space=pltpu.VMEM)] * count


def kernel_params(mib):
    return pltpu.CompilerParams(vmem_limit_bytes=mib * 1024 * 1024)


def pack_kernel(
    domain_ref, slot_ref, key_ref, value_ref, key_out, value_out, target_ref, local_ref, count, sems
):
    rows = key_ref.shape[0]
    groups, _, capacity = key_out.shape[:3]
    per_group = slot_ref.shape[0] // groups
    for group in range(groups):
        count[group] = 0

    def place(row, carry):
        slot = slot_ref[domain_ref[row]]
        dest = lax.div(slot, per_group)
        position = jnp.minimum(count[dest], capacity - 1)
        count[dest] = position + 1
        target_ref[row] = dest * capacity + position
        local_ref[row] = slot - dest * per_group
        pltpu.make_async_copy(
            key_ref.at[row], key_out.at[dest, :, position], sems.at[0, row]
        ).start()
        pltpu.make_async_copy(
            value_ref.at[row], value_out.at[dest, :, position], sems.at[1, row]
        ).start()
        return carry

    lax.fori_loop(0, rows, place, 0)

    def finish(row, carry):
        pltpu.make_async_copy(key_ref.at[row], key_out.at[0, :, 0], sems.at[0, row]).wait()
        pltpu.make_async_copy(value_ref.at[row], value_out.at[0, :, 0], sems.at[1, row]).wait()
        return carry

    lax.fori_loop(0, rows, finish, 0)


def pack_rows(domains, slots, keys, values, groups, capacity):
    rows, kv_local, context, head_dim = keys.shape
    moved = jax.ShapeDtypeStruct((groups, kv_local, capacity, context, head_dim), keys.dtype)
    number = jax.ShapeDtypeStruct((rows,), jnp.int32)
    smem = pl.BlockSpec(memory_space=pltpu.SMEM)
    anywhere = pl.BlockSpec(memory_space=pl.ANY)
    return pl.pallas_call(
        pack_kernel,
        out_shape=(moved, moved, number, number),
        in_specs=[smem, smem, anywhere, anywhere],
        out_specs=(anywhere, anywhere, smem, smem),
        scratch_shapes=[
            pltpu.SMEM((groups,), jnp.int32),
            pltpu.SemaphoreType.DMA((2, rows)),
        ],
        name="pack_rows",
    )(domains, slots, keys, values)


def one_of_slots(slot_column, total):
    ids = lax.broadcasted_iota(jnp.int32, (1, total), 1).astype(f32)
    return slot_column == ids


def spread_over_slots(factor, chosen, total):
    return jnp.concatenate(
        [jnp.where(chosen[:, d : d + 1], factor, 0.0) for d in range(total)], axis=1
    ).astype(bf16)


def pick_slot(product, chosen, total):
    rank = product.shape[1] // total
    picked = jnp.where(chosen[:, 0:1], product[:, :rank], 0.0)
    for d in range(1, total):
        picked = picked + jnp.where(chosen[:, d : d + 1], product[:, d * rank : (d + 1) * rank], 0.0)
    return picked


def partial_low(state, gain, chosen, down_ref, total):
    scaled = (state * gain).astype(bf16)
    product = lax.dot_general(scaled, down_ref[...], NT, preferred_element_type=f32)
    return pick_slot(product, chosen, total).astype(bf16)


def enter_kernel(total, state_ref, gain_ref, down_ref, send_ref):
    width = down_ref.shape[1]
    state = state_ref[:, :width].astype(f32)
    slot = state_ref[:, width + 1 : width + 2].astype(f32)
    chosen = one_of_slots(slot, total)
    low = partial_low(state, gain_ref[...], chosen, down_ref, total)
    for n in range(send_ref.shape[0]):
        send_ref[n, :, :width] = state_ref[:, :width]
        send_ref[n, :, width:] = low


def new_state(total, chosen, received_ref, state_ref, up_ref, width):
    parts = received_ref.shape[0]
    low_out = received_ref[0, :, width:].astype(f32)
    projected = received_ref[0, :, :width].astype(f32)
    for n in range(1, parts):
        low_out = low_out + received_ref[n, :, width:].astype(f32)
        projected = projected + received_ref[n, :, :width].astype(f32)
    spread = spread_over_slots(low_out, chosen, total)
    delta = jnp.dot(spread, up_ref[...], preferred_element_type=f32).astype(bf16)
    return (state_ref[...].astype(f32) + projected + delta.astype(f32)).astype(bf16)


def between_kernel(
    total, received_ref, state_ref, slot_ref, up_ref, gain_ref, down_ref, state_out, send_ref
):
    width = down_ref.shape[1]
    chosen = one_of_slots(slot_ref[:, 1:2].astype(f32), total)
    state = new_state(total, chosen, received_ref, state_ref, up_ref, width)
    state_out[...] = state
    low = partial_low(state.astype(f32), gain_ref[...], chosen, down_ref, total)
    for n in range(send_ref.shape[0]):
        send_ref[n, :, :width] = state
        send_ref[n, :, width:] = low


def leave_kernel(total, received_ref, state_ref, slot_ref, up_ref, state_out):
    width = state_ref.shape[1]
    chosen = one_of_slots(slot_ref[:, 1:2].astype(f32), total)
    state_out[...] = new_state(total, chosen, received_ref, state_ref, up_ref, width)


def norm_and_rotate(vector, gain, cosine, sine):
    head_dim = vector.shape[1]
    mean = jnp.mean(vector * vector, axis=1, keepdims=True)
    scaled = vector * lax.rsqrt(mean + epsilon) * gain
    return (scaled * cosine + pltpu.roll(scaled, head_dim // 2, 1) * sine).astype(bf16)


def step_kernel(total, step, *refs):
    (
        gathered_ref,
        slot_ref,
        gain_ref,
        query_weight,
        key_weight,
        value_weight,
        query_up,
        key_up,
        value_up,
        query_gain,
        key_gain,
        cosine_ref,
        sine_ref,
        bias_ref,
        key_cache,
        value_cache,
    ) = refs[:16]
    earlier = refs[16 : 16 + 2 * step]
    output_weight, output_down = refs[16 + 2 * step : 18 + 2 * step]
    send_ref, key_fresh, value_fresh, attended = refs[18 + 2 * step :]
    parts, rows, wide = gathered_ref.shape
    features = gain_ref.shape[1]
    width = features // parts
    rank = query_up.shape[0] // total
    groups, kv_local, keys_block, head_dim = key_cache.shape
    capacity = rows // groups
    heads = query_weight.shape[1] // head_dim
    per_kv = heads // kv_local

    chosen = one_of_slots(slot_ref[:, 1:2].astype(f32), total)
    state = [gathered_ref[n, :, :width].astype(f32) for n in range(parts)]
    squares = jnp.sum(state[0] * state[0], axis=1, keepdims=True)
    low = gathered_ref[0, :, width:].astype(f32)
    for n in range(1, parts):
        squares = squares + jnp.sum(state[n] * state[n], axis=1, keepdims=True)
        low = low + gathered_ref[n, :, width:].astype(f32)
    inverse = lax.rsqrt(squares / features + epsilon)
    low = low * inverse
    normed = [
        (state[n] * inverse * gain_ref[:, n * width : (n + 1) * width]).astype(bf16)
        for n in range(parts)
    ]

    def project(weight_ref, up_ref, index):
        spread = spread_over_slots(low[:, index * rank : (index + 1) * rank], chosen, total)
        delta = jnp.dot(spread, up_ref[...], preferred_element_type=f32).astype(bf16)
        result = delta.astype(f32)
        for n in range(parts):
            result = result + jnp.dot(
                normed[n],
                weight_ref[n * width : (n + 1) * width, :],
                preferred_element_type=f32,
            )
        return result

    cosine = cosine_ref[step]
    sine = sine_ref[step]
    key = project(key_weight, key_up, 1)
    value = project(value_weight, value_up, 2).astype(bf16)
    for g in range(kv_local):
        columns = slice(g * head_dim, (g + 1) * head_dim)
        key_fresh[g] = norm_and_rotate(key[:, columns], key_gain[...], cosine, sine)
        value_fresh[g] = value[:, columns]
    query = project(query_weight, query_up, 0)
    query_heads = [
        norm_and_rotate(query[:, h * head_dim : (h + 1) * head_dim], query_gain[...], cosine, sine)
        for h in range(heads)
    ]

    scale = head_dim ** (-0.5)
    fresh_count = (step + 1) * capacity
    key_row = lax.broadcasted_iota(jnp.int32, (per_kv * capacity, fresh_count), 1) % capacity
    own_row = lax.broadcasted_iota(jnp.int32, (per_kv * capacity, fresh_count), 0) % capacity
    same_row = key_row == own_row
    for b in range(groups):
        block = slice(b * capacity, (b + 1) * capacity)
        bias = jnp.concatenate([bias_ref[block, :]] * per_kv, axis=0)
        for g in range(kv_local):
            queries = jnp.concatenate(
                [query_heads[g * per_kv + h][block] for h in range(per_kv)], axis=0
            )
            fresh_keys = jnp.concatenate(
                [earlier[2 * t][g, block, :] for t in range(step)] + [key_fresh[g, block, :]], axis=0
            )
            fresh_values = jnp.concatenate(
                [earlier[2 * t + 1][g, block, :] for t in range(step)] + [value_fresh[g, block, :]],
                axis=0,
            )
            cached = (
                lax.dot_general(queries, key_cache[b, g], NT, preferred_element_type=f32) * scale
                + bias
            )
            fresh = lax.dot_general(queries, fresh_keys, NT, preferred_element_type=f32) * scale
            fresh = jnp.where(same_row, fresh, blocked)
            largest = jnp.maximum(
                jnp.max(cached, axis=1, keepdims=True), jnp.max(fresh, axis=1, keepdims=True)
            )
            cached = jnp.exp(cached - largest)
            fresh = jnp.exp(fresh - largest)
            sums = jnp.sum(cached, axis=1, keepdims=True) + jnp.sum(fresh, axis=1, keepdims=True)
            mixed = jnp.dot(cached.astype(bf16), value_cache[b, g], preferred_element_type=f32)
            mixed = mixed + jnp.dot(fresh.astype(bf16), fresh_values, preferred_element_type=f32)
            mixed = (mixed / sums).astype(bf16)
            for h in range(per_kv):
                head = g * per_kv + h
                attended[block, head * head_dim : (head + 1) * head_dim] = mixed[
                    h * capacity : (h + 1) * capacity
                ]

    attended_rows = attended[...]
    product = lax.dot_general(attended_rows, output_down[...], NT, preferred_element_type=f32)
    low_out = pick_slot(product, chosen, total).astype(bf16)
    for n in range(parts):
        term = jnp.dot(
            attended_rows,
            output_weight[:, n * width : (n + 1) * width],
            preferred_element_type=f32,
        )
        send_ref[n, :, :width] = term.astype(bf16)
        send_ref[n, :, width:] = low_out


def exchange(blocks, axis):
    return lax.all_to_all(blocks, axis, split_axis=0, concat_axis=0, tiled=True)


def shards(
    hidden,
    input_norm_gain,
    query_projection_weight,
    key_projection_weight,
    value_projection_weight,
    query_norm_gain,
    key_norm_gain,
    output_projection_weight,
    stacked_down_factors,
    query_up_factor,
    key_up_factor,
    value_up_factor,
    output_down_factor,
    output_up_factor,
    cached_key_rows,
    cached_value_rows,
    cached_length_rows,
    domain_of_row,
    slot_of_domain,
):
    groups = lax.axis_size("wide")
    parts = lax.axis_size("narrow")
    wide_index = lax.axis_index("wide")
    narrow_index = lax.axis_index("narrow")
    row_group, width = hidden.shape
    capacity = row_group // 4
    rows = groups * capacity
    total = stacked_down_factors.shape[0]
    low_width = stacked_down_factors.shape[1]
    rank = output_up_factor.shape[1]
    _, kv_local, context, head_dim = cached_key_rows.shape
    features = input_norm_gain.shape[0]
    query_width = query_projection_weight.shape[1]

    domains = lax.dynamic_slice_in_dim(domain_of_row, wide_index * row_group, row_group)
    key_blocks, value_blocks, target, local = pack_rows(
        domains, slot_of_domain, cached_key_rows, cached_value_rows, groups, capacity
    )
    place = jnp.arange(rows)[:, None] == target[None, :]
    column = jnp.arange(128)[None, :]
    facts = jnp.where(
        column == 0, cached_length_rows[:, None], jnp.where(column == 1, local[:, None], 0)
    ).astype(bf16)
    outgoing = jnp.dot(
        place.astype(bf16), jnp.concatenate([hidden, facts], axis=1), preferred_element_type=f32
    ).astype(bf16)
    arrived = exchange(outgoing.reshape(groups, capacity, width + 128), "wide").reshape(
        rows, width + 128
    )
    key_cache = exchange(key_blocks, "wide").reshape(groups, kv_local, capacity * context, head_dim)
    value_cache = exchange(value_blocks, "wide").reshape(
        groups, kv_local, capacity * context, head_dim
    )

    state = arrived[:, :width]
    facts_here = arrived[:, width:]
    lengths = facts_here[:, 0].astype(f32)
    frequency = rope_base ** (-(jnp.arange(head_dim // 2, dtype=f32) * 2.0) / head_dim)
    positions = lengths[None, :] + jnp.arange(STEPS, dtype=f32)[:, None]
    angles = positions[:, :, None] * frequency
    cosine = jnp.cos(angles)
    sine = jnp.sin(angles)
    cosine = jnp.concatenate([cosine, cosine], axis=-1)
    sine = jnp.concatenate([-sine, sine], axis=-1)
    key_index = jnp.arange(capacity * context)[None, :]
    visible = (key_index // context == (jnp.arange(rows) % capacity)[:, None]) & (
        (key_index % context).astype(f32) < lengths[:, None]
    )
    bias = jnp.where(visible, 0.0, blocked).astype(f32)

    gain_row = input_norm_gain.reshape(1, features)
    gain_slice = lax.dynamic_slice_in_dim(gain_row, narrow_index * width, width, axis=1)
    down = stacked_down_factors.reshape(total * low_width, width)
    query_up = query_up_factor.reshape(total * rank, query_width)
    key_up = key_up_factor.reshape(total * rank, -1)
    value_up = value_up_factor.reshape(total * rank, -1)
    output_down = output_down_factor.reshape(total * rank, query_width)
    output_up = output_up_factor.reshape(total * rank, width)
    query_gain = query_norm_gain.reshape(1, head_dim)
    key_gain = key_norm_gain.reshape(1, head_dim)

    sent_state = jax.ShapeDtypeStruct((parts, rows, width + low_width), bf16)
    sent_terms = jax.ShapeDtypeStruct((parts, rows, width + rank), bf16)
    state_slice = jax.ShapeDtypeStruct((rows, width), bf16)
    fresh = jax.ShapeDtypeStruct((kv_local, rows, head_dim), bf16)

    send = pl.pallas_call(
        functools.partial(enter_kernel, total),
        out_shape=sent_state,
        in_specs=vmem_specs(3),
        out_specs=vmem_specs(1)[0],
        compiler_params=kernel_params(48),
        name="enter",
    )(arrived, gain_slice, down)

    earlier = []
    for step in range(STEPS):
        gathered = exchange(send, "narrow")
        terms, key_fresh, value_fresh = pl.pallas_call(
            functools.partial(step_kernel, total, step),
            out_shape=(sent_terms, fresh, fresh),
            in_specs=vmem_specs(18 + 2 * step),
            out_specs=tuple(vmem_specs(3)),
            scratch_shapes=[pltpu.VMEM((rows, query_width), bf16)],
            compiler_params=kernel_params(48),
            name="attend_step",
        )(
            gathered,
            facts_here,
            gain_row,
            query_projection_weight,
            key_projection_weight,
            value_projection_weight,
            query_up,
            key_up,
            value_up,
            query_gain,
            key_gain,
            cosine,
            sine,
            bias,
            key_cache,
            value_cache,
            *earlier,
            output_projection_weight,
            output_down,
        )
        earlier += [key_fresh, value_fresh]
        received = exchange(terms, "narrow")
        if step < STEPS - 1:
            state, send = pl.pallas_call(
                functools.partial(between_kernel, total),
                out_shape=(state_slice, sent_state),
                in_specs=vmem_specs(6),
                out_specs=tuple(vmem_specs(2)),
                compiler_params=kernel_params(48),
                name="between",
            )(received, state, facts_here, output_up, gain_slice, down)
        else:
            state = pl.pallas_call(
                functools.partial(leave_kernel, total),
                out_shape=state_slice,
                in_specs=vmem_specs(4),
                out_specs=vmem_specs(1)[0],
                compiler_params=kernel_params(48),
                name="leave",
            )(received, state, facts_here, output_up)

    back = exchange(state.reshape(groups, capacity, width), "wide").reshape(rows, width)
    return lax.dot_general(
        place.astype(bf16), back, (((0,), (0,)), ((), ())), preferred_element_type=f32
    ).astype(bf16)


def solution(mesh):
    placed = (
        P(("parts", "wide"), "narrow"),
        P(),
        P(None, "narrow"),
        P(None, "narrow"),
        P(None, "narrow"),
        P(),
        P(),
        P("narrow", None),
        P(("parts", "wide"), None, "narrow"),
        P(("parts", "wide"), None, "narrow"),
        P(("parts", "wide"), None, "narrow"),
        P(("parts", "wide"), None, "narrow"),
        P(("parts", "wide"), None, "narrow"),
        P(("parts", "wide"), None, "narrow"),
        P(("parts", "wide"), "narrow", None, None),
        P(("parts", "wide"), "narrow", None, None),
        P(("parts", "wide")),
        P("parts"),
        P("parts"),
    )
    return jax.shard_map(
        shards,
        mesh=mesh,
        in_specs=placed,
        out_specs=P(("parts", "wide"), "narrow"),
        check_vma=False,
    )
```

```python
import functools

import jax
import jax.numpy as jnp
from jax import lax
from jax.experimental import pallas as pl
from jax.experimental.pallas import tpu as pltpu
from jax.sharding import PartitionSpec as P

STEPS = 4

epsilon = 1e-06
rope_base = 1000000.0
blocked = -1e30
f32 = jnp.float32
bf16 = jnp.bfloat16

NT = (((1,), (1,)), ((), ()))


def kernel_params(mib):
    return pltpu.CompilerParams(vmem_limit_bytes=mib * 1024 * 1024)


def route_kernel(
    group_ref, domain_ref, slot_ref, length_ref, hidden_ref, target_ref, place_ref, *refs
):
    groups = len(refs) - 3
    outgoing = refs[:groups]
    count, place, facts = refs[groups:]
    rows, width = hidden_ref.shape
    capacity = outgoing[0].shape[0]
    per_group = slot_ref.shape[0] // groups
    here = group_ref[0]
    for group in range(groups):
        count[group] = 0
    places = lax.broadcasted_iota(jnp.int32, (1, groups * capacity), 1)
    columns = lax.broadcasted_iota(jnp.int32, (1, facts.shape[1]), 1)

    def put(row, carry):
        slot = slot_ref[domain_ref[here * rows + row]]
        dest = lax.div(slot, per_group)
        position = jnp.minimum(count[dest], capacity - 1)
        count[dest] = position + 1
        target = lax.rem(dest - here + groups, groups) * capacity + position
        target_ref[row] = target
        place[pl.ds(row, 1), :] = jnp.where(places == target, 1.0, 0.0)
        length = length_ref[row].astype(f32)
        local = (slot - dest * per_group).astype(f32)
        facts[pl.ds(row, 1), :] = jnp.where(
            columns == 0, length, jnp.where(columns == 1, local, 0.0)
        )
        return carry

    lax.fori_loop(0, rows, put, 0)
    chosen = place[...].astype(bf16)
    place_ref[...] = chosen
    across = (((0,), (0,)), ((), ()))
    state = lax.dot_general(chosen, hidden_ref[...], across, preferred_element_type=f32)
    known = lax.dot_general(
        chosen, facts[...].astype(bf16), across, preferred_element_type=f32
    )
    for s in range(groups):
        block = slice(s * capacity, (s + 1) * capacity)
        outgoing[s][:, :width] = state[block].astype(bf16)
        outgoing[s][:, width:] = known[block].astype(bf16)


def pack_kernel(target_ref, key_ref, value_ref, *refs):
    groups = len(refs) - 1
    outgoing, packed = refs[:groups], refs[groups]
    rows, kv_local = key_ref.shape[:2]
    capacity = packed.shape[2]
    if groups * capacity > rows:
        packed[...] = jnp.zeros_like(packed)

    def put(row, carry):
        target = target_ref[row]
        block = lax.div(target, capacity)
        position = target - block * capacity
        for g in range(kv_local):
            packed[block, g, position] = key_ref[row, g]
            packed[block, kv_local + g, position] = value_ref[row, g]
        return carry

    lax.fori_loop(0, rows, put, 0)
    for s in range(groups):
        outgoing[s][...] = packed[s]


def one_of_slots(slot_column, total):
    ids = lax.broadcasted_iota(jnp.int32, (1, total), 1).astype(f32)
    return slot_column == ids


def spread_over_slots(factor, chosen, total):
    return jnp.concatenate(
        [jnp.where(chosen[:, d : d + 1], factor, 0.0) for d in range(total)], axis=1
    ).astype(bf16)


def pick_slot(product, chosen, total):
    rank = product.shape[1] // total
    picked = jnp.where(chosen[:, 0:1], product[:, :rank], 0.0)
    for d in range(1, total):
        picked = picked + jnp.where(chosen[:, d : d + 1], product[:, d * rank : (d + 1) * rank], 0.0)
    return picked


def partial_low(state, gain, chosen, down_ref, total):
    scaled = (state * gain).astype(bf16)
    product = lax.dot_general(scaled, down_ref[...], NT, preferred_element_type=f32)
    return pick_slot(product, chosen, total).astype(bf16)


def enter_kernel(total, state_ref, gain_ref, down_ref, send_ref):
    width = down_ref.shape[1]
    state = state_ref[:, :width].astype(f32)
    slot = state_ref[:, width + 1 : width + 2].astype(f32)
    chosen = one_of_slots(slot, total)
    send_ref[:, :width] = state_ref[:, :width]
    send_ref[:, width:] = partial_low(state, gain_ref[...], chosen, down_ref, total)


def new_state(total, chosen, received, state, up_ref):
    width = state.shape[1]
    low_out = received[0][:, width:].astype(f32)
    projected = received[0][:, :width].astype(f32)
    for part in received[1:]:
        low_out = low_out + part[:, width:].astype(f32)
        projected = projected + part[:, :width].astype(f32)
    spread = spread_over_slots(low_out, chosen, total)
    delta = jnp.dot(spread, up_ref[...], preferred_element_type=f32).astype(bf16)
    return (state.astype(f32) + projected + delta.astype(f32)).astype(bf16)


def between_kernel(total, parts, *refs):
    received = refs[:parts]
    state_ref, slot_ref, up_ref, gain_ref, down_ref, send_ref = refs[parts:]
    width = down_ref.shape[1]
    chosen = one_of_slots(slot_ref[:, 1:2].astype(f32), total)
    state = new_state(total, chosen, received, state_ref[:, :width], up_ref)
    send_ref[:, :width] = state
    send_ref[:, width:] = partial_low(state.astype(f32), gain_ref[...], chosen, down_ref, total)


def leave_kernel(total, parts, *refs):
    received = refs[:parts]
    state_ref, slot_ref, up_ref = refs[parts : parts + 3]
    outgoing = refs[parts + 3 :]
    width = up_ref.shape[1]
    capacity = outgoing[0].shape[0]
    chosen = one_of_slots(slot_ref[:, 1:2].astype(f32), total)
    state = new_state(total, chosen, received, state_ref[:, :width], up_ref)
    for s in range(len(outgoing)):
        outgoing[s][...] = state[s * capacity : (s + 1) * capacity]


def restore_kernel(place_ref, *refs):
    blocks, out_ref = refs[:-1], refs[-1]
    back = jnp.concatenate([block[...] for block in blocks], axis=0)
    out_ref[...] = jnp.dot(place_ref[...], back, preferred_element_type=f32).astype(bf16)


def norm_and_rotate(vector, gain, cosine, sine):
    head_dim = vector.shape[1]
    mean = jnp.mean(vector * vector, axis=1, keepdims=True)
    scaled = vector * lax.rsqrt(mean + epsilon) * gain
    return (scaled * cosine + pltpu.roll(scaled, head_dim // 2, 1) * sine).astype(bf16)


def step_kernel(total, step, parts, groups, *refs):
    refs = list(refs)

    def take(count):
        taken = refs[:count]
        del refs[:count]
        return taken

    gathered = take(parts)
    (
        index_ref,
        slot_ref,
        gain_ref,
        query_weight,
        key_weight,
        value_weight,
        query_up,
        key_up,
        value_up,
        query_gain,
        key_gain,
        cosine_ref,
        sine_ref,
        bias_ref,
    ) = take(14)
    cache = take(groups)
    earlier = take(2 * step)
    output_weight, output_down = take(2)
    outgoing = take(parts)
    key_fresh, value_fresh, attended, terms = refs
    features = parts * gain_ref.shape[2]
    width = features // parts
    rows = gathered[0].shape[0]
    rank = query_up.shape[0] // total
    head_dim = cache[0].shape[2]
    kv_local = cache[0].shape[0] // 2
    capacity = rows // groups
    heads = query_weight.shape[1] // head_dim
    per_kv = heads // kv_local
    here = index_ref[0]

    chosen = one_of_slots(slot_ref[:, 1:2].astype(f32), total)
    state = [gathered[s][:, :width].astype(f32) for s in range(parts)]
    squares = jnp.sum(state[0] * state[0], axis=1, keepdims=True)
    low = gathered[0][:, width:].astype(f32)
    for s in range(1, parts):
        squares = squares + jnp.sum(state[s] * state[s], axis=1, keepdims=True)
        low = low + gathered[s][:, width:].astype(f32)
    inverse = lax.rsqrt(squares / features + epsilon)
    low = low * inverse
    source = [lax.rem(here - s + parts, parts) for s in range(parts)]
    normed = [(state[s] * inverse * gain_ref[source[s]]).astype(bf16) for s in range(parts)]

    def project(weight_ref, up_ref, index):
        spread = spread_over_slots(low[:, index * rank : (index + 1) * rank], chosen, total)
        delta = jnp.dot(spread, up_ref[...], preferred_element_type=f32).astype(bf16)
        result = delta.astype(f32)
        for s in range(parts):
            features_there = pl.ds(pl.multiple_of(source[s] * width, 64), width)
            result = result + jnp.dot(
                normed[s], weight_ref[features_there, :], preferred_element_type=f32
            )
        return result

    cosine = cosine_ref[step]
    sine = sine_ref[step]
    key = project(key_weight, key_up, 1)
    value = project(value_weight, value_up, 2).astype(bf16)
    for g in range(kv_local):
        columns = slice(g * head_dim, (g + 1) * head_dim)
        key_fresh[g] = norm_and_rotate(key[:, columns], key_gain[...], cosine, sine)
        value_fresh[g] = value[:, columns]
    query = project(query_weight, query_up, 0)
    query_heads = [
        norm_and_rotate(query[:, h * head_dim : (h + 1) * head_dim], query_gain[...], cosine, sine)
        for h in range(heads)
    ]

    scale = head_dim ** (-0.5)
    fresh_count = (step + 1) * capacity
    key_row = lax.broadcasted_iota(jnp.int32, (per_kv * capacity, fresh_count), 1) % capacity
    own_row = lax.broadcasted_iota(jnp.int32, (per_kv * capacity, fresh_count), 0) % capacity
    same_row = key_row == own_row
    for b in range(groups):
        block = slice(b * capacity, (b + 1) * capacity)
        bias = jnp.concatenate([bias_ref[block, :]] * per_kv, axis=0)
        for g in range(kv_local):
            queries = jnp.concatenate(
                [query_heads[g * per_kv + h][block] for h in range(per_kv)], axis=0
            )
            fresh_keys = jnp.concatenate(
                [earlier[2 * t][g, block, :] for t in range(step)] + [key_fresh[g, block, :]], axis=0
            )
            fresh_values = jnp.concatenate(
                [earlier[2 * t + 1][g, block, :] for t in range(step)] + [value_fresh[g, block, :]],
                axis=0,
            )
            cached = (
                lax.dot_general(queries, cache[b][g], NT, preferred_element_type=f32) * scale
                + bias
            )
            fresh = lax.dot_general(queries, fresh_keys, NT, preferred_element_type=f32) * scale
            fresh = jnp.where(same_row, fresh, blocked)
            largest = jnp.maximum(
                jnp.max(cached, axis=1, keepdims=True), jnp.max(fresh, axis=1, keepdims=True)
            )
            cached = jnp.exp(cached - largest)
            fresh = jnp.exp(fresh - largest)
            sums = jnp.sum(cached, axis=1, keepdims=True) + jnp.sum(fresh, axis=1, keepdims=True)
            mixed = jnp.dot(cached.astype(bf16), cache[b][kv_local + g], preferred_element_type=f32)
            mixed = mixed + jnp.dot(fresh.astype(bf16), fresh_values, preferred_element_type=f32)
            mixed = (mixed / sums).astype(bf16)
            for h in range(per_kv):
                head = g * per_kv + h
                attended[block, head * head_dim : (head + 1) * head_dim] = mixed[
                    h * capacity : (h + 1) * capacity
                ]

    attended_rows = attended[...]
    product = lax.dot_general(attended_rows, output_down[...], NT, preferred_element_type=f32)
    low_out = pick_slot(product, chosen, total).astype(bf16)
    for n in range(parts):
        term = jnp.dot(
            attended_rows,
            output_weight[:, n * width : (n + 1) * width],
            preferred_element_type=f32,
        )
        terms[lax.rem(n - here + parts, parts)] = term.astype(bf16)
    for s in range(parts):
        outgoing[s][:, :width] = terms[s]
        outgoing[s][:, width:] = low_out


def shift(block, axis, by):
    size = lax.axis_size(axis)
    return lax.ppermute(block, axis, [(i, (i + by) % size) for i in range(size)])


def shards(
    hidden,
    input_norm_gain,
    query_projection_weight,
    key_projection_weight,
    value_projection_weight,
    query_norm_gain,
    key_norm_gain,
    output_projection_weight,
    stacked_down_factors,
    query_up_factor,
    key_up_factor,
    value_up_factor,
    output_down_factor,
    output_up_factor,
    cached_key_rows,
    cached_value_rows,
    cached_length_rows,
    domain_of_row,
    slot_of_domain,
):
    groups = lax.axis_size("wide")
    parts = lax.axis_size("narrow")
    wide_index = lax.axis_index("wide")
    narrow_index = lax.axis_index("narrow")
    row_group, width = hidden.shape
    capacity = row_group // 4
    rows = groups * capacity
    total = stacked_down_factors.shape[0]
    low_width = stacked_down_factors.shape[1]
    rank = output_up_factor.shape[1]
    _, kv_local, context, head_dim = cached_key_rows.shape
    features = input_norm_gain.shape[0]
    query_width = query_projection_weight.shape[1]

    smem = pl.BlockSpec(memory_space=pltpu.SMEM)
    vmem = pl.BlockSpec(memory_space=pltpu.VMEM)
    outgoing_shape = jax.ShapeDtypeStruct((capacity, width + 128), bf16)
    target, place, *outgoing = pl.pallas_call(
        route_kernel,
        out_shape=[
            jax.ShapeDtypeStruct((row_group,), jnp.int32),
            jax.ShapeDtypeStruct((row_group, rows), bf16),
        ]
        + [outgoing_shape] * groups,
        in_specs=[smem] * 4 + [vmem],
        out_specs=[smem] + [vmem] * (groups + 1),
        scratch_shapes=[
            pltpu.SMEM((groups,), jnp.int32),
            pltpu.VMEM((row_group, rows), f32),
            pltpu.VMEM((row_group, 128), f32),
        ],
        compiler_params=kernel_params(8),
        name="route_rows",
    )(wide_index.reshape(1), domain_of_row, slot_of_domain, cached_length_rows, hidden)
    arrived = jnp.concatenate(
        [outgoing[0]] + [shift(outgoing[s], "wide", s) for s in range(1, groups)], axis=0
    )
    packed_shape = (2 * kv_local, capacity, context, head_dim)
    packed = pl.pallas_call(
        pack_kernel,
        out_shape=[jax.ShapeDtypeStruct(packed_shape, bf16)] * groups,
        in_specs=[smem, vmem, vmem],
        out_specs=[vmem] * groups,
        scratch_shapes=[pltpu.VMEM((groups,) + packed_shape, bf16)],
        compiler_params=kernel_params(16),
        name="pack_cache",
    )(target, cached_key_rows, cached_value_rows)
    cache = [packed[0]] + [shift(packed[s], "wide", s) for s in range(1, groups)]
    cache = [block.reshape(2 * kv_local, capacity * context, head_dim) for block in cache]

    facts_here = arrived[:, width:]
    lengths = facts_here[:, 0].astype(f32)
    frequency = rope_base ** (-(jnp.arange(head_dim // 2, dtype=f32) * 2.0) / head_dim)
    positions = lengths[None, :] + jnp.arange(STEPS, dtype=f32)[:, None]
    angles = positions[:, :, None] * frequency
    cosine = jnp.cos(angles)
    sine = jnp.sin(angles)
    cosine = jnp.concatenate([cosine, cosine], axis=-1)
    sine = jnp.concatenate([-sine, sine], axis=-1)
    key_index = jnp.arange(capacity * context)[None, :]
    visible = (key_index // context == (jnp.arange(rows) % capacity)[:, None]) & (
        (key_index % context).astype(f32) < lengths[:, None]
    )
    bias = jnp.where(visible, 0.0, blocked).astype(f32)

    gain_rows = input_norm_gain.reshape(parts, 1, width)
    gain_slice = lax.dynamic_index_in_dim(gain_rows, narrow_index, 0, keepdims=False)
    down = stacked_down_factors.reshape(total * low_width, width)
    query_up = query_up_factor.reshape(total * rank, query_width)
    key_up = key_up_factor.reshape(total * rank, -1)
    value_up = value_up_factor.reshape(total * rank, -1)
    output_down = output_down_factor.reshape(total * rank, query_width)
    output_up = output_up_factor.reshape(total * rank, width)
    query_gain = query_norm_gain.reshape(1, head_dim)
    key_gain = key_norm_gain.reshape(1, head_dim)

    sent_state = jax.ShapeDtypeStruct((rows, width + low_width), bf16)
    sent_terms = jax.ShapeDtypeStruct((rows, width + rank), bf16)
    fresh = jax.ShapeDtypeStruct((kv_local, rows, head_dim), bf16)

    send = pl.pallas_call(
        functools.partial(enter_kernel, total),
        out_shape=sent_state,
        in_specs=[vmem] * 3,
        out_specs=vmem,
        compiler_params=kernel_params(8),
        name="enter",
    )(arrived, gain_slice, down)

    earlier = []
    for step in range(STEPS):
        gathered = [send] + [shift(send, "narrow", s) for s in range(1, parts)]
        *terms, key_fresh, value_fresh = pl.pallas_call(
            functools.partial(step_kernel, total, step, parts, groups),
            out_shape=[sent_terms] * parts + [fresh] * 2,
            in_specs=[vmem] * parts + [smem] + [vmem] * (15 + groups + 2 * step),
            out_specs=[vmem] * (parts + 2),
            scratch_shapes=[
                pltpu.VMEM((rows, query_width), bf16),
                pltpu.VMEM((parts, rows, width), bf16),
            ],
            compiler_params=kernel_params(24),
            name="attend_step",
        )(
            *gathered,
            narrow_index.reshape(1),
            facts_here,
            gain_rows,
            query_projection_weight,
            key_projection_weight,
            value_projection_weight,
            query_up,
            key_up,
            value_up,
            query_gain,
            key_gain,
            cosine,
            sine,
            bias,
            *cache,
            *earlier,
            output_projection_weight,
            output_down,
        )
        earlier += [key_fresh, value_fresh]
        received = [terms[0]] + [shift(terms[s], "narrow", s) for s in range(1, parts)]
        if step < STEPS - 1:
            send = pl.pallas_call(
                functools.partial(between_kernel, total, parts),
                out_shape=sent_state,
                in_specs=[vmem] * (parts + 5),
                out_specs=vmem,
                compiler_params=kernel_params(8),
                name="between",
            )(*received, send, facts_here, output_up, gain_slice, down)
        else:
            leaving = pl.pallas_call(
                functools.partial(leave_kernel, total, parts),
                out_shape=[jax.ShapeDtypeStruct((capacity, width), bf16)] * groups,
                in_specs=[vmem] * (parts + 3),
                out_specs=[vmem] * groups,
                compiler_params=kernel_params(8),
                name="leave",
            )(*received, send, facts_here, output_up)

    back = [leaving[0]] + [shift(leaving[s], "wide", -s) for s in range(1, groups)]
    return pl.pallas_call(
        restore_kernel,
        out_shape=jax.ShapeDtypeStruct((row_group, width), bf16),
        in_specs=[vmem] * (groups + 1),
        out_specs=vmem,
        compiler_params=kernel_params(8),
        name="restore",
    )(place, *back)


def solution(mesh):
    placed = (
        P(("parts", "wide"), "narrow"),
        P(),
        P(None, "narrow"),
        P(None, "narrow"),
        P(None, "narrow"),
        P(),
        P(),
        P("narrow", None),
        P(("parts", "wide"), None, "narrow"),
        P(("parts", "wide"), None, "narrow"),
        P(("parts", "wide"), None, "narrow"),
        P(("parts", "wide"), None, "narrow"),
        P(("parts", "wide"), None, "narrow"),
        P(("parts", "wide"), None, "narrow"),
        P(("parts", "wide"), "narrow", None, None),
        P(("parts", "wide"), "narrow", None, None),
        P(("parts", "wide")),
        P("parts"),
        P("parts"),
    )
    return jax.shard_map(
        shards,
        mesh=mesh,
        in_specs=placed,
        out_specs=P(("parts", "wide"), "narrow"),
        check_vma=False,
    )
```

```python
import functools

import jax
import jax.numpy as jnp
from jax import lax
from jax.experimental import pallas as pl
from jax.experimental.pallas import tpu as pltpu
from jax.sharding import PartitionSpec as P

STEPS = 4

epsilon = 1e-06
rope_base = 1000000.0
blocked = -1e30
f32 = jnp.float32
bf16 = jnp.bfloat16

NT = (((1,), (1,)), ((), ()))


def kernel_params(mib):
    return pltpu.CompilerParams(vmem_limit_bytes=mib * 1024 * 1024)


def copy_all(pairs, sems):
    copies = [
        pltpu.make_async_copy(source, target, sems.at[index])
        for index, (source, target) in enumerate(pairs)
    ]
    for copy in copies:
        copy.start()
    return copies


def route_kernel(
    group_ref, domain_hbm, slot_hbm, length_hbm, hidden_hbm, target_ref, place_ref, *refs
):
    groups = len(refs) - 8
    outgoing = refs[:groups]
    count, place, facts, domain_ref, slot_ref, length_ref, hidden_ref, sems = refs[groups:]
    rows, width = hidden_ref.shape
    capacity = outgoing[0].shape[0]
    per_group = slot_ref.shape[0] // groups
    here = group_ref[0]
    *tables, hidden_copy = copy_all(
        [
            (domain_hbm, domain_ref),
            (slot_hbm, slot_ref),
            (length_hbm, length_ref),
            (hidden_hbm, hidden_ref),
        ],
        sems,
    )
    for group in range(groups):
        count[group] = 0
    places = lax.broadcasted_iota(jnp.int32, (1, groups * capacity), 1)
    columns = lax.broadcasted_iota(jnp.int32, (1, facts.shape[1]), 1)
    for copy in tables:
        copy.wait()

    def put(row, carry):
        slot = slot_ref[domain_ref[here * rows + row]]
        dest = lax.div(slot, per_group)
        position = jnp.minimum(count[dest], capacity - 1)
        count[dest] = position + 1
        target = lax.rem(dest - here + groups, groups) * capacity + position
        target_ref[row] = target
        place[pl.ds(row, 1), :] = jnp.where(places == target, 1.0, 0.0)
        length = length_ref[row].astype(f32)
        local = (slot - dest * per_group).astype(f32)
        facts[pl.ds(row, 1), :] = jnp.where(
            columns == 0, length, jnp.where(columns == 1, local, 0.0)
        )
        return carry

    lax.fori_loop(0, rows, put, 0)
    chosen = place[...].astype(bf16)
    place_ref[...] = chosen
    across = (((0,), (0,)), ((), ()))
    known = lax.dot_general(
        chosen, facts[...].astype(bf16), across, preferred_element_type=f32
    ).astype(bf16)
    hidden_copy.wait()
    state = lax.dot_general(
        chosen, hidden_ref[...], across, preferred_element_type=f32
    ).astype(bf16)
    for s in range(groups):
        block = slice(s * capacity, (s + 1) * capacity)
        outgoing[s][:, :width] = state[block]
        outgoing[s][:, width:] = known[block]


def pack_kernel(target_ref, key_hbm, value_hbm, *refs):
    groups = len(refs) - 4
    outgoing = refs[:groups]
    packed, key_ref, value_ref, sems = refs[groups:]
    rows, kv_local = key_ref.shape[:2]
    capacity = packed.shape[2]
    copies = copy_all([(key_hbm, key_ref), (value_hbm, value_ref)], sems)
    if groups * capacity > rows:
        packed[...] = jnp.zeros_like(packed)
    for copy in copies:
        copy.wait()

    def put(row, carry):
        target = target_ref[row]
        block = lax.div(target, capacity)
        position = target - block * capacity
        for g in range(kv_local):
            packed[block, g, position] = key_ref[row, g]
            packed[block, kv_local + g, position] = value_ref[row, g]
        return carry

    lax.fori_loop(0, rows, put, 0)
    for s in range(groups):
        outgoing[s][...] = packed[s]


def load_kernel(rank, *refs):
    query, key, value, query_up, key_up, value_up, output, output_down, output_up, down = refs[:10]
    inputs, *same, down_out = refs[10:18]
    sems = refs[18]
    total, kinds = down.shape[0], down.shape[1] // rank
    pairs = []
    column = 0
    for weight in (query, key, value):
        width = weight.shape[1]
        pairs.append((weight, inputs.at[:, column : column + width]))
        column += width
    pairs += zip((query_up, key_up, value_up, output, output_down, output_up), same)
    for kind in range(kinds):
        for d in range(total):
            pairs.append(
                (
                    down.at[d, kind * rank : (kind + 1) * rank, :],
                    down_out.at[kind, d * rank : (d + 1) * rank, :],
                )
            )
    for copy in copy_all(pairs, sems):
        copy.wait()


def own_slots(slot, total, rank):
    lane = lax.broadcasted_iota(jnp.int32, (1, 2 * rank), 1)
    second = (lane >= rank).astype(f32)
    return [slot == 2.0 * j + second for j in range(total // 2)]


def spread_over_slots(factor, own):
    twice = jnp.concatenate([factor, factor], axis=1)
    return jnp.concatenate([jnp.where(mask, twice, 0.0).astype(bf16) for mask in own], axis=1)


def pick_slot(product, own):
    wide = own[0].shape[1]
    picked = jnp.where(own[0], product[:, :wide], 0.0)
    for j in range(1, len(own)):
        picked = picked + jnp.where(own[j], product[:, j * wide : (j + 1) * wide], 0.0)
    return picked[:, : wide // 2] + picked[:, wide // 2 :]


def partial_low(state, gain, own, down_ref):
    scaled = (state * gain).astype(bf16)
    picked = []
    for kind in range(down_ref.shape[0]):
        product = lax.dot_general(scaled, down_ref[kind], NT, preferred_element_type=f32)
        picked.append(pick_slot(product, own).astype(bf16))
    return jnp.concatenate(picked, axis=1)


def enter_kernel(total, rank, groups, *refs):
    blocks = refs[:groups]
    gain_ref, down_ref, send_ref, facts_ref = refs[groups:]
    width = down_ref.shape[2]
    everything = jnp.concatenate([block[...] for block in blocks], axis=0)
    facts = everything[:, width:].astype(f32)
    own = own_slots(facts[:, 1:2], total, rank)
    facts_ref[...] = facts
    send_ref[:, :width] = everything[:, :width]
    send_ref[:, width:] = partial_low(
        everything[:, :width].astype(f32), gain_ref[...], own, down_ref
    )


def new_state(own, received, state, up_ref):
    width = state.shape[1]
    low_out = received[0][:, width:].astype(f32)
    projected = received[0][:, :width].astype(f32)
    for part in received[1:]:
        low_out = low_out + part[:, width:].astype(f32)
        projected = projected + part[:, :width].astype(f32)
    spread = spread_over_slots(low_out, own)
    delta = jnp.dot(spread, up_ref[...], preferred_element_type=f32).astype(bf16)
    return (state.astype(f32) + projected + delta.astype(f32)).astype(bf16)


def between_kernel(total, rank, parts, *refs):
    received = refs[:parts]
    state_ref, facts_ref, up_ref, gain_ref, down_ref, send_ref = refs[parts:]
    width = down_ref.shape[2]
    own = own_slots(facts_ref[:, 1:2], total, rank)
    state = new_state(own, received, state_ref[:, :width], up_ref)
    send_ref[:, :width] = state
    send_ref[:, width:] = partial_low(state.astype(f32), gain_ref[...], own, down_ref)


def leave_kernel(total, rank, parts, *refs):
    received = refs[:parts]
    state_ref, facts_ref, up_ref = refs[parts : parts + 3]
    outgoing = refs[parts + 3 :]
    width = up_ref.shape[1]
    capacity = outgoing[0].shape[0]
    own = own_slots(facts_ref[:, 1:2], total, rank)
    state = new_state(own, received, state_ref[:, :width], up_ref)
    for s in range(len(outgoing)):
        outgoing[s][...] = state[s * capacity : (s + 1) * capacity]


def restore_kernel(place_ref, *refs):
    blocks, out_ref = refs[:-1], refs[-1]
    back = jnp.concatenate([block[...] for block in blocks], axis=0)
    out_ref[...] = jnp.dot(place_ref[...], back, preferred_element_type=f32).astype(bf16)


def norm_and_rotate(vector, gain, cosine, sine):
    head_dim = vector.shape[1]
    mean = jnp.mean(vector * vector, axis=1, keepdims=True)
    scaled = vector * lax.rsqrt(mean + epsilon) * gain
    return (scaled * cosine + pltpu.roll(scaled, head_dim // 2, 1) * sine).astype(bf16)


def project_slices(slices, masks, here, gain_ref, weight_ref):
    width = gain_ref.shape[2]
    products, squares, low = None, None, None
    for piece, mask in zip(slices, masks):
        source = jnp.bitwise_xor(here, mask)
        state = piece[:, :width].astype(f32)
        scaled = (state * gain_ref[source]).astype(bf16)
        features_there = pl.ds(pl.multiple_of(source * width, 64), width)
        product = jnp.dot(scaled, weight_ref[features_there, :], preferred_element_type=f32)
        square = jnp.sum(state * state, axis=1, keepdims=True)
        part = piece[:, width:].astype(f32)
        products = product if products is None else products + product
        squares = square if squares is None else squares + square
        low = part if low is None else low + part
    return products, squares, low


def early_kernel(masks, *refs):
    slices = refs[: len(masks)]
    index_ref, gain_ref, weight_ref, products_ref, squares_ref, low_ref = refs[len(masks) :]
    products, squares, low = project_slices(slices, masks, index_ref[0], gain_ref, weight_ref)
    products_ref[...] = products
    squares_ref[...] = jnp.broadcast_to(squares, squares_ref.shape)
    low_ref[...] = low


def step_kernel(total, rank, step, parts, masks, groups, *refs):
    refs = list(refs)

    def take(count):
        taken = refs[:count]
        del refs[:count]
        return taken

    slices = take(len(masks))
    (
        index_ref,
        products_ref,
        squares_ref,
        low_ref,
        facts_ref,
        gain_ref,
        weight_ref,
        query_up,
        key_up,
        value_up,
        query_gain,
        key_gain,
        cosine_ref,
        sine_ref,
        bias_ref,
    ) = take(15)
    cache = take(groups)
    earlier = take(2 * step)
    output_weight, output_down = take(2)
    outgoing = take(parts)
    key_fresh, value_fresh, attended, terms = refs
    features = weight_ref.shape[0]
    width = features // parts
    rows = products_ref.shape[0]
    head_dim = cache[0].shape[2]
    kv_local = cache[0].shape[0] // 2
    capacity = rows // groups
    query_width = query_up.shape[1]
    key_width = key_up.shape[1]
    heads = query_width // head_dim
    per_kv = heads // kv_local
    here = index_ref[0]

    own = own_slots(facts_ref[:, 1:2], total, rank)
    products, squares, low = project_slices(slices, masks, here, gain_ref, weight_ref)
    inverse = lax.rsqrt((squares_ref[:, :1] + squares) / features + epsilon)
    low = (low_ref[...] + low) * inverse

    def project(columns, up_ref, index):
        spread = spread_over_slots(low[:, index * rank : (index + 1) * rank], own)
        delta = jnp.dot(spread, up_ref[...], preferred_element_type=f32).astype(bf16)
        whole = (products_ref[:, columns] + products[:, columns]) * inverse
        return whole + delta.astype(f32)

    cosine = cosine_ref[step]
    sine = sine_ref[step]
    key = project(slice(query_width, query_width + key_width), key_up, 1)
    value = project(slice(query_width + key_width, None), value_up, 2).astype(bf16)
    for g in range(kv_local):
        columns = slice(g * head_dim, (g + 1) * head_dim)
        key_fresh[g] = norm_and_rotate(key[:, columns], key_gain[...], cosine, sine)
        value_fresh[g] = value[:, columns]
    query = project(slice(0, query_width), query_up, 0)
    query_heads = [
        norm_and_rotate(query[:, h * head_dim : (h + 1) * head_dim], query_gain[...], cosine, sine)
        for h in range(heads)
    ]

    scale = head_dim ** (-0.5)
    fresh_count = (step + 1) * capacity
    lanes = 128 * (-(-fresh_count // 128))
    filler = jnp.zeros((lanes - fresh_count, head_dim), bf16)
    key_place = lax.broadcasted_iota(jnp.int32, (per_kv * capacity, lanes), 1)
    own_row = lax.broadcasted_iota(jnp.int32, (per_kv * capacity, lanes), 0) % capacity
    same_row = (key_place % capacity == own_row) & (key_place < fresh_count)
    cached_count = bias_ref.shape[1]
    for b in range(groups):
        block = slice(b * capacity, (b + 1) * capacity)
        bias = jnp.concatenate([bias_ref[block, :]] * per_kv, axis=0)
        for g in range(kv_local):
            queries = jnp.concatenate(
                [query_heads[g * per_kv + h][block] for h in range(per_kv)], axis=0
            )
            fresh_keys = jnp.concatenate(
                [earlier[2 * t][g, block, :] for t in range(step)]
                + [key_fresh[g, block, :], filler],
                axis=0,
            )
            fresh_values = jnp.concatenate(
                [earlier[2 * t + 1][g, block, :] for t in range(step)]
                + [value_fresh[g, block, :], filler],
                axis=0,
            )
            cached = (
                lax.dot_general(queries, cache[b][g], NT, preferred_element_type=f32) * scale + bias
            )
            fresh = lax.dot_general(queries, fresh_keys, NT, preferred_element_type=f32) * scale
            fresh = jnp.where(same_row, fresh, blocked)
            scores = jnp.concatenate([cached, fresh], axis=1)
            largest = jnp.max(scores, axis=1, keepdims=True)
            weights = jnp.exp(scores - largest).astype(bf16)
            values = jnp.concatenate([cache[b][kv_local + g], fresh_values], axis=0)
            summing = jnp.concatenate([values, jnp.ones_like(values)], axis=1)
            mixed = jnp.dot(weights, summing, preferred_element_type=f32)
            mixed = (mixed[:, :head_dim] / mixed[:, head_dim:]).astype(bf16)
            for h in range(per_kv):
                head = g * per_kv + h
                attended[block, head * head_dim : (head + 1) * head_dim] = mixed[
                    h * capacity : (h + 1) * capacity
                ]

    attended_rows = attended[...]
    product = lax.dot_general(attended_rows, output_down[...], NT, preferred_element_type=f32)
    low_out = pick_slot(product, own).astype(bf16)
    for n in range(parts):
        term = jnp.dot(
            attended_rows,
            output_weight[:, n * width : (n + 1) * width],
            preferred_element_type=f32,
        )
        terms[jnp.bitwise_xor(here, n)] = term.astype(bf16)
    for mask in range(parts):
        outgoing[mask][:, :width] = terms[mask]
        outgoing[mask][:, width:] = low_out


def shift(block, axis, by):
    size = lax.axis_size(axis)
    return lax.ppermute(block, axis, [(i, (i + by) % size) for i in range(size)])


def swap(block, axis, mask):
    return lax.ppermute(block, axis, [(i, i ^ mask) for i in range(lax.axis_size(axis))])


def shards(
    hidden,
    input_norm_gain,
    query_projection_weight,
    key_projection_weight,
    value_projection_weight,
    query_norm_gain,
    key_norm_gain,
    output_projection_weight,
    stacked_down_factors,
    query_up_factor,
    key_up_factor,
    value_up_factor,
    output_down_factor,
    output_up_factor,
    cached_key_rows,
    cached_value_rows,
    cached_length_rows,
    domain_of_row,
    slot_of_domain,
):
    groups = lax.axis_size("wide")
    parts = lax.axis_size("narrow")
    wide_index = lax.axis_index("wide")
    narrow_index = lax.axis_index("narrow")
    row_group, width = hidden.shape
    capacity = row_group // 4
    rows = groups * capacity
    total = stacked_down_factors.shape[0]
    low_width = stacked_down_factors.shape[1]
    rank = output_up_factor.shape[1]
    _, kv_local, context, head_dim = cached_key_rows.shape
    features = input_norm_gain.shape[0]
    query_width = query_projection_weight.shape[1]

    smem = pl.BlockSpec(memory_space=pltpu.SMEM)
    vmem = pl.BlockSpec(memory_space=pltpu.VMEM)
    hbm = pl.BlockSpec(memory_space=pltpu.HBM)
    outgoing_shape = jax.ShapeDtypeStruct((capacity, width + 128), bf16)
    target, place, *outgoing = pl.pallas_call(
        route_kernel,
        out_shape=[
            jax.ShapeDtypeStruct((row_group,), jnp.int32),
            jax.ShapeDtypeStruct((row_group, rows), bf16),
        ]
        + [outgoing_shape] * groups,
        in_specs=[smem] + [hbm] * 4,
        out_specs=[smem] + [vmem] * (groups + 1),
        scratch_shapes=[
            pltpu.SMEM((groups,), jnp.int32),
            pltpu.VMEM((row_group, rows), f32),
            pltpu.VMEM((row_group, 128), f32),
            pltpu.SMEM(domain_of_row.shape, jnp.int32),
            pltpu.SMEM(slot_of_domain.shape, jnp.int32),
            pltpu.SMEM(cached_length_rows.shape, jnp.int32),
            pltpu.VMEM(hidden.shape, bf16),
            pltpu.SemaphoreType.DMA((4,)),
        ],
        compiler_params=kernel_params(8),
        name="route_rows",
    )(wide_index.reshape(1), domain_of_row, slot_of_domain, cached_length_rows, hidden)
    arrived = [outgoing[0]] + [shift(outgoing[s], "wide", s) for s in range(1, groups)]
    packed_shape = (2 * kv_local, capacity, context, head_dim)
    packed = pl.pallas_call(
        pack_kernel,
        out_shape=[jax.ShapeDtypeStruct(packed_shape, bf16)] * groups,
        in_specs=[smem, hbm, hbm],
        out_specs=[vmem] * groups,
        scratch_shapes=[
            pltpu.VMEM((groups,) + packed_shape, bf16),
            pltpu.VMEM(cached_key_rows.shape, bf16),
            pltpu.VMEM(cached_value_rows.shape, bf16),
            pltpu.SemaphoreType.DMA((2,)),
        ],
        compiler_params=kernel_params(16),
        name="pack_cache",
    )(target, cached_key_rows, cached_value_rows)
    cache = [packed[0]] + [shift(packed[s], "wide", s) for s in range(1, groups)]
    cache = [block.reshape(2 * kv_local, capacity * context, head_dim) for block in cache]

    key_width = key_projection_weight.shape[1]
    stored = [
        (features, query_width + 2 * key_width),
        (total * rank, query_width),
        (total * rank, key_width),
        (total * rank, key_width),
        output_projection_weight.shape,
        (total * rank, query_width),
        (total * rank, width),
        (low_width // rank, total * rank, width),
    ]
    weights = pl.pallas_call(
        functools.partial(load_kernel, rank),
        out_shape=[jax.ShapeDtypeStruct(shape, bf16) for shape in stored],
        in_specs=[hbm] * 10,
        out_specs=[vmem] * 8,
        scratch_shapes=[pltpu.SemaphoreType.DMA((9 + total * low_width // rank,))],
        compiler_params=kernel_params(24),
        cost_estimate=pl.CostEstimate(flops=0, bytes_accessed=40000000, transcendentals=0),
        name="load_weights",
    )(
        query_projection_weight,
        key_projection_weight,
        value_projection_weight,
        query_up_factor.reshape(total * rank, query_width),
        key_up_factor.reshape(total * rank, key_width),
        value_up_factor.reshape(total * rank, key_width),
        output_projection_weight,
        output_down_factor.reshape(total * rank, query_width),
        output_up_factor.reshape(total * rank, width),
        stacked_down_factors,
    )
    input_weight, query_up, key_up, value_up, output_weight, output_down, output_up, down = weights

    gain_rows = input_norm_gain.reshape(parts, 1, width)
    gain_slice = lax.dynamic_index_in_dim(gain_rows, narrow_index, 0, keepdims=False)
    sent_state = jax.ShapeDtypeStruct((rows, width + low_width), bf16)
    send, facts_here = pl.pallas_call(
        functools.partial(enter_kernel, total, rank, groups),
        out_shape=[sent_state, jax.ShapeDtypeStruct((rows, 128), f32)],
        in_specs=[vmem] * (groups + 2),
        out_specs=[vmem] * 2,
        compiler_params=kernel_params(8),
        name="enter",
    )(*arrived, gain_slice, down)
    lengths = facts_here[:, 0]
    frequency = rope_base ** (-(jnp.arange(head_dim // 2, dtype=f32) * 2.0) / head_dim)
    positions = lengths[None, :] + jnp.arange(STEPS, dtype=f32)[:, None]
    angles = positions[:, :, None] * frequency
    cosine = jnp.cos(angles)
    sine = jnp.sin(angles)
    cosine = jnp.concatenate([cosine, cosine], axis=-1)
    sine = jnp.concatenate([-sine, sine], axis=-1)
    key_index = jnp.arange(capacity * context)[None, :]
    visible = (key_index // context == (jnp.arange(rows) % capacity)[:, None]) & (
        (key_index % context).astype(f32) < lengths[:, None]
    )
    bias = jnp.where(visible, 0.0, blocked).astype(f32)

    query_gain = query_norm_gain.reshape(1, head_dim)
    key_gain = key_norm_gain.reshape(1, head_dim)
    index_here = narrow_index.reshape(1)
    sent_terms = jax.ShapeDtypeStruct((rows, width + rank), bf16)
    fresh = jax.ShapeDtypeStruct((kv_local, rows, head_dim), bf16)
    far = [mask for mask in range(parts - 1, 1, -1) if mask % 2 == 1]
    early = [0, 1] + far
    late = [mask ^ 1 for mask in far]

    earlier = []
    for step in range(STEPS):
        from_far = [swap(send, "narrow", mask) for mask in far]
        slices = [send, swap(send, "narrow", 1)] + from_far
        passed_on = [swap(piece, "narrow", 1) for piece in from_far]
        sums = pl.pallas_call(
            functools.partial(early_kernel, early),
            out_shape=[
                jax.ShapeDtypeStruct((rows, input_weight.shape[1]), f32),
                jax.ShapeDtypeStruct((rows, 128), f32),
                jax.ShapeDtypeStruct((rows, low_width), f32),
            ],
            in_specs=[vmem] * len(early) + [smem] + [vmem] * 2,
            out_specs=[vmem] * 3,
            compiler_params=kernel_params(16),
            cost_estimate=pl.CostEstimate(
                flops=2 * rows * features * input_weight.shape[1],
                bytes_accessed=10000000,
                transcendentals=0,
            ),
            name="project_early",
        )(*slices, index_here, gain_rows, input_weight)
        *terms, key_fresh, value_fresh = pl.pallas_call(
            functools.partial(step_kernel, total, rank, step, parts, late, groups),
            out_shape=[sent_terms] * parts + [fresh] * 2,
            in_specs=[vmem] * len(late) + [smem] + [vmem] * (16 + groups + 2 * step),
            out_specs=[vmem] * (parts + 2),
            scratch_shapes=[
                pltpu.VMEM((rows, query_width), bf16),
                pltpu.VMEM((parts, rows, width), bf16),
            ],
            compiler_params=kernel_params(24),
            name="attend_step",
        )(
            *passed_on,
            index_here,
            *sums,
            facts_here,
            gain_rows,
            input_weight,
            query_up,
            key_up,
            value_up,
            query_gain,
            key_gain,
            cosine,
            sine,
            bias,
            *cache,
            *earlier,
            output_weight,
            output_down,
        )
        earlier += [key_fresh, value_fresh]
        received = [terms[0]] + [swap(terms[mask], "narrow", mask) for mask in range(parts - 1, 0, -1)]
        if step < STEPS - 1:
            send = pl.pallas_call(
                functools.partial(between_kernel, total, rank, parts),
                out_shape=sent_state,
                in_specs=[vmem] * (parts + 5),
                out_specs=vmem,
                compiler_params=kernel_params(8),
                name="between",
            )(*received, send, facts_here, output_up, gain_slice, down)
        else:
            leaving = pl.pallas_call(
                functools.partial(leave_kernel, total, rank, parts),
                out_shape=[jax.ShapeDtypeStruct((capacity, width), bf16)] * groups,
                in_specs=[vmem] * (parts + 3),
                out_specs=[vmem] * groups,
                compiler_params=kernel_params(8),
                name="leave",
            )(*received, send, facts_here, output_up)

    back = [leaving[0]] + [shift(leaving[s], "wide", -s) for s in range(1, groups)]
    return pl.pallas_call(
        restore_kernel,
        out_shape=jax.ShapeDtypeStruct((row_group, width), bf16),
        in_specs=[vmem] * (groups + 1),
        out_specs=vmem,
        compiler_params=kernel_params(8),
        name="restore",
    )(place, *back)


def solution(mesh):
    placed = (
        P(("parts", "wide"), "narrow"),
        P(),
        P(None, "narrow"),
        P(None, "narrow"),
        P(None, "narrow"),
        P(),
        P(),
        P("narrow", None),
        P(("parts", "wide"), None, "narrow"),
        P(("parts", "wide"), None, "narrow"),
        P(("parts", "wide"), None, "narrow"),
        P(("parts", "wide"), None, "narrow"),
        P(("parts", "wide"), None, "narrow"),
        P(("parts", "wide"), None, "narrow"),
        P(("parts", "wide"), "narrow", None, None),
        P(("parts", "wide"), "narrow", None, None),
        P(("parts", "wide")),
        P("parts"),
        P("parts"),
    )
    return jax.shard_map(
        shards,
        mesh=mesh,
        in_specs=placed,
        out_specs=P(("parts", "wide"), "narrow"),
        check_vma=False,
    )
```

```python
import functools

import jax
import jax.numpy as jnp
from jax import lax
from jax.experimental import pallas as pl
from jax.experimental.pallas import tpu as pltpu
from jax.sharding import PartitionSpec as P

STEPS = 4

epsilon = 1e-06
rope_base = 1000000.0
blocked = -1e30
f32 = jnp.float32
bf16 = jnp.bfloat16

NT = (((1,), (1,)), ((), ()))


def kernel_params(mib):
    return pltpu.CompilerParams(vmem_limit_bytes=mib * 1024 * 1024)


def in_hbm(array):
    return pltpu.with_memory_space_constraint(array, pltpu.HBM)


def copy_all(pairs, sems):
    copies = [
        pltpu.make_async_copy(source, target, sems.at[index])
        for index, (source, target) in enumerate(pairs)
    ]
    for copy in copies:
        copy.start()
    return copies


def route_kernel(
    group_ref, domain_hbm, slot_hbm, length_hbm, hidden_hbm, target_ref, place_ref, *refs
):
    groups = len(refs) - 8
    outgoing = refs[:groups]
    count, place, facts, domain_ref, slot_ref, length_ref, hidden_ref, sems = refs[groups:]
    rows, width = hidden_ref.shape
    capacity = outgoing[0].shape[0]
    per_group = slot_ref.shape[0] // groups
    here = group_ref[0]
    *tables, hidden_copy = copy_all(
        [
            (domain_hbm, domain_ref),
            (slot_hbm, slot_ref),
            (length_hbm, length_ref),
            (hidden_hbm, hidden_ref),
        ],
        sems,
    )
    for group in range(groups):
        count[group] = 0
    places = lax.broadcasted_iota(jnp.int32, (1, groups * capacity), 1)
    columns = lax.broadcasted_iota(jnp.int32, (1, facts.shape[1]), 1)
    for copy in tables:
        copy.wait()

    def put(row, carry):
        slot = slot_ref[domain_ref[here * rows + row]]
        dest = lax.div(slot, per_group)
        position = jnp.minimum(count[dest], capacity - 1)
        count[dest] = position + 1
        target = lax.rem(dest - here + groups, groups) * capacity + position
        target_ref[row] = target
        place[pl.ds(row, 1), :] = jnp.where(places == target, 1.0, 0.0)
        length = length_ref[row].astype(f32)
        local = (slot - dest * per_group).astype(f32)
        facts[pl.ds(row, 1), :] = jnp.where(
            columns == 0, length, jnp.where(columns == 1, local, 0.0)
        )
        return carry

    lax.fori_loop(0, rows, put, 0)
    chosen = place[...].astype(bf16)
    place_ref[...] = chosen
    across = (((0,), (0,)), ((), ()))
    known = lax.dot_general(
        chosen, facts[...].astype(bf16), across, preferred_element_type=f32
    ).astype(bf16)
    hidden_copy.wait()
    state = lax.dot_general(
        chosen, hidden_ref[...], across, preferred_element_type=f32
    ).astype(bf16)
    for s in range(groups):
        block = slice(s * capacity, (s + 1) * capacity)
        outgoing[s][:, :width] = state[block]
        outgoing[s][:, width:] = known[block]


def pack_kernel(target_ref, key_hbm, value_hbm, *refs):
    groups = len(refs) - 4
    outgoing = refs[:groups]
    packed, key_ref, value_ref, sems = refs[groups:]
    rows, kv_local = key_ref.shape[:2]
    capacity = packed.shape[2]
    copies = copy_all([(key_hbm, key_ref), (value_hbm, value_ref)], sems)
    if groups * capacity > rows:
        packed[...] = jnp.zeros_like(packed)
    for copy in copies:
        copy.wait()

    def put(row, carry):
        target = target_ref[row]
        block = lax.div(target, capacity)
        position = target - block * capacity
        for g in range(kv_local):
            packed[block, g, position] = key_ref[row, g]
            packed[block, kv_local + g, position] = value_ref[row, g]
        return carry

    lax.fori_loop(0, rows, put, 0)
    for s in range(groups):
        outgoing[s][...] = packed[s]


def load_kernel(rank, *refs):
    query, key, value, query_up, key_up, value_up, output, output_down, output_up, down = refs[:10]
    inputs, *same, down_out = refs[10:18]
    sems = refs[18]
    total, kinds = down.shape[0], down.shape[1] // rank
    pairs = []
    column = 0
    for weight in (query, key, value):
        width = weight.shape[1]
        pairs.append((weight, inputs.at[:, column : column + width]))
        column += width
    pairs += zip((query_up, key_up, value_up, output, output_down, output_up), same)
    for kind in range(kinds):
        for d in range(total):
            pairs.append(
                (
                    down.at[d, kind * rank : (kind + 1) * rank, :],
                    down_out.at[kind, d * rank : (d + 1) * rank, :],
                )
            )
    for copy in copy_all(pairs, sems):
        copy.wait()


def own_slots(slot, total, rank):
    lane = lax.broadcasted_iota(jnp.int32, (1, 2 * rank), 1)
    second = (lane >= rank).astype(f32)
    return [slot == 2.0 * j + second for j in range(total // 2)]


def spread_over_slots(factor, own):
    twice = jnp.concatenate([factor, factor], axis=1)
    return jnp.concatenate([jnp.where(mask, twice, 0.0).astype(bf16) for mask in own], axis=1)


def pick_slot(product, own):
    wide = own[0].shape[1]
    picked = jnp.where(own[0], product[:, :wide], 0.0)
    for j in range(1, len(own)):
        picked = picked + jnp.where(own[j], product[:, j * wide : (j + 1) * wide], 0.0)
    return picked[:, : wide // 2] + picked[:, wide // 2 :]


def partial_low(state, gain, own, down_ref):
    scaled = (state * gain).astype(bf16)
    picked = []
    for kind in range(down_ref.shape[0]):
        product = lax.dot_general(scaled, down_ref[kind], NT, preferred_element_type=f32)
        picked.append(pick_slot(product, own).astype(bf16))
    return jnp.concatenate(picked, axis=1)


def enter_kernel(total, rank, groups, *refs):
    blocks = refs[:groups]
    gain_ref, down_ref, send_ref, facts_ref = refs[groups:]
    width = down_ref.shape[2]
    everything = jnp.concatenate([block[...] for block in blocks], axis=0)
    facts = everything[:, width:].astype(f32)
    own = own_slots(facts[:, 1:2], total, rank)
    facts_ref[...] = facts
    send_ref[:, :width] = everything[:, :width]
    send_ref[:, width:] = partial_low(
        everything[:, :width].astype(f32), gain_ref[...], own, down_ref
    )


def new_state(own, received, state, up_ref):
    width = state.shape[1]
    low_out = received[0][:, width:].astype(f32)
    projected = received[0][:, :width].astype(f32)
    for part in received[1:]:
        low_out = low_out + part[:, width:].astype(f32)
        projected = projected + part[:, :width].astype(f32)
    spread = spread_over_slots(low_out, own)
    delta = jnp.dot(spread, up_ref[...], preferred_element_type=f32).astype(bf16)
    return (state.astype(f32) + projected + delta.astype(f32)).astype(bf16)


def between_kernel(total, rank, parts, *refs):
    received = refs[:parts]
    state_ref, facts_ref, up_ref, gain_ref, down_ref, send_ref = refs[parts:]
    width = down_ref.shape[2]
    own = own_slots(facts_ref[:, 1:2], total, rank)
    state = new_state(own, received, state_ref[:, :width], up_ref)
    send_ref[:, :width] = state
    send_ref[:, width:] = partial_low(state.astype(f32), gain_ref[...], own, down_ref)


def leave_kernel(total, rank, parts, *refs):
    received = refs[:parts]
    state_ref, facts_ref, up_ref = refs[parts : parts + 3]
    outgoing = refs[parts + 3 :]
    width = up_ref.shape[1]
    capacity = outgoing[0].shape[0]
    own = own_slots(facts_ref[:, 1:2], total, rank)
    state = new_state(own, received, state_ref[:, :width], up_ref)
    for s in range(len(outgoing)):
        outgoing[s][...] = state[s * capacity : (s + 1) * capacity]


def restore_kernel(place_ref, *refs):
    blocks, out_ref = refs[:-1], refs[-1]
    back = jnp.concatenate([block[...] for block in blocks], axis=0)
    out_ref[...] = jnp.dot(place_ref[...], back, preferred_element_type=f32).astype(bf16)


def norm_and_rotate(vector, gain, cosine, sine):
    head_dim = vector.shape[1]
    mean = jnp.mean(vector * vector, axis=1, keepdims=True)
    scaled = vector * lax.rsqrt(mean + epsilon) * gain
    return (scaled * cosine + pltpu.roll(scaled, head_dim // 2, 1) * sine).astype(bf16)


def project_slices(slices, masks, here, gain_ref, weight_ref):
    width = gain_ref.shape[2]
    products, squares, low = None, None, None
    for piece, mask in zip(slices, masks):
        source = jnp.bitwise_xor(here, mask)
        state = piece[:, :width].astype(f32)
        scaled = (state * gain_ref[source]).astype(bf16)
        features_there = pl.ds(pl.multiple_of(source * width, 64), width)
        product = jnp.dot(scaled, weight_ref[features_there, :], preferred_element_type=f32)
        square = jnp.sum(state * state, axis=1, keepdims=True)
        part = piece[:, width:].astype(f32)
        products = product if products is None else products + product
        squares = square if squares is None else squares + square
        low = part if low is None else low + part
    return products, squares, low


def early_kernel(masks, *refs):
    slices = refs[: len(masks)]
    index_ref, gain_ref, weight_ref, products_ref, squares_ref, low_ref = refs[len(masks) :]
    products, squares, low = project_slices(slices, masks, index_ref[0], gain_ref, weight_ref)
    products_ref[...] = products
    squares_ref[...] = jnp.broadcast_to(squares, squares_ref.shape)
    low_ref[...] = low


def step_kernel(total, rank, step, parts, masks, groups, *refs):
    refs = list(refs)

    def take(count):
        taken = refs[:count]
        del refs[:count]
        return taken

    slices = take(len(masks))
    (
        index_ref,
        products_ref,
        squares_ref,
        low_ref,
        facts_ref,
        gain_ref,
        weight_ref,
        query_up,
        key_up,
        value_up,
        query_gain,
        key_gain,
        cosine_ref,
        sine_ref,
        bias_ref,
    ) = take(15)
    cache = take(groups)
    earlier = take(2 * step)
    output_weight, output_down = take(2)
    outgoing = take(parts)
    key_fresh, value_fresh, attended, terms = refs
    features = weight_ref.shape[0]
    width = features // parts
    rows = products_ref.shape[0]
    head_dim = cache[0].shape[2]
    kv_local = cache[0].shape[0] // 2
    capacity = rows // groups
    query_width = query_up.shape[1]
    key_width = key_up.shape[1]
    heads = query_width // head_dim
    per_kv = heads // kv_local
    here = index_ref[0]

    own = own_slots(facts_ref[:, 1:2], total, rank)
    products, squares, low = project_slices(slices, masks, here, gain_ref, weight_ref)
    inverse = lax.rsqrt((squares_ref[:, :1] + squares) / features + epsilon)
    low = (low_ref[...] + low) * inverse

    def project(columns, up_ref, index):
        spread = spread_over_slots(low[:, index * rank : (index + 1) * rank], own)
        delta = jnp.dot(spread, up_ref[...], preferred_element_type=f32).astype(bf16)
        whole = (products_ref[:, columns] + products[:, columns]) * inverse
        return whole + delta.astype(f32)

    cosine = cosine_ref[step]
    sine = sine_ref[step]
    key = project(slice(query_width, query_width + key_width), key_up, 1)
    value = project(slice(query_width + key_width, None), value_up, 2).astype(bf16)
    for g in range(kv_local):
        columns = slice(g * head_dim, (g + 1) * head_dim)
        key_fresh[g] = norm_and_rotate(key[:, columns], key_gain[...], cosine, sine)
        value_fresh[g] = value[:, columns]
    query = project(slice(0, query_width), query_up, 0)
    query_heads = [
        norm_and_rotate(query[:, h * head_dim : (h + 1) * head_dim], query_gain[...], cosine, sine)
        for h in range(heads)
    ]

    scale = head_dim ** (-0.5)
    fresh_count = (step + 1) * capacity
    lanes = 128 * (-(-fresh_count // 128))
    filler = jnp.zeros((lanes - fresh_count, head_dim), bf16)
    key_place = lax.broadcasted_iota(jnp.int32, (per_kv * capacity, lanes), 1)
    own_row = lax.broadcasted_iota(jnp.int32, (per_kv * capacity, lanes), 0) % capacity
    same_row = (key_place % capacity == own_row) & (key_place < fresh_count)
    cached_count = bias_ref.shape[1]
    for b in range(groups):
        block = slice(b * capacity, (b + 1) * capacity)
        bias = jnp.concatenate([bias_ref[block, :]] * per_kv, axis=0)
        for g in range(kv_local):
            queries = jnp.concatenate(
                [query_heads[g * per_kv + h][block] for h in range(per_kv)], axis=0
            )
            fresh_keys = jnp.concatenate(
                [earlier[2 * t][g, block, :] for t in range(step)]
                + [key_fresh[g, block, :], filler],
                axis=0,
            )
            fresh_values = jnp.concatenate(
                [earlier[2 * t + 1][g, block, :] for t in range(step)]
                + [value_fresh[g, block, :], filler],
                axis=0,
            )
            cached = (
                lax.dot_general(queries, cache[b][g], NT, preferred_element_type=f32) * scale + bias
            )
            fresh = lax.dot_general(queries, fresh_keys, NT, preferred_element_type=f32) * scale
            fresh = jnp.where(same_row, fresh, blocked)
            scores = jnp.concatenate([cached, fresh], axis=1)
            largest = jnp.max(scores, axis=1, keepdims=True)
            weights = jnp.exp(scores - largest).astype(bf16)
            values = jnp.concatenate([cache[b][kv_local + g], fresh_values], axis=0)
            summing = jnp.concatenate([values, jnp.ones_like(values)], axis=1)
            mixed = jnp.dot(weights, summing, preferred_element_type=f32)
            mixed = (mixed[:, :head_dim] / mixed[:, head_dim:]).astype(bf16)
            for h in range(per_kv):
                head = g * per_kv + h
                attended[block, head * head_dim : (head + 1) * head_dim] = mixed[
                    h * capacity : (h + 1) * capacity
                ]

    attended_rows = attended[...]
    product = lax.dot_general(attended_rows, output_down[...], NT, preferred_element_type=f32)
    low_out = pick_slot(product, own).astype(bf16)
    for n in range(parts):
        term = jnp.dot(
            attended_rows,
            output_weight[:, n * width : (n + 1) * width],
            preferred_element_type=f32,
        )
        terms[jnp.bitwise_xor(here, n)] = term.astype(bf16)
    for mask in range(parts):
        outgoing[mask][:, :width] = terms[mask]
        outgoing[mask][:, width:] = low_out


def shift(block, axis, by):
    size = lax.axis_size(axis)
    return lax.ppermute(block, axis, [(i, (i + by) % size) for i in range(size)])


def swap(block, axis, mask):
    return lax.ppermute(block, axis, [(i, i ^ mask) for i in range(lax.axis_size(axis))])


def shards(
    hidden,
    input_norm_gain,
    query_projection_weight,
    key_projection_weight,
    value_projection_weight,
    query_norm_gain,
    key_norm_gain,
    output_projection_weight,
    stacked_down_factors,
    query_up_factor,
    key_up_factor,
    value_up_factor,
    output_down_factor,
    output_up_factor,
    cached_key_rows,
    cached_value_rows,
    cached_length_rows,
    domain_of_row,
    slot_of_domain,
):
    groups = lax.axis_size("wide")
    parts = lax.axis_size("narrow")
    wide_index = lax.axis_index("wide")
    narrow_index = lax.axis_index("narrow")
    row_group, width = hidden.shape
    capacity = row_group // 4
    rows = groups * capacity
    total = stacked_down_factors.shape[0]
    low_width = stacked_down_factors.shape[1]
    rank = output_up_factor.shape[1]
    _, kv_local, context, head_dim = cached_key_rows.shape
    features = input_norm_gain.shape[0]
    query_width = query_projection_weight.shape[1]

    smem = pl.BlockSpec(memory_space=pltpu.SMEM)
    vmem = pl.BlockSpec(memory_space=pltpu.VMEM)
    hbm = pl.BlockSpec(memory_space=pltpu.HBM)
    outgoing_shape = jax.ShapeDtypeStruct((capacity, width + 128), bf16)
    target, place, *outgoing = pl.pallas_call(
        route_kernel,
        out_shape=[
            jax.ShapeDtypeStruct((row_group,), jnp.int32),
            jax.ShapeDtypeStruct((row_group, rows), bf16),
        ]
        + [outgoing_shape] * groups,
        in_specs=[smem] + [hbm] * 4,
        out_specs=[smem] + [vmem] * (groups + 1),
        scratch_shapes=[
            pltpu.SMEM((groups,), jnp.int32),
            pltpu.VMEM((row_group, rows), f32),
            pltpu.VMEM((row_group, 128), f32),
            pltpu.SMEM(domain_of_row.shape, jnp.int32),
            pltpu.SMEM(slot_of_domain.shape, jnp.int32),
            pltpu.SMEM(cached_length_rows.shape, jnp.int32),
            pltpu.VMEM(hidden.shape, bf16),
            pltpu.SemaphoreType.DMA((4,)),
        ],
        compiler_params=kernel_params(8),
        name="route_rows",
    )(
        wide_index.reshape(1),
        in_hbm(domain_of_row),
        in_hbm(slot_of_domain),
        in_hbm(cached_length_rows),
        in_hbm(hidden),
    )
    arrived = [outgoing[0]] + [shift(outgoing[s], "wide", s) for s in range(1, groups)]
    packed_shape = (2 * kv_local, capacity, context, head_dim)
    packed = pl.pallas_call(
        pack_kernel,
        out_shape=[jax.ShapeDtypeStruct(packed_shape, bf16)] * groups,
        in_specs=[smem, hbm, hbm],
        out_specs=[vmem] * groups,
        scratch_shapes=[
            pltpu.VMEM((groups,) + packed_shape, bf16),
            pltpu.VMEM(cached_key_rows.shape, bf16),
            pltpu.VMEM(cached_value_rows.shape, bf16),
            pltpu.SemaphoreType.DMA((2,)),
        ],
        compiler_params=kernel_params(16),
        name="pack_cache",
    )(target, in_hbm(cached_key_rows), in_hbm(cached_value_rows))
    cache = [packed[0]] + [shift(packed[s], "wide", s) for s in range(1, groups)]
    cache = [block.reshape(2 * kv_local, capacity * context, head_dim) for block in cache]

    key_width = key_projection_weight.shape[1]
    stored = [
        (features, query_width + 2 * key_width),
        (total * rank, query_width),
        (total * rank, key_width),
        (total * rank, key_width),
        output_projection_weight.shape,
        (total * rank, query_width),
        (total * rank, width),
        (low_width // rank, total * rank, width),
    ]
    weights = pl.pallas_call(
        functools.partial(load_kernel, rank),
        out_shape=[jax.ShapeDtypeStruct(shape, bf16) for shape in stored],
        in_specs=[hbm] * 10,
        out_specs=[vmem] * 8,
        scratch_shapes=[pltpu.SemaphoreType.DMA((9 + total * low_width // rank,))],
        compiler_params=kernel_params(24),
        cost_estimate=pl.CostEstimate(flops=0, bytes_accessed=40000000, transcendentals=0),
        name="load_weights",
    )(
        in_hbm(query_projection_weight),
        in_hbm(key_projection_weight),
        in_hbm(value_projection_weight),
        in_hbm(query_up_factor.reshape(total * rank, query_width)),
        in_hbm(key_up_factor.reshape(total * rank, key_width)),
        in_hbm(value_up_factor.reshape(total * rank, key_width)),
        in_hbm(output_projection_weight),
        in_hbm(output_down_factor.reshape(total * rank, query_width)),
        in_hbm(output_up_factor.reshape(total * rank, width)),
        in_hbm(stacked_down_factors),
    )
    input_weight, query_up, key_up, value_up, output_weight, output_down, output_up, down = weights

    gain_rows = input_norm_gain.reshape(parts, 1, width)
    gain_slice = lax.dynamic_index_in_dim(gain_rows, narrow_index, 0, keepdims=False)
    sent_state = jax.ShapeDtypeStruct((rows, width + low_width), bf16)
    send, facts_here = pl.pallas_call(
        functools.partial(enter_kernel, total, rank, groups),
        out_shape=[sent_state, jax.ShapeDtypeStruct((rows, 128), f32)],
        in_specs=[vmem] * (groups + 2),
        out_specs=[vmem] * 2,
        compiler_params=kernel_params(8),
        name="enter",
    )(*arrived, gain_slice, down)
    lengths = facts_here[:, 0]
    frequency = rope_base ** (-(jnp.arange(head_dim // 2, dtype=f32) * 2.0) / head_dim)
    positions = lengths[None, :] + jnp.arange(STEPS, dtype=f32)[:, None]
    angles = positions[:, :, None] * frequency
    cosine = jnp.cos(angles)
    sine = jnp.sin(angles)
    cosine = jnp.concatenate([cosine, cosine], axis=-1)
    sine = jnp.concatenate([-sine, sine], axis=-1)
    key_index = jnp.arange(capacity * context)[None, :]
    visible = (key_index // context == (jnp.arange(rows) % capacity)[:, None]) & (
        (key_index % context).astype(f32) < lengths[:, None]
    )
    bias = jnp.where(visible, 0.0, blocked).astype(f32)

    query_gain = query_norm_gain.reshape(1, head_dim)
    key_gain = key_norm_gain.reshape(1, head_dim)
    index_here = narrow_index.reshape(1)
    sent_terms = jax.ShapeDtypeStruct((rows, width + rank), bf16)
    fresh = jax.ShapeDtypeStruct((kv_local, rows, head_dim), bf16)
    far = [mask for mask in range(parts - 1, 1, -1) if mask % 2 == 1]
    early = [0, 1] + far
    late = [mask ^ 1 for mask in far]

    earlier = []
    for step in range(STEPS):
        from_far = [swap(send, "narrow", mask) for mask in far]
        slices = [send, swap(send, "narrow", 1)] + from_far
        passed_on = [swap(piece, "narrow", 1) for piece in from_far]
        sums = pl.pallas_call(
            functools.partial(early_kernel, early),
            out_shape=[
                jax.ShapeDtypeStruct((rows, input_weight.shape[1]), f32),
                jax.ShapeDtypeStruct((rows, 128), f32),
                jax.ShapeDtypeStruct((rows, low_width), f32),
            ],
            in_specs=[vmem] * len(early) + [smem] + [vmem] * 2,
            out_specs=[vmem] * 3,
            compiler_params=kernel_params(16),
            cost_estimate=pl.CostEstimate(
                flops=2 * rows * features * input_weight.shape[1],
                bytes_accessed=10000000,
                transcendentals=0,
            ),
            name="project_early",
        )(*slices, index_here, gain_rows, input_weight)
        *terms, key_fresh, value_fresh = pl.pallas_call(
            functools.partial(step_kernel, total, rank, step, parts, late, groups),
            out_shape=[sent_terms] * parts + [fresh] * 2,
            in_specs=[vmem] * len(late) + [smem] + [vmem] * (16 + groups + 2 * step),
            out_specs=[vmem] * (parts + 2),
            scratch_shapes=[
                pltpu.VMEM((rows, query_width), bf16),
                pltpu.VMEM((parts, rows, width), bf16),
            ],
            compiler_params=kernel_params(24),
            name="attend_step",
        )(
            *passed_on,
            index_here,
            *sums,
            facts_here,
            gain_rows,
            input_weight,
            query_up,
            key_up,
            value_up,
            query_gain,
            key_gain,
            cosine,
            sine,
            bias,
            *cache,
            *earlier,
            output_weight,
            output_down,
        )
        earlier += [key_fresh, value_fresh]
        received = [terms[0]] + [swap(terms[mask], "narrow", mask) for mask in range(parts - 1, 0, -1)]
        if step < STEPS - 1:
            send = pl.pallas_call(
                functools.partial(between_kernel, total, rank, parts),
                out_shape=sent_state,
                in_specs=[vmem] * (parts + 5),
                out_specs=vmem,
                compiler_params=kernel_params(8),
                name="between",
            )(*received, send, facts_here, output_up, gain_slice, down)
        else:
            leaving = pl.pallas_call(
                functools.partial(leave_kernel, total, rank, parts),
                out_shape=[jax.ShapeDtypeStruct((capacity, width), bf16)] * groups,
                in_specs=[vmem] * (parts + 3),
                out_specs=[vmem] * groups,
                compiler_params=kernel_params(8),
                name="leave",
            )(*received, send, facts_here, output_up)

    back = [leaving[0]] + [shift(leaving[s], "wide", -s) for s in range(1, groups)]
    return pl.pallas_call(
        restore_kernel,
        out_shape=jax.ShapeDtypeStruct((row_group, width), bf16),
        in_specs=[vmem] * (groups + 1),
        out_specs=vmem,
        compiler_params=kernel_params(8),
        name="restore",
    )(place, *back)


def solution(mesh):
    placed = (
        P(("parts", "wide"), "narrow"),
        P(),
        P(None, "narrow"),
        P(None, "narrow"),
        P(None, "narrow"),
        P(),
        P(),
        P("narrow", None),
        P(("parts", "wide"), None, "narrow"),
        P(("parts", "wide"), None, "narrow"),
        P(("parts", "wide"), None, "narrow"),
        P(("parts", "wide"), None, "narrow"),
        P(("parts", "wide"), None, "narrow"),
        P(("parts", "wide"), None, "narrow"),
        P(("parts", "wide"), "narrow", None, None),
        P(("parts", "wide"), "narrow", None, None),
        P(("parts", "wide")),
        P("parts"),
        P("parts"),
    )
    return jax.shard_map(
        shards,
        mesh=mesh,
        in_specs=placed,
        out_specs=P(("parts", "wide"), "narrow"),
        check_vma=False,
    )
```

```python
import functools

import jax
import jax.numpy as jnp
from jax import lax
from jax.experimental import pallas as pl
from jax.experimental.pallas import tpu as pltpu
from jax.sharding import PartitionSpec as P

STEPS = 4

epsilon = 1e-06
rope_base = 1000000.0
blocked = -1e30
f32 = jnp.float32
bf16 = jnp.bfloat16

NT = (((1,), (1,)), ((), ()))


def kernel_params(mib):
    return pltpu.CompilerParams(vmem_limit_bytes=mib * 1024 * 1024)


def in_hbm(array):
    return pltpu.with_memory_space_constraint(array, pltpu.HBM)


def in_order(refs, order):
    return [refs[order.index(block)] for block in range(len(order))]


def copy_all(pairs, sems):
    copies = [
        pltpu.make_async_copy(source, target, sems.at[index])
        for index, (source, target) in enumerate(pairs)
    ]
    for copy in copies:
        copy.start()
    return copies


def route_kernel(
    group_ref, domain_hbm, slot_hbm, length_hbm, hidden_hbm, target_ref, place_ref, *refs
):
    groups = len(refs) - 8
    outgoing = refs[:groups]
    count, place, facts, domain_ref, slot_ref, length_ref, hidden_ref, sems = refs[groups:]
    rows, width = hidden_ref.shape
    capacity = outgoing[0].shape[0]
    per_group = slot_ref.shape[0] // groups
    here = group_ref[0]
    *tables, hidden_copy = copy_all(
        [
            (domain_hbm, domain_ref),
            (slot_hbm, slot_ref),
            (length_hbm, length_ref),
            (hidden_hbm, hidden_ref),
        ],
        sems,
    )
    for group in range(groups):
        count[group] = 0
    places = lax.broadcasted_iota(jnp.int32, (1, groups * capacity), 1)
    columns = lax.broadcasted_iota(jnp.int32, (1, facts.shape[1]), 1)
    for copy in tables:
        copy.wait()

    def put(row, carry):
        slot = slot_ref[domain_ref[here * rows + row]]
        dest = lax.div(slot, per_group)
        position = jnp.minimum(count[dest], capacity - 1)
        count[dest] = position + 1
        target = jnp.bitwise_xor(dest, here) * capacity + position
        target_ref[row] = target
        place[pl.ds(row, 1), :] = jnp.where(places == target, 1.0, 0.0)
        length = length_ref[row].astype(f32)
        local = (slot - dest * per_group).astype(f32)
        facts[pl.ds(row, 1), :] = jnp.where(
            columns == 0, length, jnp.where(columns == 1, local, 0.0)
        )
        return carry

    lax.fori_loop(0, rows, put, 0)
    chosen = place[...].astype(bf16)
    place_ref[...] = chosen
    across = (((0,), (0,)), ((), ()))
    known = lax.dot_general(
        chosen, facts[...].astype(bf16), across, preferred_element_type=f32
    ).astype(bf16)
    hidden_copy.wait()
    state = lax.dot_general(
        chosen, hidden_ref[...], across, preferred_element_type=f32
    ).astype(bf16)
    for s in range(groups):
        block = slice(s * capacity, (s + 1) * capacity)
        outgoing[s][:, :width] = state[block]
        outgoing[s][:, width:] = known[block]


def pack_kernel(target_ref, key_hbm, value_hbm, *refs):
    groups = len(refs) - 4
    outgoing = refs[:groups]
    packed, key_ref, value_ref, sems = refs[groups:]
    rows, kv_local = key_ref.shape[:2]
    capacity = packed.shape[2]
    copies = copy_all([(key_hbm, key_ref), (value_hbm, value_ref)], sems)
    if groups * capacity > rows:
        packed[...] = jnp.zeros_like(packed)
    for copy in copies:
        copy.wait()

    def put(row, carry):
        target = target_ref[row]
        block = lax.div(target, capacity)
        position = target - block * capacity
        for g in range(kv_local):
            packed[block, g, position] = key_ref[row, g]
            packed[block, kv_local + g, position] = value_ref[row, g]
        return carry

    lax.fori_loop(0, rows, put, 0)
    for s in range(groups):
        outgoing[s][...] = packed[s]


def load_inputs_kernel(query, key, value, after, inputs, sems):
    pairs = []
    column = 0
    for weight in (query, key, value):
        width = weight.shape[1]
        pairs.append((weight, inputs.at[:, column : column + width]))
        column += width
    for copy in copy_all(pairs, sems):
        copy.wait()


def load_others_kernel(*refs):
    count = (len(refs) - 2) // 2
    for copy in copy_all(zip(refs[:count], refs[count + 1 : -1]), refs[-1]):
        copy.wait()


def own_slots(slot, total, rank):
    lane = lax.broadcasted_iota(jnp.int32, (1, 2 * rank), 1)
    second = (lane >= rank).astype(f32)
    return [slot == 2.0 * j + second for j in range(total // 2)]


def spread_over_slots(factor, own):
    twice = jnp.concatenate([factor, factor], axis=1)
    return jnp.concatenate([jnp.where(mask, twice, 0.0).astype(bf16) for mask in own], axis=1)


def pick_slot(product, own):
    wide = own[0].shape[1]
    picked = jnp.where(own[0], product[:, :wide], 0.0)
    for j in range(1, len(own)):
        picked = picked + jnp.where(own[j], product[:, j * wide : (j + 1) * wide], 0.0)
    return picked[:, : wide // 2] + picked[:, wide // 2 :]


def partial_low(state, gain, own, down_ref):
    scaled = (state * gain).astype(bf16)
    picked = []
    for kind in range(down_ref.shape[0]):
        product = lax.dot_general(scaled, down_ref[kind], NT, preferred_element_type=f32)
        picked.append(pick_slot(product, own).astype(bf16))
    return jnp.concatenate(picked, axis=1)


def enter_kernel(total, rank, order, *refs):
    groups = len(order)
    blocks = in_order(refs[:groups], order)
    gain_ref, down_hbm, send_ref, facts_ref, down_ref, sems = refs[groups:]
    width = down_ref.shape[2]
    pairs = []
    for kind in range(down_ref.shape[0]):
        for d in range(total):
            pairs.append(
                (
                    down_hbm.at[d, kind * rank : (kind + 1) * rank, :],
                    down_ref.at[kind, d * rank : (d + 1) * rank, :],
                )
            )
    copies = copy_all(pairs, sems)
    everything = jnp.concatenate([block[...] for block in blocks], axis=0)
    facts = everything[:, width:].astype(f32)
    own = own_slots(facts[:, 1:2], total, rank)
    facts_ref[...] = facts
    send_ref[:, :width] = everything[:, :width]
    for copy in copies:
        copy.wait()
    send_ref[:, width:] = partial_low(
        everything[:, :width].astype(f32), gain_ref[...], own, down_ref
    )


def new_state(own, received, state, up_ref):
    width = state.shape[1]
    low_out = received[0][:, width:].astype(f32)
    projected = received[0][:, :width].astype(f32)
    for part in received[1:]:
        low_out = low_out + part[:, width:].astype(f32)
        projected = projected + part[:, :width].astype(f32)
    spread = spread_over_slots(low_out, own)
    delta = jnp.dot(spread, up_ref[...], preferred_element_type=f32).astype(bf16)
    return (state.astype(f32) + projected + delta.astype(f32)).astype(bf16)


def between_kernel(total, rank, parts, *refs):
    received = refs[:parts]
    state_ref, facts_ref, up_ref, gain_ref, down_ref, send_ref = refs[parts:]
    width = down_ref.shape[2]
    own = own_slots(facts_ref[:, 1:2], total, rank)
    state = new_state(own, received, state_ref[:, :width], up_ref)
    send_ref[:, :width] = state
    send_ref[:, width:] = partial_low(state.astype(f32), gain_ref[...], own, down_ref)


def leave_kernel(total, rank, parts, *refs):
    received = refs[:parts]
    state_ref, facts_ref, up_ref = refs[parts : parts + 3]
    outgoing = refs[parts + 3 :]
    width = up_ref.shape[1]
    capacity = outgoing[0].shape[0]
    own = own_slots(facts_ref[:, 1:2], total, rank)
    state = new_state(own, received, state_ref[:, :width], up_ref)
    for s in range(len(outgoing)):
        outgoing[s][...] = state[s * capacity : (s + 1) * capacity]


def restore_kernel(order, place_ref, *refs):
    blocks, out_ref = in_order(refs[:-1], order), refs[-1]
    back = jnp.concatenate([block[...] for block in blocks], axis=0)
    out_ref[...] = jnp.dot(place_ref[...], back, preferred_element_type=f32).astype(bf16)


def norm_and_rotate(vector, gain, cosine, sine):
    head_dim = vector.shape[1]
    mean = jnp.mean(vector * vector, axis=1, keepdims=True)
    scaled = vector * lax.rsqrt(mean + epsilon) * gain
    return (scaled * cosine + pltpu.roll(scaled, head_dim // 2, 1) * sine).astype(bf16)


def project_slices(slices, masks, here, gain_ref, weight_ref):
    width = gain_ref.shape[2]
    products, squares, low = None, None, None
    for piece, mask in zip(slices, masks):
        source = jnp.bitwise_xor(here, mask)
        state = piece[:, :width].astype(f32)
        scaled = (state * gain_ref[source]).astype(bf16)
        features_there = pl.ds(pl.multiple_of(source * width, 64), width)
        product = jnp.dot(scaled, weight_ref[features_there, :], preferred_element_type=f32)
        square = jnp.sum(state * state, axis=1, keepdims=True)
        part = piece[:, width:].astype(f32)
        products = product if products is None else products + product
        squares = square if squares is None else squares + square
        low = part if low is None else low + part
    return products, squares, low


def early_kernel(masks, *refs):
    slices = refs[: len(masks)]
    index_ref, gain_ref, weight_ref, products_ref, squares_ref, low_ref = refs[len(masks) :]
    products, squares, low = project_slices(slices, masks, index_ref[0], gain_ref, weight_ref)
    products_ref[...] = products
    squares_ref[...] = jnp.broadcast_to(squares, squares_ref.shape)
    low_ref[...] = low


def step_kernel(total, rank, step, parts, masks, order, *refs):
    groups = len(order)
    refs = list(refs)

    def take(count):
        taken = refs[:count]
        del refs[:count]
        return taken

    slices = take(len(masks))
    (
        index_ref,
        products_ref,
        squares_ref,
        low_ref,
        facts_ref,
        gain_ref,
        weight_ref,
        query_up,
        key_up,
        value_up,
        query_gain,
        key_gain,
        cosine_ref,
        sine_ref,
        bias_ref,
    ) = take(15)
    cache = in_order(take(groups), order)
    earlier = take(2 * step)
    output_weight, output_down = take(2)
    outgoing = take(parts)
    key_fresh, value_fresh, attended, terms = refs
    features = weight_ref.shape[0]
    width = features // parts
    rows = products_ref.shape[0]
    head_dim = cache[0].shape[2]
    kv_local = cache[0].shape[0] // 2
    capacity = rows // groups
    query_width = query_up.shape[1]
    key_width = key_up.shape[1]
    heads = query_width // head_dim
    per_kv = heads // kv_local
    here = index_ref[0]

    own = own_slots(facts_ref[:, 1:2], total, rank)
    products, squares, low = project_slices(slices, masks, here, gain_ref, weight_ref)
    inverse = lax.rsqrt((squares_ref[:, :1] + squares) / features + epsilon)
    low = (low_ref[...] + low) * inverse

    def project(columns, up_ref, index):
        spread = spread_over_slots(low[:, index * rank : (index + 1) * rank], own)
        delta = jnp.dot(spread, up_ref[...], preferred_element_type=f32).astype(bf16)
        whole = (products_ref[:, columns] + products[:, columns]) * inverse
        return whole + delta.astype(f32)

    cosine = cosine_ref[step]
    sine = sine_ref[step]
    key = project(slice(query_width, query_width + key_width), key_up, 1)
    value = project(slice(query_width + key_width, None), value_up, 2).astype(bf16)
    for g in range(kv_local):
        columns = slice(g * head_dim, (g + 1) * head_dim)
        key_fresh[g] = norm_and_rotate(key[:, columns], key_gain[...], cosine, sine)
        value_fresh[g] = value[:, columns]
    query = project(slice(0, query_width), query_up, 0)
    query_heads = [
        norm_and_rotate(query[:, h * head_dim : (h + 1) * head_dim], query_gain[...], cosine, sine)
        for h in range(heads)
    ]

    scale = head_dim ** (-0.5)
    fresh_count = (step + 1) * capacity
    lanes = 128 * (-(-fresh_count // 128))
    filler = jnp.zeros((lanes - fresh_count, head_dim), bf16)
    key_place = lax.broadcasted_iota(jnp.int32, (per_kv * capacity, lanes), 1)
    own_row = lax.broadcasted_iota(jnp.int32, (per_kv * capacity, lanes), 0) % capacity
    same_row = (key_place % capacity == own_row) & (key_place < fresh_count)
    cached_count = bias_ref.shape[1]
    for b in range(groups):
        block = slice(b * capacity, (b + 1) * capacity)
        bias = jnp.concatenate([bias_ref[block, :]] * per_kv, axis=0)
        for g in range(kv_local):
            queries = jnp.concatenate(
                [query_heads[g * per_kv + h][block] for h in range(per_kv)], axis=0
            )
            fresh_keys = jnp.concatenate(
                [earlier[2 * t][g, block, :] for t in range(step)]
                + [key_fresh[g, block, :], filler],
                axis=0,
            )
            fresh_values = jnp.concatenate(
                [earlier[2 * t + 1][g, block, :] for t in range(step)]
                + [value_fresh[g, block, :], filler],
                axis=0,
            )
            cached = (
                lax.dot_general(queries, cache[b][g], NT, preferred_element_type=f32) * scale + bias
            )
            fresh = lax.dot_general(queries, fresh_keys, NT, preferred_element_type=f32) * scale
            fresh = jnp.where(same_row, fresh, blocked)
            scores = jnp.concatenate([cached, fresh], axis=1)
            largest = jnp.max(scores, axis=1, keepdims=True)
            weights = jnp.exp(scores - largest).astype(bf16)
            values = jnp.concatenate([cache[b][kv_local + g], fresh_values], axis=0)
            summing = jnp.concatenate([values, jnp.ones_like(values)], axis=1)
            mixed = jnp.dot(weights, summing, preferred_element_type=f32)
            mixed = (mixed[:, :head_dim] / mixed[:, head_dim:]).astype(bf16)
            for h in range(per_kv):
                head = g * per_kv + h
                attended[block, head * head_dim : (head + 1) * head_dim] = mixed[
                    h * capacity : (h + 1) * capacity
                ]

    attended_rows = attended[...]
    product = lax.dot_general(attended_rows, output_down[...], NT, preferred_element_type=f32)
    low_out = pick_slot(product, own).astype(bf16)
    for n in range(parts):
        term = jnp.dot(
            attended_rows,
            output_weight[:, n * width : (n + 1) * width],
            preferred_element_type=f32,
        )
        terms[jnp.bitwise_xor(here, n)] = term.astype(bf16)
    for mask in range(parts):
        outgoing[mask][:, :width] = terms[mask]
        outgoing[mask][:, width:] = low_out


def swap(block, axis, mask):
    return lax.ppermute(block, axis, [(i, i ^ mask) for i in range(lax.axis_size(axis))])


def swap_all(blocks, axis, order):
    return [blocks[0]] + [swap(blocks[mask], axis, mask) for mask in order[1:]]


def shards(
    hidden,
    input_norm_gain,
    query_projection_weight,
    key_projection_weight,
    value_projection_weight,
    query_norm_gain,
    key_norm_gain,
    output_projection_weight,
    stacked_down_factors,
    query_up_factor,
    key_up_factor,
    value_up_factor,
    output_down_factor,
    output_up_factor,
    cached_key_rows,
    cached_value_rows,
    cached_length_rows,
    domain_of_row,
    slot_of_domain,
):
    groups = lax.axis_size("wide")
    parts = lax.axis_size("narrow")
    wide_index = lax.axis_index("wide")
    narrow_index = lax.axis_index("narrow")
    row_group, width = hidden.shape
    capacity = row_group // 4
    rows = groups * capacity
    total = stacked_down_factors.shape[0]
    low_width = stacked_down_factors.shape[1]
    rank = output_up_factor.shape[1]
    _, kv_local, context, head_dim = cached_key_rows.shape
    features = input_norm_gain.shape[0]
    query_width = query_projection_weight.shape[1]

    load_cost = pl.CostEstimate(flops=0, bytes_accessed=20000000, transcendentals=0)
    smem = pl.BlockSpec(memory_space=pltpu.SMEM)
    vmem = pl.BlockSpec(memory_space=pltpu.VMEM)
    hbm = pl.BlockSpec(memory_space=pltpu.HBM)
    outgoing_shape = jax.ShapeDtypeStruct((capacity, width + 128), bf16)
    target, place, *outgoing = pl.pallas_call(
        route_kernel,
        out_shape=[
            jax.ShapeDtypeStruct((row_group,), jnp.int32),
            jax.ShapeDtypeStruct((row_group, rows), bf16),
        ]
        + [outgoing_shape] * groups,
        in_specs=[smem] + [hbm] * 4,
        out_specs=[smem] + [vmem] * (groups + 1),
        scratch_shapes=[
            pltpu.SMEM((groups,), jnp.int32),
            pltpu.VMEM((row_group, rows), f32),
            pltpu.VMEM((row_group, 128), f32),
            pltpu.SMEM(domain_of_row.shape, jnp.int32),
            pltpu.SMEM(slot_of_domain.shape, jnp.int32),
            pltpu.SMEM(cached_length_rows.shape, jnp.int32),
            pltpu.VMEM(hidden.shape, bf16),
            pltpu.SemaphoreType.DMA((4,)),
        ],
        compiler_params=kernel_params(8),
        name="route_rows",
    )(
        wide_index.reshape(1),
        in_hbm(domain_of_row),
        in_hbm(slot_of_domain),
        in_hbm(cached_length_rows),
        in_hbm(hidden),
    )
    by_group = [0] + list(range(groups - 1, 0, -1))
    arrived = swap_all(outgoing, "wide", by_group)
    packed_shape = (2 * kv_local, capacity, context, head_dim)
    packed = pl.pallas_call(
        pack_kernel,
        out_shape=[jax.ShapeDtypeStruct(packed_shape, bf16)] * groups,
        in_specs=[smem, hbm, hbm],
        out_specs=[vmem] * groups,
        scratch_shapes=[
            pltpu.VMEM((groups,) + packed_shape, bf16),
            pltpu.VMEM(cached_key_rows.shape, bf16),
            pltpu.VMEM(cached_value_rows.shape, bf16),
            pltpu.SemaphoreType.DMA((2,)),
        ],
        compiler_params=kernel_params(16),
        name="pack_cache",
    )(target, in_hbm(cached_key_rows), in_hbm(cached_value_rows))
    cache = swap_all(packed, "wide", by_group)
    cache = [block.reshape(2 * kv_local, capacity * context, head_dim) for block in cache]

    gain_rows = input_norm_gain.reshape(parts, 1, width)
    gain_slice = lax.dynamic_index_in_dim(gain_rows, narrow_index, 0, keepdims=False)
    sent_state = jax.ShapeDtypeStruct((rows, width + low_width), bf16)
    kinds = low_width // rank
    send, facts_here, down = pl.pallas_call(
        functools.partial(enter_kernel, total, rank, by_group),
        out_shape=[
            sent_state,
            jax.ShapeDtypeStruct((rows, 128), f32),
            jax.ShapeDtypeStruct((kinds, total * rank, width), bf16),
        ],
        in_specs=[vmem] * (groups + 1) + [hbm],
        out_specs=[vmem] * 3,
        scratch_shapes=[pltpu.SemaphoreType.DMA((kinds * total,))],
        compiler_params=kernel_params(8),
        name="enter",
    )(*arrived, gain_slice, in_hbm(stacked_down_factors))

    key_width = key_projection_weight.shape[1]
    input_width = query_width + 2 * key_width

    def load_inputs(after):
        return pl.pallas_call(
            load_inputs_kernel,
            out_shape=jax.ShapeDtypeStruct((features, input_width), bf16),
            in_specs=[hbm] * 3 + [vmem],
            out_specs=vmem,
            scratch_shapes=[pltpu.SemaphoreType.DMA((3,))],
            compiler_params=kernel_params(16),
            cost_estimate=load_cost,
            name="load_inputs",
        )(
            in_hbm(query_projection_weight),
            in_hbm(key_projection_weight),
            in_hbm(value_projection_weight),
            after,
        )

    def load_others(after):
        others = [
            query_up_factor.reshape(total * rank, query_width),
            key_up_factor.reshape(total * rank, key_width),
            value_up_factor.reshape(total * rank, key_width),
            output_projection_weight,
            output_down_factor.reshape(total * rank, query_width),
            output_up_factor.reshape(total * rank, width),
        ]
        return pl.pallas_call(
            load_others_kernel,
            out_shape=[jax.ShapeDtypeStruct(array.shape, bf16) for array in others],
            in_specs=[hbm] * len(others) + [vmem],
            out_specs=[vmem] * len(others),
            scratch_shapes=[pltpu.SemaphoreType.DMA((len(others),))],
            compiler_params=kernel_params(16),
            cost_estimate=load_cost,
            name="load_others",
        )(*[in_hbm(array) for array in others], after)

    lengths = facts_here[:, 0]
    frequency = rope_base ** (-(jnp.arange(head_dim // 2, dtype=f32) * 2.0) / head_dim)
    positions = lengths[None, :] + jnp.arange(STEPS, dtype=f32)[:, None]
    angles = positions[:, :, None] * frequency
    cosine = jnp.cos(angles)
    sine = jnp.sin(angles)
    cosine = jnp.concatenate([cosine, cosine], axis=-1)
    sine = jnp.concatenate([-sine, sine], axis=-1)
    key_index = jnp.arange(capacity * context)[None, :]
    visible = (key_index // context == (jnp.arange(rows) % capacity)[:, None]) & (
        (key_index % context).astype(f32) < lengths[:, None]
    )
    bias = jnp.where(visible, 0.0, blocked).astype(f32)

    query_gain = query_norm_gain.reshape(1, head_dim)
    key_gain = key_norm_gain.reshape(1, head_dim)
    index_here = narrow_index.reshape(1)
    sent_terms = jax.ShapeDtypeStruct((rows, width + rank), bf16)
    fresh = jax.ShapeDtypeStruct((kv_local, rows, head_dim), bf16)
    far = [mask for mask in range(2, parts) if mask % 2 == 0]
    early = [0, 1] + far
    late = [mask ^ 1 for mask in far]

    earlier = []
    for step in range(STEPS):
        from_far = [swap(send, "narrow", mask) for mask in far]
        slices = [send, swap(send, "narrow", 1)] + from_far
        passed_on = [swap(piece, "narrow", 1) for piece in from_far]
        if step == 0:
            input_weight = load_inputs(facts_here)
            query_up, key_up, value_up, output_weight, output_down, output_up = load_others(
                from_far[0]
            )
        sums = pl.pallas_call(
            functools.partial(early_kernel, early),
            out_shape=[
                jax.ShapeDtypeStruct((rows, input_width), f32),
                jax.ShapeDtypeStruct((rows, 128), f32),
                jax.ShapeDtypeStruct((rows, low_width), f32),
            ],
            in_specs=[vmem] * len(early) + [smem] + [vmem] * 2,
            out_specs=[vmem] * 3,
            compiler_params=kernel_params(16),
            cost_estimate=pl.CostEstimate(
                flops=2 * rows * features * input_width,
                bytes_accessed=10000000,
                transcendentals=0,
            ),
            name="project_early",
        )(*slices, index_here, gain_rows, input_weight)
        *terms, key_fresh, value_fresh = pl.pallas_call(
            functools.partial(step_kernel, total, rank, step, parts, late, by_group),
            out_shape=[sent_terms] * parts + [fresh] * 2,
            in_specs=[vmem] * len(late) + [smem] + [vmem] * (16 + groups + 2 * step),
            out_specs=[vmem] * (parts + 2),
            scratch_shapes=[
                pltpu.VMEM((rows, query_width), bf16),
                pltpu.VMEM((parts, rows, width), bf16),
            ],
            compiler_params=kernel_params(24),
            name="attend_step",
        )(
            *passed_on,
            index_here,
            *sums,
            facts_here,
            gain_rows,
            input_weight,
            query_up,
            key_up,
            value_up,
            query_gain,
            key_gain,
            cosine,
            sine,
            bias,
            *cache,
            *earlier,
            output_weight,
            output_down,
        )
        earlier += [key_fresh, value_fresh]
        received = swap_all(
            terms, "narrow", [0] + far + [mask + 1 for mask in far] + [1]
        )
        if step < STEPS - 1:
            send = pl.pallas_call(
                functools.partial(between_kernel, total, rank, parts),
                out_shape=sent_state,
                in_specs=[vmem] * (parts + 5),
                out_specs=vmem,
                compiler_params=kernel_params(8),
                name="between",
            )(*received, send, facts_here, output_up, gain_slice, down)
        else:
            leaving = pl.pallas_call(
                functools.partial(leave_kernel, total, rank, parts),
                out_shape=[jax.ShapeDtypeStruct((capacity, width), bf16)] * groups,
                in_specs=[vmem] * (parts + 3),
                out_specs=[vmem] * groups,
                compiler_params=kernel_params(8),
                name="leave",
            )(*received, send, facts_here, output_up)

    back = swap_all(leaving, "wide", by_group)
    return pl.pallas_call(
        functools.partial(restore_kernel, by_group),
        out_shape=jax.ShapeDtypeStruct((row_group, width), bf16),
        in_specs=[vmem] * (groups + 1),
        out_specs=vmem,
        compiler_params=kernel_params(8),
        name="restore",
    )(place, *back)


def solution(mesh):
    placed = (
        P(("parts", "wide"), "narrow"),
        P(),
        P(None, "narrow"),
        P(None, "narrow"),
        P(None, "narrow"),
        P(),
        P(),
        P("narrow", None),
        P(("parts", "wide"), None, "narrow"),
        P(("parts", "wide"), None, "narrow"),
        P(("parts", "wide"), None, "narrow"),
        P(("parts", "wide"), None, "narrow"),
        P(("parts", "wide"), None, "narrow"),
        P(("parts", "wide"), None, "narrow"),
        P(("parts", "wide"), "narrow", None, None),
        P(("parts", "wide"), "narrow", None, None),
        P(("parts", "wide")),
        P("parts"),
        P("parts"),
    )
    return jax.shard_map(
        shards,
        mesh=mesh,
        in_specs=placed,
        out_specs=P(("parts", "wide"), "narrow"),
        check_vma=False,
    )
```

```python
import functools

import jax
import jax.numpy as jnp
from jax import lax
from jax.experimental import pallas as pl
from jax.experimental.pallas import tpu as pltpu
from jax.sharding import PartitionSpec as P

STEPS = 4

epsilon = 1e-06
rope_base = 1000000.0
blocked = -1e30
f32 = jnp.float32
bf16 = jnp.bfloat16

NT = (((1,), (1,)), ((), ()))
NN = (((1,), (0,)), ((), ()))


def kernel_params(mib):
    return pltpu.CompilerParams(vmem_limit_bytes=mib * 1024 * 1024)


def in_hbm(array):
    return pltpu.with_memory_space_constraint(array, pltpu.HBM)


def in_order(refs, order):
    return [refs[order.index(block)] for block in range(len(order))]


def copy_all(pairs, sems):
    copies = [
        pltpu.make_async_copy(source, target, sems.at[index])
        for index, (source, target) in enumerate(pairs)
    ]
    for copy in copies:
        copy.start()
    return copies


def route_kernel(
    group_ref, domain_hbm, slot_hbm, length_hbm, hidden_hbm, target_ref, place_ref, *refs
):
    groups = len(refs) - 8
    outgoing = refs[:groups]
    count, place, facts, domain_ref, slot_ref, length_ref, hidden_ref, sems = refs[groups:]
    rows, width = hidden_ref.shape
    capacity = outgoing[0].shape[0]
    per_group = slot_ref.shape[0] // groups
    here = group_ref[0]
    *tables, hidden_copy = copy_all(
        [
            (domain_hbm, domain_ref),
            (slot_hbm, slot_ref),
            (length_hbm, length_ref),
            (hidden_hbm, hidden_ref),
        ],
        sems,
    )
    for group in range(groups):
        count[group] = 0
    places = lax.broadcasted_iota(jnp.int32, (1, groups * capacity), 1)
    columns = lax.broadcasted_iota(jnp.int32, (1, facts.shape[1]), 1)
    for copy in tables:
        copy.wait()

    def put(row, carry):
        slot = slot_ref[domain_ref[here * rows + row]]
        dest = lax.div(slot, per_group)
        position = jnp.minimum(count[dest], capacity - 1)
        count[dest] = position + 1
        target = jnp.bitwise_xor(dest, here) * capacity + position
        target_ref[row] = target
        place[pl.ds(row, 1), :] = jnp.where(places == target, 1.0, 0.0)
        length = length_ref[row].astype(f32)
        local = (slot - dest * per_group).astype(f32)
        facts[pl.ds(row, 1), :] = jnp.where(
            columns == 0, length, jnp.where(columns == 1, local, 0.0)
        )
        return carry

    lax.fori_loop(0, rows, put, 0)
    chosen = place[...].astype(bf16)
    place_ref[...] = chosen
    across = (((0,), (0,)), ((), ()))
    known = lax.dot_general(
        chosen, facts[...].astype(bf16), across, preferred_element_type=f32
    ).astype(bf16)
    hidden_copy.wait()
    state = lax.dot_general(
        chosen, hidden_ref[...], across, preferred_element_type=f32
    ).astype(bf16)
    for s in range(groups):
        block = slice(s * capacity, (s + 1) * capacity)
        outgoing[s][:, :width] = state[block]
        outgoing[s][:, width:] = known[block]


def pack_kernel(target_ref, key_hbm, value_hbm, down_hbm, *refs):
    groups = len(refs) - 5
    outgoing = refs[:groups]
    down_ref, packed, key_ref, value_ref, sems = refs[groups:]
    rows, kv_local = key_ref.shape[:2]
    capacity = packed.shape[2]
    kinds = down_ref.shape[0]
    total = down_hbm.shape[0]
    rank = down_hbm.shape[1] // kinds
    pairs = [(key_hbm, key_ref), (value_hbm, value_ref)]
    for kind in range(kinds):
        for d in range(total):
            pairs.append(
                (
                    down_hbm.at[d, kind * rank : (kind + 1) * rank, :],
                    down_ref.at[kind, d * rank : (d + 1) * rank, :],
                )
            )
    copies = copy_all(pairs, sems)
    if groups * capacity > rows:
        packed[...] = jnp.zeros_like(packed)
    for copy in copies[:2]:
        copy.wait()

    def put(row, carry):
        target = target_ref[row]
        block = lax.div(target, capacity)
        position = target - block * capacity
        for g in range(kv_local):
            packed[block, g, position] = key_ref[row, g]
            packed[block, kv_local + g, position] = value_ref[row, g]
        return carry

    lax.fori_loop(0, rows, put, 0)
    for s in range(groups):
        outgoing[s][...] = packed[s]
    for copy in copies[2:]:
        copy.wait()


def load_inputs_kernel(query, key, value, after, inputs, sems):
    pairs = []
    column = 0
    for weight in (query, key, value):
        width = weight.shape[1]
        pairs.append((weight, inputs.at[:, column : column + width]))
        column += width
    for copy in copy_all(pairs, sems):
        copy.wait()


def load_others_kernel(*refs):
    count = (len(refs) - 4) // 2 - 1
    sources, output_down, down, _ = refs[:count], *refs[count : count + 3]
    targets = refs[count + 3 : 2 * count + 3]
    output_down_across, down_across, held, sems = refs[2 * count + 3 :]
    copies = copy_all([(output_down, held), *zip(sources, targets)], sems)
    for kind in range(down.shape[0]):
        down_across[kind] = down[kind].T
    copies[0].wait()
    output_down_across[...] = held[...].T
    for copy in copies[1:]:
        copy.wait()


def own_slots(slot, total, rank):
    lane = lax.broadcasted_iota(jnp.int32, (1, 2 * rank), 1)
    second = (lane >= rank).astype(f32)
    return [slot == 2.0 * j + second for j in range(total // 2)]


def spread_over_slots(factor, own):
    twice = jnp.concatenate([factor, factor], axis=1)
    return jnp.concatenate([jnp.where(mask, twice, 0.0).astype(bf16) for mask in own], axis=1)


def pick_slot(product, own):
    wide = own[0].shape[1]
    picked = jnp.where(own[0], product[:, :wide], 0.0)
    for j in range(1, len(own)):
        picked = picked + jnp.where(own[j], product[:, j * wide : (j + 1) * wide], 0.0)
    return picked[:, : wide // 2] + picked[:, wide // 2 :]


def partial_low(state, gain, own, down_ref, form):
    scaled = (state * gain).astype(bf16)
    picked = []
    for kind in range(down_ref.shape[0]):
        product = lax.dot_general(scaled, down_ref[kind], form, preferred_element_type=f32)
        picked.append(pick_slot(product, own).astype(bf16))
    return jnp.concatenate(picked, axis=1)


def enter_kernel(total, rank, order, *refs):
    groups = len(order)
    blocks = in_order(refs[:groups], order)
    gain_ref, down_ref, send_ref, facts_ref = refs[groups:]
    width = down_ref.shape[2]
    everything = jnp.concatenate([block[...] for block in blocks], axis=0)
    facts = everything[:, width:].astype(f32)
    own = own_slots(facts[:, 1:2], total, rank)
    facts_ref[...] = facts
    send_ref[:, :width] = everything[:, :width]
    send_ref[:, width:] = partial_low(
        everything[:, :width].astype(f32), gain_ref[...], own, down_ref, NT
    )


def new_state(own, received, state, up_ref):
    width = state.shape[1]
    low_out = received[0][:, width:].astype(f32)
    projected = received[0][:, :width].astype(f32)
    for part in received[1:]:
        low_out = low_out + part[:, width:].astype(f32)
        projected = projected + part[:, :width].astype(f32)
    spread = spread_over_slots(low_out, own)
    delta = jnp.dot(spread, up_ref[...], preferred_element_type=f32).astype(bf16)
    return (state.astype(f32) + projected + delta.astype(f32)).astype(bf16)


def between_kernel(total, rank, parts, *refs):
    received = refs[:parts]
    state_ref, facts_ref, up_ref, gain_ref, down_ref, send_ref = refs[parts:]
    width = down_ref.shape[1]
    own = own_slots(facts_ref[:, 1:2], total, rank)
    state = new_state(own, received, state_ref[:, :width], up_ref)
    send_ref[:, :width] = state
    send_ref[:, width:] = partial_low(state.astype(f32), gain_ref[...], own, down_ref, NN)


def leave_kernel(total, rank, parts, *refs):
    received = refs[:parts]
    state_ref, facts_ref, up_ref = refs[parts : parts + 3]
    outgoing = refs[parts + 3 :]
    width = up_ref.shape[1]
    capacity = outgoing[0].shape[0]
    own = own_slots(facts_ref[:, 1:2], total, rank)
    state = new_state(own, received, state_ref[:, :width], up_ref)
    for s in range(len(outgoing)):
        outgoing[s][...] = state[s * capacity : (s + 1) * capacity]


def restore_kernel(order, place_ref, *refs):
    blocks, out_ref = in_order(refs[:-1], order), refs[-1]
    back = jnp.concatenate([block[...] for block in blocks], axis=0)
    out_ref[...] = jnp.dot(place_ref[...], back, preferred_element_type=f32).astype(bf16)


def norm_and_rotate(vector, gain, cosine, sine):
    head_dim = vector.shape[1]
    mean = jnp.mean(vector * vector, axis=1, keepdims=True)
    scaled = vector * lax.rsqrt(mean + epsilon) * gain
    return (scaled * cosine + pltpu.roll(scaled, head_dim // 2, 1) * sine).astype(bf16)


def project_slices(slices, masks, here, gain_ref, weight_ref):
    width = gain_ref.shape[2]
    products, squares, low = None, None, None
    for piece, mask in zip(slices, masks):
        source = jnp.bitwise_xor(here, mask)
        state = piece[:, :width].astype(f32)
        scaled = (state * gain_ref[source]).astype(bf16)
        features_there = pl.ds(pl.multiple_of(source * width, 64), width)
        product = jnp.dot(scaled, weight_ref[features_there, :], preferred_element_type=f32)
        square = jnp.sum(state * state, axis=1, keepdims=True)
        part = piece[:, width:].astype(f32)
        products = product if products is None else products + product
        squares = square if squares is None else squares + square
        low = part if low is None else low + part
    return products, squares, low


def early_kernel(masks, *refs):
    slices = refs[: len(masks)]
    index_ref, gain_ref, weight_ref, products_ref, squares_ref, low_ref = refs[len(masks) :]
    products, squares, low = project_slices(slices, masks, index_ref[0], gain_ref, weight_ref)
    products_ref[...] = products
    squares_ref[...] = jnp.broadcast_to(squares, squares_ref.shape)
    low_ref[...] = low


def step_kernel(total, rank, step, parts, masks, order, *refs):
    groups = len(order)
    refs = list(refs)

    def take(count):
        taken = refs[:count]
        del refs[:count]
        return taken

    slices = take(len(masks))
    (
        index_ref,
        products_ref,
        squares_ref,
        low_ref,
        facts_ref,
        gain_ref,
        weight_ref,
        query_up,
        key_up,
        value_up,
        query_gain,
        key_gain,
        cosine_ref,
        sine_ref,
        bias_ref,
    ) = take(15)
    cache = in_order(take(groups), order)
    earlier = take(2 * step)
    output_weight, output_down = take(2)
    outgoing = take(parts)
    key_fresh, value_fresh, attended, terms = refs
    features = weight_ref.shape[0]
    width = features // parts
    rows = products_ref.shape[0]
    head_dim = cache[0].shape[2]
    kv_local = cache[0].shape[0] // 2
    capacity = rows // groups
    query_width = query_up.shape[1]
    key_width = key_up.shape[1]
    heads = query_width // head_dim
    per_kv = heads // kv_local
    here = index_ref[0]

    own = own_slots(facts_ref[:, 1:2], total, rank)
    products, squares, low = project_slices(slices, masks, here, gain_ref, weight_ref)
    inverse = lax.rsqrt((squares_ref[:, :1] + squares) / features + epsilon)
    low = (low_ref[...] + low) * inverse

    def project(columns, up_ref, index):
        spread = spread_over_slots(low[:, index * rank : (index + 1) * rank], own)
        delta = jnp.dot(spread, up_ref[...], preferred_element_type=f32).astype(bf16)
        whole = (products_ref[:, columns] + products[:, columns]) * inverse
        return whole + delta.astype(f32)

    cosine = cosine_ref[step]
    sine = sine_ref[step]
    key = project(slice(query_width, query_width + key_width), key_up, 1)
    value = project(slice(query_width + key_width, None), value_up, 2).astype(bf16)
    for g in range(kv_local):
        columns = slice(g * head_dim, (g + 1) * head_dim)
        key_fresh[g] = norm_and_rotate(key[:, columns], key_gain[...], cosine, sine)
        value_fresh[g] = value[:, columns]
    query = project(slice(0, query_width), query_up, 0)
    query_heads = [
        norm_and_rotate(query[:, h * head_dim : (h + 1) * head_dim], query_gain[...], cosine, sine)
        for h in range(heads)
    ]

    scale = head_dim ** (-0.5)
    fresh_count = (step + 1) * capacity
    lanes = 128 * (-(-fresh_count // 128))
    filler = jnp.zeros((lanes - fresh_count, head_dim), bf16)
    key_place = lax.broadcasted_iota(jnp.int32, (per_kv * capacity, lanes), 1)
    own_row = lax.broadcasted_iota(jnp.int32, (per_kv * capacity, lanes), 0) % capacity
    same_row = (key_place % capacity == own_row) & (key_place < fresh_count)
    def fresh_rows(now, which, g, block):
        return jnp.concatenate(
            [earlier[2 * t + which][g, block, :] for t in range(step)] + [now[g, block, :], filler],
            axis=0,
        )

    together = 4
    for first in range(0, groups, together):
        blocks = [
            (b, slice(b * capacity, (b + 1) * capacity), g)
            for g in range(kv_local)
            for b in range(first, min(first + together, groups))
        ]
        scores = []
        for b, block, g in blocks:
            queries = jnp.concatenate(
                [query_heads[g * per_kv + h][block] for h in range(per_kv)], axis=0
            )
            bias = jnp.concatenate([bias_ref[block, :]] * per_kv, axis=0)
            cached = lax.dot_general(queries, cache[b][g], NT, preferred_element_type=f32)
            fresh = lax.dot_general(
                queries, fresh_rows(key_fresh, 0, g, block), NT, preferred_element_type=f32
            )
            fresh = jnp.where(same_row, fresh * scale, blocked)
            scores.append(jnp.concatenate([cached * scale + bias, fresh], axis=1))
        largest = [jnp.max(score, axis=1, keepdims=True) for score in scores]
        weights = [
            jnp.exp(score - top).astype(bf16) for score, top in zip(scores, largest)
        ]
        mixes = []
        for (b, block, g), weight in zip(blocks, weights):
            values = jnp.concatenate(
                [cache[b][kv_local + g], fresh_rows(value_fresh, 1, g, block)], axis=0
            )
            summing = jnp.concatenate([values, jnp.ones_like(values)], axis=1)
            mixes.append(jnp.dot(weight, summing, preferred_element_type=f32))
        for (b, block, g), mixed in zip(blocks, mixes):
            mixed = (mixed[:, :head_dim] / mixed[:, head_dim:]).astype(bf16)
            for h in range(per_kv):
                head = g * per_kv + h
                attended[block, head * head_dim : (head + 1) * head_dim] = mixed[
                    h * capacity : (h + 1) * capacity
                ]

    attended_rows = attended[...]
    product = jnp.dot(attended_rows, output_down[...], preferred_element_type=f32)
    low_out = pick_slot(product, own).astype(bf16)
    for n in range(parts):
        term = jnp.dot(
            attended_rows,
            output_weight[:, n * width : (n + 1) * width],
            preferred_element_type=f32,
        )
        terms[jnp.bitwise_xor(here, n)] = term.astype(bf16)
    for mask in range(parts):
        outgoing[mask][:, :width] = terms[mask]
        outgoing[mask][:, width:] = low_out


def swap(block, axis, mask):
    return lax.ppermute(block, axis, [(i, i ^ mask) for i in range(lax.axis_size(axis))])


def swap_all(blocks, axis, order):
    return [blocks[0]] + [swap(blocks[mask], axis, mask) for mask in order[1:]]


def shards(
    hidden,
    input_norm_gain,
    query_projection_weight,
    key_projection_weight,
    value_projection_weight,
    query_norm_gain,
    key_norm_gain,
    output_projection_weight,
    stacked_down_factors,
    query_up_factor,
    key_up_factor,
    value_up_factor,
    output_down_factor,
    output_up_factor,
    cached_key_rows,
    cached_value_rows,
    cached_length_rows,
    domain_of_row,
    slot_of_domain,
):
    groups = lax.axis_size("wide")
    parts = lax.axis_size("narrow")
    wide_index = lax.axis_index("wide")
    narrow_index = lax.axis_index("narrow")
    row_group, width = hidden.shape
    capacity = row_group // 4
    rows = groups * capacity
    total = stacked_down_factors.shape[0]
    low_width = stacked_down_factors.shape[1]
    rank = output_up_factor.shape[1]
    _, kv_local, context, head_dim = cached_key_rows.shape
    features = input_norm_gain.shape[0]
    query_width = query_projection_weight.shape[1]

    load_cost = pl.CostEstimate(flops=0, bytes_accessed=20000000, transcendentals=0)
    smem = pl.BlockSpec(memory_space=pltpu.SMEM)
    vmem = pl.BlockSpec(memory_space=pltpu.VMEM)
    hbm = pl.BlockSpec(memory_space=pltpu.HBM)
    outgoing_shape = jax.ShapeDtypeStruct((capacity, width + 128), bf16)
    target, place, *outgoing = pl.pallas_call(
        route_kernel,
        out_shape=[
            jax.ShapeDtypeStruct((row_group,), jnp.int32),
            jax.ShapeDtypeStruct((row_group, rows), bf16),
        ]
        + [outgoing_shape] * groups,
        in_specs=[smem] + [hbm] * 4,
        out_specs=[smem] + [vmem] * (groups + 1),
        scratch_shapes=[
            pltpu.SMEM((groups,), jnp.int32),
            pltpu.VMEM((row_group, rows), f32),
            pltpu.VMEM((row_group, 128), f32),
            pltpu.SMEM(domain_of_row.shape, jnp.int32),
            pltpu.SMEM(slot_of_domain.shape, jnp.int32),
            pltpu.SMEM(cached_length_rows.shape, jnp.int32),
            pltpu.VMEM(hidden.shape, bf16),
            pltpu.SemaphoreType.DMA((4,)),
        ],
        compiler_params=kernel_params(8),
        name="route_rows",
    )(
        wide_index.reshape(1),
        in_hbm(domain_of_row),
        in_hbm(slot_of_domain),
        in_hbm(cached_length_rows),
        in_hbm(hidden),
    )
    by_group = [0] + list(range(groups - 1, 0, -1))
    arrived = swap_all(outgoing, "wide", by_group)
    packed_shape = (2 * kv_local, capacity, context, head_dim)
    kinds = low_width // rank
    *packed, down = pl.pallas_call(
        pack_kernel,
        out_shape=[jax.ShapeDtypeStruct(packed_shape, bf16)] * groups
        + [jax.ShapeDtypeStruct((kinds, total * rank, width), bf16)],
        in_specs=[smem, hbm, hbm, hbm],
        out_specs=[vmem] * (groups + 1),
        scratch_shapes=[
            pltpu.VMEM((groups,) + packed_shape, bf16),
            pltpu.VMEM(cached_key_rows.shape, bf16),
            pltpu.VMEM(cached_value_rows.shape, bf16),
            pltpu.SemaphoreType.DMA((2 + kinds * total,)),
        ],
        compiler_params=kernel_params(16),
        name="pack_cache",
    )(target, in_hbm(cached_key_rows), in_hbm(cached_value_rows), in_hbm(stacked_down_factors))
    cache = swap_all(packed, "wide", by_group)
    cache = [block.reshape(2 * kv_local, capacity * context, head_dim) for block in cache]

    gain_rows = input_norm_gain.reshape(parts, 1, width)
    gain_slice = lax.dynamic_index_in_dim(gain_rows, narrow_index, 0, keepdims=False)
    sent_state = jax.ShapeDtypeStruct((rows, width + low_width), bf16)
    send, facts_here = pl.pallas_call(
        functools.partial(enter_kernel, total, rank, by_group),
        out_shape=[sent_state, jax.ShapeDtypeStruct((rows, 128), f32)],
        in_specs=[vmem] * (groups + 2),
        out_specs=[vmem] * 2,
        compiler_params=kernel_params(8),
        name="enter",
    )(*arrived, gain_slice, down)

    key_width = key_projection_weight.shape[1]
    input_width = query_width + 2 * key_width

    def load_inputs(after):
        return pl.pallas_call(
            load_inputs_kernel,
            out_shape=jax.ShapeDtypeStruct((features, input_width), bf16),
            in_specs=[hbm] * 3 + [vmem],
            out_specs=vmem,
            scratch_shapes=[pltpu.SemaphoreType.DMA((3,))],
            compiler_params=kernel_params(16),
            cost_estimate=load_cost,
            name="load_inputs",
        )(
            in_hbm(query_projection_weight),
            in_hbm(key_projection_weight),
            in_hbm(value_projection_weight),
            after,
        )

    def load_others(after):
        others = [
            query_up_factor.reshape(total * rank, query_width),
            key_up_factor.reshape(total * rank, key_width),
            value_up_factor.reshape(total * rank, key_width),
            output_projection_weight,
            output_up_factor.reshape(total * rank, width),
        ]
        turned = [
            jax.ShapeDtypeStruct((query_width, total * rank), bf16),
            jax.ShapeDtypeStruct((kinds, width, total * rank), bf16),
        ]
        return pl.pallas_call(
            load_others_kernel,
            out_shape=[jax.ShapeDtypeStruct(array.shape, bf16) for array in others] + turned,
            in_specs=[hbm] * (len(others) + 1) + [vmem] * 2,
            out_specs=[vmem] * (len(others) + 2),
            scratch_shapes=[
                pltpu.VMEM((total * rank, query_width), bf16),
                pltpu.SemaphoreType.DMA((len(others) + 1,)),
            ],
            compiler_params=kernel_params(20),
            cost_estimate=load_cost,
            name="load_others",
        )(
            *[in_hbm(array) for array in others],
            in_hbm(output_down_factor.reshape(total * rank, query_width)),
            down,
            after,
        )

    lengths = facts_here[:, 0]
    frequency = rope_base ** (-(jnp.arange(head_dim // 2, dtype=f32) * 2.0) / head_dim)
    positions = lengths[None, :] + jnp.arange(STEPS, dtype=f32)[:, None]
    angles = positions[:, :, None] * frequency
    cosine = jnp.cos(angles)
    sine = jnp.sin(angles)
    cosine = jnp.concatenate([cosine, cosine], axis=-1)
    sine = jnp.concatenate([-sine, sine], axis=-1)
    key_index = jnp.arange(capacity * context)[None, :]
    visible = (key_index // context == (jnp.arange(rows) % capacity)[:, None]) & (
        (key_index % context).astype(f32) < lengths[:, None]
    )
    bias = jnp.where(visible, 0.0, blocked).astype(f32)

    query_gain = query_norm_gain.reshape(1, head_dim)
    key_gain = key_norm_gain.reshape(1, head_dim)
    index_here = narrow_index.reshape(1)
    sent_terms = jax.ShapeDtypeStruct((rows, width + rank), bf16)
    fresh = jax.ShapeDtypeStruct((kv_local, rows, head_dim), bf16)
    far = [mask for mask in range(2, parts) if mask % 2 == 0]
    early = [0, 1] + far
    late = [mask ^ 1 for mask in far]

    earlier = []
    for step in range(STEPS):
        from_far = [swap(send, "narrow", mask) for mask in far]
        from_near = swap(send, "narrow", 1)
        if step == 0:
            input_weight = load_inputs(facts_here)
            input_weight, *from_far = lax.optimization_barrier((input_weight, *from_far))
        passed_on = [swap(piece, "narrow", 1) for piece in from_far]
        if step == 0:
            *others, output_down, down_across = load_others(from_far[0])
            query_up, key_up, value_up, output_weight, output_up = others
        sums = pl.pallas_call(
            functools.partial(early_kernel, early),
            out_shape=[
                jax.ShapeDtypeStruct((rows, input_width), f32),
                jax.ShapeDtypeStruct((rows, 128), f32),
                jax.ShapeDtypeStruct((rows, low_width), f32),
            ],
            in_specs=[vmem] * len(early) + [smem] + [vmem] * 2,
            out_specs=[vmem] * 3,
            compiler_params=kernel_params(16),
            cost_estimate=pl.CostEstimate(
                flops=2 * rows * features * input_width,
                bytes_accessed=10000000,
                transcendentals=0,
            ),
            name="project_early",
        )(send, from_near, *from_far, index_here, gain_rows, input_weight)
        *terms, key_fresh, value_fresh = pl.pallas_call(
            functools.partial(step_kernel, total, rank, step, parts, late, by_group),
            out_shape=[sent_terms] * parts + [fresh] * 2,
            in_specs=[vmem] * len(late) + [smem] + [vmem] * (16 + groups + 2 * step),
            out_specs=[vmem] * (parts + 2),
            scratch_shapes=[
                pltpu.VMEM((rows, query_width), bf16),
                pltpu.VMEM((parts, rows, width), bf16),
            ],
            compiler_params=kernel_params(24),
            name="attend_step",
        )(
            *passed_on,
            index_here,
            *sums,
            facts_here,
            gain_rows,
            input_weight,
            query_up,
            key_up,
            value_up,
            query_gain,
            key_gain,
            cosine,
            sine,
            bias,
            *cache,
            *earlier,
            output_weight,
            output_down,
        )
        earlier += [key_fresh, value_fresh]
        received = swap_all(
            terms, "narrow", [0] + far + [mask + 1 for mask in far] + [1]
        )
        if step < STEPS - 1:
            send = pl.pallas_call(
                functools.partial(between_kernel, total, rank, parts),
                out_shape=sent_state,
                in_specs=[vmem] * (parts + 5),
                out_specs=vmem,
                compiler_params=kernel_params(8),
                name="between",
            )(*received, send, facts_here, output_up, gain_slice, down_across)
        else:
            leaving = pl.pallas_call(
                functools.partial(leave_kernel, total, rank, parts),
                out_shape=[jax.ShapeDtypeStruct((capacity, width), bf16)] * groups,
                in_specs=[vmem] * (parts + 3),
                out_specs=[vmem] * groups,
                compiler_params=kernel_params(8),
                name="leave",
            )(*received, send, facts_here, output_up)

    back = swap_all(leaving, "wide", by_group)
    return pl.pallas_call(
        functools.partial(restore_kernel, by_group),
        out_shape=jax.ShapeDtypeStruct((row_group, width), bf16),
        in_specs=[vmem] * (groups + 1),
        out_specs=vmem,
        compiler_params=kernel_params(8),
        name="restore",
    )(place, *back)


def solution(mesh):
    placed = (
        P(("parts", "wide"), "narrow"),
        P(),
        P(None, "narrow"),
        P(None, "narrow"),
        P(None, "narrow"),
        P(),
        P(),
        P("narrow", None),
        P(("parts", "wide"), None, "narrow"),
        P(("parts", "wide"), None, "narrow"),
        P(("parts", "wide"), None, "narrow"),
        P(("parts", "wide"), None, "narrow"),
        P(("parts", "wide"), None, "narrow"),
        P(("parts", "wide"), None, "narrow"),
        P(("parts", "wide"), "narrow", None, None),
        P(("parts", "wide"), "narrow", None, None),
        P(("parts", "wide")),
        P("parts"),
        P("parts"),
    )
    return jax.shard_map(
        shards,
        mesh=mesh,
        in_specs=placed,
        out_specs=P(("parts", "wide"), "narrow"),
        check_vma=False,
    )
```

```python
import functools

import jax
import jax.numpy as jnp
from jax import lax
from jax.experimental import pallas as pl
from jax.experimental.pallas import tpu as pltpu
from jax.sharding import PartitionSpec as P

STEPS = 4

epsilon = 1e-06
rope_base = 1000000.0
blocked = -1e30
f32 = jnp.float32
bf16 = jnp.bfloat16

NT = (((1,), (1,)), ((), ()))
NN = (((1,), (0,)), ((), ()))


def kernel_params(mib):
    return pltpu.CompilerParams(vmem_limit_bytes=mib * 1024 * 1024)


def in_hbm(array):
    return pltpu.with_memory_space_constraint(array, pltpu.HBM)


def in_order(refs, order):
    return [refs[order.index(block)] for block in range(len(order))]


def copy_all(pairs, sems):
    copies = [
        pltpu.make_async_copy(source, target, sems.at[index])
        for index, (source, target) in enumerate(pairs)
    ]
    for copy in copies:
        copy.start()
    return copies


def route_kernel(
    group_ref, domain_hbm, slot_hbm, length_hbm, hidden_hbm, target_ref, place_ref, *refs
):
    groups = len(refs) - 8
    outgoing = refs[:groups]
    count, place, facts, domain_ref, slot_ref, length_ref, hidden_ref, sems = refs[groups:]
    rows, width = hidden_ref.shape
    capacity = outgoing[0].shape[0]
    per_group = slot_ref.shape[0] // groups
    here = group_ref[0]
    *tables, hidden_copy = copy_all(
        [
            (domain_hbm, domain_ref),
            (slot_hbm, slot_ref),
            (length_hbm, length_ref),
            (hidden_hbm, hidden_ref),
        ],
        sems,
    )
    for group in range(groups):
        count[group] = 0
    places = lax.broadcasted_iota(jnp.int32, (1, groups * capacity), 1)
    columns = lax.broadcasted_iota(jnp.int32, (1, facts.shape[1]), 1)
    for copy in tables:
        copy.wait()

    def put(row, carry):
        slot = slot_ref[domain_ref[here * rows + row]]
        dest = lax.div(slot, per_group)
        position = jnp.minimum(count[dest], capacity - 1)
        count[dest] = position + 1
        target = jnp.bitwise_xor(dest, here) * capacity + position
        target_ref[row] = target
        place[pl.ds(row, 1), :] = jnp.where(places == target, 1.0, 0.0)
        length = length_ref[row].astype(f32)
        local = (slot - dest * per_group).astype(f32)
        facts[pl.ds(row, 1), :] = jnp.where(
            columns == 0, length, jnp.where(columns == 1, local, 0.0)
        )
        return carry

    lax.fori_loop(0, rows, put, 0)
    chosen = place[...].astype(bf16)
    place_ref[...] = chosen
    across = (((0,), (0,)), ((), ()))
    known = lax.dot_general(
        chosen, facts[...].astype(bf16), across, preferred_element_type=f32
    ).astype(bf16)
    hidden_copy.wait()
    state = lax.dot_general(
        chosen, hidden_ref[...], across, preferred_element_type=f32
    ).astype(bf16)
    for s in range(groups):
        block = slice(s * capacity, (s + 1) * capacity)
        outgoing[s][:, :width] = state[block]
        outgoing[s][:, width:] = known[block]


def pack_kernel(target_ref, key_hbm, value_hbm, down_hbm, *refs):
    groups = len(refs) - 5
    outgoing = refs[:groups]
    down_ref, packed, key_ref, value_ref, sems = refs[groups:]
    rows, kv_local = key_ref.shape[:2]
    capacity = packed.shape[2]
    kinds = down_ref.shape[0]
    total = down_hbm.shape[0]
    rank = down_hbm.shape[1] // kinds
    pairs = [(key_hbm, key_ref), (value_hbm, value_ref)]
    for kind in range(kinds):
        for d in range(total):
            pairs.append(
                (
                    down_hbm.at[d, kind * rank : (kind + 1) * rank, :],
                    down_ref.at[kind, d * rank : (d + 1) * rank, :],
                )
            )
    copies = copy_all(pairs, sems)
    if groups * capacity > rows:
        packed[...] = jnp.zeros_like(packed)
    for copy in copies[:2]:
        copy.wait()

    def put(row, carry):
        target = target_ref[row]
        block = lax.div(target, capacity)
        position = target - block * capacity
        for g in range(kv_local):
            packed[block, g, position] = key_ref[row, g]
            packed[block, kv_local + g, position] = value_ref[row, g]
        return carry

    lax.fori_loop(0, rows, put, 0)
    for s in range(groups):
        outgoing[s][...] = packed[s]
    for copy in copies[2:]:
        copy.wait()


def load_inputs_kernel(turn, turn_ref, query, key, value, after, *refs):
    inputs, sems = refs[-2:]

    @pl.when(turn_ref[0] == turn)
    def _():
        pairs = []
        column = 0
        for weight in (query, key, value):
            width = weight.shape[1]
            pairs.append((weight, inputs.at[:, column : column + width]))
            column += width
        for copy in copy_all(pairs, sems):
            copy.wait()

    for held in refs[:-2]:

        @pl.when(turn_ref[0] != turn)
        def _():
            copy = pltpu.make_async_copy(held, inputs, sems.at[0])
            copy.start()
            copy.wait()


def load_others_kernel(*refs):
    count = (len(refs) - 4) // 2 - 1
    sources, output_down, down, _ = refs[:count], *refs[count : count + 3]
    targets = refs[count + 3 : 2 * count + 3]
    output_down_across, down_across, held, sems = refs[2 * count + 3 :]
    copies = copy_all([(output_down, held), *zip(sources, targets)], sems)
    for kind in range(down.shape[0]):
        down_across[kind] = down[kind].T
    copies[0].wait()
    output_down_across[...] = held[...].T
    for copy in copies[1:]:
        copy.wait()


def own_slots(slot, total, rank):
    lane = lax.broadcasted_iota(jnp.int32, (1, 2 * rank), 1)
    second = (lane >= rank).astype(f32)
    return [slot == 2.0 * j + second for j in range(total // 2)]


def spread_over_slots(factor, own):
    twice = jnp.concatenate([factor, factor], axis=1)
    return jnp.concatenate([jnp.where(mask, twice, 0.0).astype(bf16) for mask in own], axis=1)


def pick_slot(product, own):
    wide = own[0].shape[1]
    picked = jnp.where(own[0], product[:, :wide], 0.0)
    for j in range(1, len(own)):
        picked = picked + jnp.where(own[j], product[:, j * wide : (j + 1) * wide], 0.0)
    return picked[:, : wide // 2] + picked[:, wide // 2 :]


def partial_low(state, gain, own, down_ref, form):
    scaled = (state * gain).astype(bf16)
    picked = []
    for kind in range(down_ref.shape[0]):
        product = lax.dot_general(scaled, down_ref[kind], form, preferred_element_type=f32)
        picked.append(pick_slot(product, own).astype(bf16))
    return jnp.concatenate(picked, axis=1)


def enter_kernel(total, rank, order, *refs):
    groups = len(order)
    blocks = in_order(refs[:groups], order)
    gain_ref, down_ref, send_ref, facts_ref = refs[groups:]
    width = down_ref.shape[2]
    everything = jnp.concatenate([block[...] for block in blocks], axis=0)
    facts = everything[:, width:].astype(f32)
    own = own_slots(facts[:, 1:2], total, rank)
    facts_ref[...] = facts
    send_ref[:, :width] = everything[:, :width]
    send_ref[:, width:] = partial_low(
        everything[:, :width].astype(f32), gain_ref[...], own, down_ref, NT
    )


def new_state(own, received, state, up_ref):
    width = state.shape[1]
    low_out = received[0][:, width:].astype(f32)
    projected = received[0][:, :width].astype(f32)
    for part in received[1:]:
        low_out = low_out + part[:, width:].astype(f32)
        projected = projected + part[:, :width].astype(f32)
    spread = spread_over_slots(low_out, own)
    delta = jnp.dot(spread, up_ref[...], preferred_element_type=f32).astype(bf16)
    return (state.astype(f32) + projected + delta.astype(f32)).astype(bf16)


def between_kernel(total, rank, parts, *refs):
    received = refs[:parts]
    state_ref, facts_ref, up_ref, gain_ref, down_ref, send_ref = refs[parts:]
    width = down_ref.shape[1]
    own = own_slots(facts_ref[:, 1:2], total, rank)
    state = new_state(own, received, state_ref[:, :width], up_ref)
    send_ref[:, :width] = state
    send_ref[:, width:] = partial_low(state.astype(f32), gain_ref[...], own, down_ref, NN)


def leave_kernel(total, rank, parts, *refs):
    received = refs[:parts]
    state_ref, facts_ref, up_ref = refs[parts : parts + 3]
    outgoing = refs[parts + 3 :]
    width = up_ref.shape[1]
    capacity = outgoing[0].shape[0]
    own = own_slots(facts_ref[:, 1:2], total, rank)
    state = new_state(own, received, state_ref[:, :width], up_ref)
    for s in range(len(outgoing)):
        outgoing[s][...] = state[s * capacity : (s + 1) * capacity]


def restore_kernel(order, place_ref, *refs):
    blocks, out_ref = in_order(refs[:-1], order), refs[-1]
    back = jnp.concatenate([block[...] for block in blocks], axis=0)
    out_ref[...] = jnp.dot(place_ref[...], back, preferred_element_type=f32).astype(bf16)


def norm_and_rotate(vector, gain, cosine, sine):
    head_dim = vector.shape[1]
    mean = jnp.mean(vector * vector, axis=1, keepdims=True)
    scaled = vector * lax.rsqrt(mean + epsilon) * gain
    return (scaled * cosine + pltpu.roll(scaled, head_dim // 2, 1) * sine).astype(bf16)


def project_slices(slices, masks, here, gain_ref, weight_ref):
    width = gain_ref.shape[2]
    products, squares, low = None, None, None
    for piece, mask in zip(slices, masks):
        source = jnp.bitwise_xor(here, mask)
        state = piece[:, :width].astype(f32)
        scaled = (state * gain_ref[source]).astype(bf16)
        features_there = pl.ds(pl.multiple_of(source * width, 64), width)
        product = jnp.dot(scaled, weight_ref[features_there, :], preferred_element_type=f32)
        square = jnp.sum(state * state, axis=1, keepdims=True)
        part = piece[:, width:].astype(f32)
        products = product if products is None else products + product
        squares = square if squares is None else squares + square
        low = part if low is None else low + part
    return products, squares, low


def early_kernel(masks, *refs):
    slices = refs[: len(masks)]
    index_ref, gain_ref, weight_ref, products_ref, squares_ref, low_ref = refs[len(masks) :]
    products, squares, low = project_slices(slices, masks, index_ref[0], gain_ref, weight_ref)
    products_ref[...] = products
    squares_ref[...] = jnp.broadcast_to(squares, squares_ref.shape)
    low_ref[...] = low


def step_kernel(total, rank, step, parts, masks, order, *refs):
    groups = len(order)
    refs = list(refs)

    def take(count):
        taken = refs[:count]
        del refs[:count]
        return taken

    slices = take(len(masks))
    (
        index_ref,
        products_ref,
        squares_ref,
        low_ref,
        facts_ref,
        gain_ref,
        weight_ref,
        query_up,
        key_up,
        value_up,
        query_gain,
        key_gain,
        cosine_ref,
        sine_ref,
        bias_ref,
    ) = take(15)
    cache = in_order(take(groups), order)
    earlier = take(2 * step)
    output_weight, output_down = take(2)
    outgoing = take(parts)
    key_fresh, value_fresh, attended, terms = refs
    features = weight_ref.shape[0]
    width = features // parts
    rows = products_ref.shape[0]
    head_dim = cache[0].shape[2]
    kv_local = cache[0].shape[0] // 2
    capacity = rows // groups
    query_width = query_up.shape[1]
    key_width = key_up.shape[1]
    heads = query_width // head_dim
    per_kv = heads // kv_local
    here = index_ref[0]

    own = own_slots(facts_ref[:, 1:2], total, rank)
    products, squares, low = project_slices(slices, masks, here, gain_ref, weight_ref)
    inverse = lax.rsqrt((squares_ref[:, :1] + squares) / features + epsilon)
    low = (low_ref[...] + low) * inverse

    def project(columns, up_ref, index):
        spread = spread_over_slots(low[:, index * rank : (index + 1) * rank], own)
        delta = jnp.dot(spread, up_ref[...], preferred_element_type=f32).astype(bf16)
        whole = (products_ref[:, columns] + products[:, columns]) * inverse
        return whole + delta.astype(f32)

    cosine = cosine_ref[step]
    sine = sine_ref[step]
    key = project(slice(query_width, query_width + key_width), key_up, 1)
    value = project(slice(query_width + key_width, None), value_up, 2).astype(bf16)
    for g in range(kv_local):
        columns = slice(g * head_dim, (g + 1) * head_dim)
        key_fresh[g] = norm_and_rotate(key[:, columns], key_gain[...], cosine, sine)
        value_fresh[g] = value[:, columns]
    query = project(slice(0, query_width), query_up, 0)
    query_heads = [
        norm_and_rotate(query[:, h * head_dim : (h + 1) * head_dim], query_gain[...], cosine, sine)
        for h in range(heads)
    ]

    scale = head_dim ** (-0.5)
    fresh_count = (step + 1) * capacity
    lanes = 128 * (-(-fresh_count // 128))
    filler = jnp.zeros((lanes - fresh_count, head_dim), bf16)
    key_place = lax.broadcasted_iota(jnp.int32, (per_kv * capacity, lanes), 1)
    own_row = lax.broadcasted_iota(jnp.int32, (per_kv * capacity, lanes), 0) % capacity
    same_row = (key_place % capacity == own_row) & (key_place < fresh_count)
    def fresh_rows(now, which, g, block):
        return jnp.concatenate(
            [earlier[2 * t + which][g, block, :] for t in range(step)] + [now[g, block, :], filler],
            axis=0,
        )

    together = 4
    for first in range(0, groups, together):
        blocks = [
            (b, slice(b * capacity, (b + 1) * capacity), g)
            for g in range(kv_local)
            for b in range(first, min(first + together, groups))
        ]
        scores = []
        for b, block, g in blocks:
            queries = jnp.concatenate(
                [query_heads[g * per_kv + h][block] for h in range(per_kv)], axis=0
            )
            bias = jnp.concatenate([bias_ref[block, :]] * per_kv, axis=0)
            cached = lax.dot_general(queries, cache[b][g], NT, preferred_element_type=f32)
            fresh = lax.dot_general(
                queries, fresh_rows(key_fresh, 0, g, block), NT, preferred_element_type=f32
            )
            fresh = jnp.where(same_row, fresh * scale, blocked)
            scores.append(jnp.concatenate([cached * scale + bias, fresh], axis=1))
        largest = [jnp.max(score, axis=1, keepdims=True) for score in scores]
        weights = [
            jnp.exp(score - top).astype(bf16) for score, top in zip(scores, largest)
        ]
        mixes = []
        for (b, block, g), weight in zip(blocks, weights):
            values = jnp.concatenate(
                [cache[b][kv_local + g], fresh_rows(value_fresh, 1, g, block)], axis=0
            )
            summing = jnp.concatenate([values, jnp.ones_like(values)], axis=1)
            mixes.append(jnp.dot(weight, summing, preferred_element_type=f32))
        for (b, block, g), mixed in zip(blocks, mixes):
            mixed = (mixed[:, :head_dim] / mixed[:, head_dim:]).astype(bf16)
            for h in range(per_kv):
                head = g * per_kv + h
                attended[block, head * head_dim : (head + 1) * head_dim] = mixed[
                    h * capacity : (h + 1) * capacity
                ]

    attended_rows = attended[...]
    product = jnp.dot(attended_rows, output_down[...], preferred_element_type=f32)
    low_out = pick_slot(product, own).astype(bf16)
    for n in range(parts):
        term = jnp.dot(
            attended_rows,
            output_weight[:, n * width : (n + 1) * width],
            preferred_element_type=f32,
        )
        terms[jnp.bitwise_xor(here, n)] = term.astype(bf16)
    for mask in range(parts):
        outgoing[mask][:, :width] = terms[mask]
        outgoing[mask][:, width:] = low_out


def swap(block, axis, mask):
    return lax.ppermute(block, axis, [(i, i ^ mask) for i in range(lax.axis_size(axis))])


def swap_all(blocks, axis, order):
    return [blocks[0]] + [swap(blocks[mask], axis, mask) for mask in order[1:]]


def shards(
    hidden,
    input_norm_gain,
    query_projection_weight,
    key_projection_weight,
    value_projection_weight,
    query_norm_gain,
    key_norm_gain,
    output_projection_weight,
    stacked_down_factors,
    query_up_factor,
    key_up_factor,
    value_up_factor,
    output_down_factor,
    output_up_factor,
    cached_key_rows,
    cached_value_rows,
    cached_length_rows,
    domain_of_row,
    slot_of_domain,
):
    groups = lax.axis_size("wide")
    parts = lax.axis_size("narrow")
    wide_index = lax.axis_index("wide")
    narrow_index = lax.axis_index("narrow")
    row_group, width = hidden.shape
    capacity = row_group // 4
    rows = groups * capacity
    total = stacked_down_factors.shape[0]
    low_width = stacked_down_factors.shape[1]
    rank = output_up_factor.shape[1]
    _, kv_local, context, head_dim = cached_key_rows.shape
    features = input_norm_gain.shape[0]
    query_width = query_projection_weight.shape[1]

    load_cost = pl.CostEstimate(flops=0, bytes_accessed=20000000, transcendentals=0)
    smem = pl.BlockSpec(memory_space=pltpu.SMEM)
    vmem = pl.BlockSpec(memory_space=pltpu.VMEM)
    hbm = pl.BlockSpec(memory_space=pltpu.HBM)
    outgoing_shape = jax.ShapeDtypeStruct((capacity, width + 128), bf16)
    target, place, *outgoing = pl.pallas_call(
        route_kernel,
        out_shape=[
            jax.ShapeDtypeStruct((row_group,), jnp.int32),
            jax.ShapeDtypeStruct((row_group, rows), bf16),
        ]
        + [outgoing_shape] * groups,
        in_specs=[smem] + [hbm] * 4,
        out_specs=[smem] + [vmem] * (groups + 1),
        scratch_shapes=[
            pltpu.SMEM((groups,), jnp.int32),
            pltpu.VMEM((row_group, rows), f32),
            pltpu.VMEM((row_group, 128), f32),
            pltpu.SMEM(domain_of_row.shape, jnp.int32),
            pltpu.SMEM(slot_of_domain.shape, jnp.int32),
            pltpu.SMEM(cached_length_rows.shape, jnp.int32),
            pltpu.VMEM(hidden.shape, bf16),
            pltpu.SemaphoreType.DMA((4,)),
        ],
        compiler_params=kernel_params(8),
        name="route_rows",
    )(
        wide_index.reshape(1),
        in_hbm(domain_of_row),
        in_hbm(slot_of_domain),
        in_hbm(cached_length_rows),
        in_hbm(hidden),
    )
    by_group = [0] + list(range(groups - 1, 0, -1))
    arrived = swap_all(outgoing, "wide", by_group)
    packed_shape = (2 * kv_local, capacity, context, head_dim)
    kinds = low_width // rank
    *packed, down = pl.pallas_call(
        pack_kernel,
        out_shape=[jax.ShapeDtypeStruct(packed_shape, bf16)] * groups
        + [jax.ShapeDtypeStruct((kinds, total * rank, width), bf16)],
        in_specs=[smem, hbm, hbm, hbm],
        out_specs=[vmem] * (groups + 1),
        scratch_shapes=[
            pltpu.VMEM((groups,) + packed_shape, bf16),
            pltpu.VMEM(cached_key_rows.shape, bf16),
            pltpu.VMEM(cached_value_rows.shape, bf16),
            pltpu.SemaphoreType.DMA((2 + kinds * total,)),
        ],
        compiler_params=kernel_params(16),
        name="pack_cache",
    )(target, in_hbm(cached_key_rows), in_hbm(cached_value_rows), in_hbm(stacked_down_factors))
    cache = swap_all(packed, "wide", by_group)
    cache = [block.reshape(2 * kv_local, capacity * context, head_dim) for block in cache]

    gain_rows = input_norm_gain.reshape(parts, 1, width)
    gain_slice = lax.dynamic_index_in_dim(gain_rows, narrow_index, 0, keepdims=False)
    sent_state = jax.ShapeDtypeStruct((rows, width + low_width), bf16)
    key_width = key_projection_weight.shape[1]
    input_width = query_width + 2 * key_width

    def load_inputs(turn, after, *held):
        return pl.pallas_call(
            functools.partial(load_inputs_kernel, turn),
            out_shape=jax.ShapeDtypeStruct((features, input_width), bf16),
            in_specs=[smem] + [hbm] * 3 + [vmem] * (1 + len(held)),
            out_specs=vmem,
            scratch_shapes=[pltpu.SemaphoreType.DMA((3,))],
            compiler_params=kernel_params(18),
            cost_estimate=load_cost,
            name="load_inputs",
        )(
            lax.rem(wide_index, 2).reshape(1),
            in_hbm(query_projection_weight),
            in_hbm(key_projection_weight),
            in_hbm(value_projection_weight),
            after,
            *held,
        )

    input_weight = load_inputs(1, arrived[-1])
    input_weight, *arrived = lax.optimization_barrier((input_weight, *arrived))
    send, facts_here = pl.pallas_call(
        functools.partial(enter_kernel, total, rank, by_group),
        out_shape=[sent_state, jax.ShapeDtypeStruct((rows, 128), f32)],
        in_specs=[vmem] * (groups + 2),
        out_specs=[vmem] * 2,
        compiler_params=kernel_params(8),
        name="enter",
    )(*arrived, gain_slice, down)

    def load_others(after):
        others = [
            query_up_factor.reshape(total * rank, query_width),
            key_up_factor.reshape(total * rank, key_width),
            value_up_factor.reshape(total * rank, key_width),
            output_projection_weight,
            output_up_factor.reshape(total * rank, width),
        ]
        turned = [
            jax.ShapeDtypeStruct((query_width, total * rank), bf16),
            jax.ShapeDtypeStruct((kinds, width, total * rank), bf16),
        ]
        return pl.pallas_call(
            load_others_kernel,
            out_shape=[jax.ShapeDtypeStruct(array.shape, bf16) for array in others] + turned,
            in_specs=[hbm] * (len(others) + 1) + [vmem] * 2,
            out_specs=[vmem] * (len(others) + 2),
            scratch_shapes=[
                pltpu.VMEM((total * rank, query_width), bf16),
                pltpu.SemaphoreType.DMA((len(others) + 1,)),
            ],
            compiler_params=kernel_params(20),
            cost_estimate=load_cost,
            name="load_others",
        )(
            *[in_hbm(array) for array in others],
            in_hbm(output_down_factor.reshape(total * rank, query_width)),
            down,
            after,
        )

    lengths = facts_here[:, 0]
    frequency = rope_base ** (-(jnp.arange(head_dim // 2, dtype=f32) * 2.0) / head_dim)
    positions = lengths[None, :] + jnp.arange(STEPS, dtype=f32)[:, None]
    angles = positions[:, :, None] * frequency
    cosine = jnp.cos(angles)
    sine = jnp.sin(angles)
    cosine = jnp.concatenate([cosine, cosine], axis=-1)
    sine = jnp.concatenate([-sine, sine], axis=-1)
    key_index = jnp.arange(capacity * context)[None, :]
    visible = (key_index // context == (jnp.arange(rows) % capacity)[:, None]) & (
        (key_index % context).astype(f32) < lengths[:, None]
    )
    bias = jnp.where(visible, 0.0, blocked).astype(f32)

    query_gain = query_norm_gain.reshape(1, head_dim)
    key_gain = key_norm_gain.reshape(1, head_dim)
    index_here = narrow_index.reshape(1)
    sent_terms = jax.ShapeDtypeStruct((rows, width + rank), bf16)
    fresh = jax.ShapeDtypeStruct((kv_local, rows, head_dim), bf16)
    far = [mask for mask in range(2, parts) if mask % 2 == 0]
    early = [0, 1] + far
    late = [mask ^ 1 for mask in far]

    earlier = []
    for step in range(STEPS):
        from_far = [swap(send, "narrow", mask) for mask in far]
        from_near = swap(send, "narrow", 1)
        if step == 0:
            input_weight = load_inputs(0, facts_here, input_weight)
            input_weight, *from_far = lax.optimization_barrier((input_weight, *from_far))
        passed_on = [swap(piece, "narrow", 1) for piece in from_far]
        if step == 0:
            *others, output_down, down_across = load_others(from_far[0])
            query_up, key_up, value_up, output_weight, output_up = others
        sums = pl.pallas_call(
            functools.partial(early_kernel, early),
            out_shape=[
                jax.ShapeDtypeStruct((rows, input_width), f32),
                jax.ShapeDtypeStruct((rows, 128), f32),
                jax.ShapeDtypeStruct((rows, low_width), f32),
            ],
            in_specs=[vmem] * len(early) + [smem] + [vmem] * 2,
            out_specs=[vmem] * 3,
            compiler_params=kernel_params(16),
            cost_estimate=pl.CostEstimate(
                flops=2 * rows * features * input_width,
                bytes_accessed=10000000,
                transcendentals=0,
            ),
            name="project_early",
        )(send, from_near, *from_far, index_here, gain_rows, input_weight)
        *terms, key_fresh, value_fresh = pl.pallas_call(
            functools.partial(step_kernel, total, rank, step, parts, late, by_group),
            out_shape=[sent_terms] * parts + [fresh] * 2,
            in_specs=[vmem] * len(late) + [smem] + [vmem] * (16 + groups + 2 * step),
            out_specs=[vmem] * (parts + 2),
            scratch_shapes=[
                pltpu.VMEM((rows, query_width), bf16),
                pltpu.VMEM((parts, rows, width), bf16),
            ],
            compiler_params=kernel_params(24),
            name="attend_step",
        )(
            *passed_on,
            index_here,
            *sums,
            facts_here,
            gain_rows,
            input_weight,
            query_up,
            key_up,
            value_up,
            query_gain,
            key_gain,
            cosine,
            sine,
            bias,
            *cache,
            *earlier,
            output_weight,
            output_down,
        )
        earlier += [key_fresh, value_fresh]
        received = swap_all(
            terms, "narrow", [0] + far + [mask + 1 for mask in far] + [1]
        )
        if step < STEPS - 1:
            send = pl.pallas_call(
                functools.partial(between_kernel, total, rank, parts),
                out_shape=sent_state,
                in_specs=[vmem] * (parts + 5),
                out_specs=vmem,
                compiler_params=kernel_params(8),
                name="between",
            )(*received, send, facts_here, output_up, gain_slice, down_across)
        else:
            leaving = pl.pallas_call(
                functools.partial(leave_kernel, total, rank, parts),
                out_shape=[jax.ShapeDtypeStruct((capacity, width), bf16)] * groups,
                in_specs=[vmem] * (parts + 3),
                out_specs=[vmem] * groups,
                compiler_params=kernel_params(8),
                name="leave",
            )(*received, send, facts_here, output_up)

    back = swap_all(leaving, "wide", by_group)
    return pl.pallas_call(
        functools.partial(restore_kernel, by_group),
        out_shape=jax.ShapeDtypeStruct((row_group, width), bf16),
        in_specs=[vmem] * (groups + 1),
        out_specs=vmem,
        compiler_params=kernel_params(8),
        name="restore",
    )(place, *back)


def solution(mesh):
    placed = (
        P(("parts", "wide"), "narrow"),
        P(),
        P(None, "narrow"),
        P(None, "narrow"),
        P(None, "narrow"),
        P(),
        P(),
        P("narrow", None),
        P(("parts", "wide"), None, "narrow"),
        P(("parts", "wide"), None, "narrow"),
        P(("parts", "wide"), None, "narrow"),
        P(("parts", "wide"), None, "narrow"),
        P(("parts", "wide"), None, "narrow"),
        P(("parts", "wide"), None, "narrow"),
        P(("parts", "wide"), "narrow", None, None),
        P(("parts", "wide"), "narrow", None, None),
        P(("parts", "wide")),
        P("parts"),
        P("parts"),
    )
    return jax.shard_map(
        shards,
        mesh=mesh,
        in_specs=placed,
        out_specs=P(("parts", "wide"), "narrow"),
        check_vma=False,
    )
```

```python
import functools

import jax
import jax.numpy as jnp
from jax import lax
from jax.experimental import pallas as pl
from jax.experimental.pallas import tpu as pltpu
from jax.sharding import PartitionSpec as P

STEPS = 4

epsilon = 1e-06
rope_base = 1000000.0
blocked = -1e30
f32 = jnp.float32
bf16 = jnp.bfloat16

NT = (((1,), (1,)), ((), ()))
NN = (((1,), (0,)), ((), ()))


def kernel_params(mib):
    return pltpu.CompilerParams(vmem_limit_bytes=mib * 1024 * 1024)


def in_hbm(array):
    return pltpu.with_memory_space_constraint(array, pltpu.HBM)


def in_order(refs, order):
    return [refs[order.index(block)] for block in range(len(order))]


def copy_all(pairs, sems, first=0):
    copies = [
        pltpu.make_async_copy(source, target, sems.at[index])
        for index, (source, target) in enumerate(pairs, first)
    ]
    for copy in copies:
        copy.start()
    return copies


def route_kernel(
    group_ref, domain_hbm, slot_hbm, length_hbm, hidden_hbm, target_ref, place_ref, *refs
):
    groups = len(refs) - 8
    outgoing = refs[:groups]
    count, place, facts, domain_ref, slot_ref, length_ref, hidden_ref, sems = refs[groups:]
    rows, width = hidden_ref.shape
    capacity = outgoing[0].shape[0]
    per_group = slot_ref.shape[0] // groups
    here = group_ref[0]
    *tables, hidden_copy = copy_all(
        [
            (domain_hbm, domain_ref),
            (slot_hbm, slot_ref),
            (length_hbm, length_ref),
            (hidden_hbm, hidden_ref),
        ],
        sems,
    )
    for group in range(groups):
        count[group] = 0
    places = lax.broadcasted_iota(jnp.int32, (1, groups * capacity), 1)
    columns = lax.broadcasted_iota(jnp.int32, (1, facts.shape[1]), 1)
    for copy in tables:
        copy.wait()

    def put(row, carry):
        slot = slot_ref[domain_ref[here * rows + row]]
        dest = lax.div(slot, per_group)
        position = jnp.minimum(count[dest], capacity - 1)
        count[dest] = position + 1
        target = jnp.bitwise_xor(dest, here) * capacity + position
        target_ref[row] = target
        place[pl.ds(row, 1), :] = jnp.where(places == target, 1.0, 0.0)
        length = length_ref[row].astype(f32)
        local = (slot - dest * per_group).astype(f32)
        facts[pl.ds(row, 1), :] = jnp.where(
            columns == 0, length, jnp.where(columns == 1, local, 0.0)
        )
        return carry

    lax.fori_loop(0, rows, put, 0, unroll=8)
    chosen = place[...].astype(bf16)
    place_ref[...] = chosen
    across = (((0,), (0,)), ((), ()))
    known = lax.dot_general(
        chosen, facts[...].astype(bf16), across, preferred_element_type=f32
    ).astype(bf16)
    hidden_copy.wait()
    state = lax.dot_general(
        chosen, hidden_ref[...], across, preferred_element_type=f32
    ).astype(bf16)
    for s in range(groups):
        block = slice(s * capacity, (s + 1) * capacity)
        outgoing[s][:, :width] = state[block]
        outgoing[s][:, width:] = known[block]


def pack_kernel(target_ref, key_hbm, value_hbm, down_hbm, *refs):
    groups = len(refs) - 5
    outgoing = refs[:groups]
    down_ref, packed, key_ref, value_ref, sems = refs[groups:]
    rows, kv_local = key_ref.shape[:2]
    capacity = packed.shape[2]
    kinds = down_ref.shape[0]
    total = down_hbm.shape[0]
    rank = down_hbm.shape[1] // kinds
    copies = copy_all([(key_hbm, key_ref), (value_hbm, value_ref)], sems)
    if groups * capacity > rows:
        packed[...] = jnp.zeros_like(packed)
    for copy in copies:
        copy.wait()
    pairs = []
    for kind in range(kinds):
        for d in range(total):
            pairs.append(
                (
                    down_hbm.at[d, kind * rank : (kind + 1) * rank, :],
                    down_ref.at[kind, d * rank : (d + 1) * rank, :],
                )
            )
    down_copies = copy_all(pairs, sems, len(copies))

    def put(row, carry):
        target = target_ref[row]
        block = lax.div(target, capacity)
        position = target - block * capacity
        for g in range(kv_local):
            packed[block, g, position] = key_ref[row, g]
            packed[block, kv_local + g, position] = value_ref[row, g]
        return carry

    lax.fori_loop(0, rows, put, 0, unroll=4)
    for s in range(groups):
        outgoing[s][...] = packed[s]
    for copy in down_copies:
        copy.wait()


def load_inputs_kernel(turn, turn_ref, query, key, value, after, *refs):
    inputs, sems = refs[-2:]

    @pl.when(turn_ref[0] == turn)
    def _():
        pairs = []
        column = 0
        for weight in (query, key, value):
            width = weight.shape[1]
            pairs.append((weight, inputs.at[:, column : column + width]))
            column += width
        for copy in copy_all(pairs, sems):
            copy.wait()

    for held in refs[:-2]:

        @pl.when(turn_ref[0] != turn)
        def _():
            copy = pltpu.make_async_copy(held, inputs, sems.at[0])
            copy.start()
            copy.wait()


def load_others_kernel(*refs):
    count = (len(refs) - 4) // 2 - 1
    sources, output_down, down, _ = refs[:count], *refs[count : count + 3]
    targets = refs[count + 3 : 2 * count + 3]
    output_down_across, down_across, held, sems = refs[2 * count + 3 :]
    copies = copy_all([(output_down, held), *zip(sources, targets)], sems)
    for kind in range(down.shape[0]):
        down_across[kind] = down[kind].T
    copies[0].wait()
    output_down_across[...] = held[...].T
    for copy in copies[1:]:
        copy.wait()


def own_slots(slot, total, rank):
    lane = lax.broadcasted_iota(jnp.int32, (1, 2 * rank), 1)
    second = (lane >= rank).astype(f32)
    return [slot == 2.0 * j + second for j in range(total // 2)]


def spread_over_slots(factor, own):
    twice = jnp.concatenate([factor, factor], axis=1)
    return jnp.concatenate([jnp.where(mask, twice, 0.0).astype(bf16) for mask in own], axis=1)


def pick_slot(product, own):
    wide = own[0].shape[1]
    picked = jnp.where(own[0], product[:, :wide], 0.0)
    for j in range(1, len(own)):
        picked = picked + jnp.where(own[j], product[:, j * wide : (j + 1) * wide], 0.0)
    return picked[:, : wide // 2] + picked[:, wide // 2 :]


def partial_low(state, gain, own, down_ref, form):
    scaled = (state * gain).astype(bf16)
    picked = []
    for kind in range(down_ref.shape[0]):
        product = lax.dot_general(scaled, down_ref[kind], form, preferred_element_type=f32)
        picked.append(pick_slot(product, own).astype(bf16))
    return jnp.concatenate(picked, axis=1)


def enter_kernel(total, rank, order, *refs):
    groups = len(order)
    blocks = in_order(refs[:groups], order)
    gain_ref, down_ref, send_ref, facts_ref = refs[groups:]
    width = down_ref.shape[2]
    everything = jnp.concatenate([block[...] for block in blocks], axis=0)
    facts = everything[:, width:].astype(f32)
    own = own_slots(facts[:, 1:2], total, rank)
    facts_ref[...] = facts
    send_ref[:, :width] = everything[:, :width]
    send_ref[:, width:] = partial_low(
        everything[:, :width].astype(f32), gain_ref[...], own, down_ref, NT
    )


def new_state(own, received, state, up_ref):
    width = state.shape[1]
    low_out = received[0][:, width:].astype(f32)
    projected = received[0][:, :width].astype(f32)
    for part in received[1:]:
        low_out = low_out + part[:, width:].astype(f32)
        projected = projected + part[:, :width].astype(f32)
    spread = spread_over_slots(low_out, own)
    delta = jnp.dot(spread, up_ref[...], preferred_element_type=f32).astype(bf16)
    return (state.astype(f32) + projected + delta.astype(f32)).astype(bf16)


def between_kernel(total, rank, parts, *refs):
    received = refs[:parts]
    state_ref, facts_ref, up_ref, gain_ref, down_ref, send_ref = refs[parts:]
    width = down_ref.shape[1]
    own = own_slots(facts_ref[:, 1:2], total, rank)
    state = new_state(own, received, state_ref[:, :width], up_ref)
    send_ref[:, :width] = state
    send_ref[:, width:] = partial_low(state.astype(f32), gain_ref[...], own, down_ref, NN)


def leave_kernel(total, rank, parts, *refs):
    received = refs[:parts]
    state_ref, facts_ref, up_ref = refs[parts : parts + 3]
    outgoing = refs[parts + 3 :]
    width = up_ref.shape[1]
    capacity = outgoing[0].shape[0]
    own = own_slots(facts_ref[:, 1:2], total, rank)
    state = new_state(own, received, state_ref[:, :width], up_ref)
    for s in range(len(outgoing)):
        outgoing[s][...] = state[s * capacity : (s + 1) * capacity]


def restore_kernel(order, place_ref, *refs):
    blocks, out_ref = in_order(refs[:-1], order), refs[-1]
    back = jnp.concatenate([block[...] for block in blocks], axis=0)
    out_ref[...] = jnp.dot(place_ref[...], back, preferred_element_type=f32).astype(bf16)


def norm_and_rotate(vector, gain, cosine, sine):
    head_dim = vector.shape[1]
    mean = jnp.mean(vector * vector, axis=1, keepdims=True)
    scaled = vector * lax.rsqrt(mean + epsilon) * gain
    return (scaled * cosine + pltpu.roll(scaled, head_dim // 2, 1) * sine).astype(bf16)


def project_slices(slices, masks, here, gain_ref, weight_ref):
    width = gain_ref.shape[2]
    products, squares, low = None, None, None
    for piece, mask in zip(slices, masks):
        source = jnp.bitwise_xor(here, mask)
        state = piece[:, :width].astype(f32)
        scaled = (state * gain_ref[source]).astype(bf16)
        features_there = pl.ds(pl.multiple_of(source * width, 64), width)
        product = jnp.dot(scaled, weight_ref[features_there, :], preferred_element_type=f32)
        square = jnp.sum(state * state, axis=1, keepdims=True)
        part = piece[:, width:].astype(f32)
        products = product if products is None else products + product
        squares = square if squares is None else squares + square
        low = part if low is None else low + part
    return products, squares, low


def early_kernel(masks, *refs):
    slices = refs[: len(masks)]
    index_ref, gain_ref, weight_ref, products_ref, squares_ref, low_ref = refs[len(masks) :]
    products, squares, low = project_slices(slices, masks, index_ref[0], gain_ref, weight_ref)
    products_ref[...] = products
    squares_ref[...] = jnp.broadcast_to(squares, squares_ref.shape)
    low_ref[...] = low


def step_kernel(total, rank, step, parts, masks, order, *refs):
    groups = len(order)
    refs = list(refs)

    def take(count):
        taken = refs[:count]
        del refs[:count]
        return taken

    slices = take(len(masks))
    (
        index_ref,
        products_ref,
        squares_ref,
        low_ref,
        facts_ref,
        gain_ref,
        weight_ref,
        query_up,
        key_up,
        value_up,
        query_gain,
        key_gain,
        cosine_ref,
        sine_ref,
        bias_ref,
    ) = take(15)
    cache = in_order(take(groups), order)
    earlier = take(2 * step)
    output_weight, output_down = take(2)
    outgoing = take(parts)
    key_fresh, value_fresh, attended, terms = refs
    features = weight_ref.shape[0]
    width = features // parts
    rows = products_ref.shape[0]
    head_dim = cache[0].shape[2]
    kv_local = cache[0].shape[0] // 2
    capacity = rows // groups
    query_width = query_up.shape[1]
    key_width = key_up.shape[1]
    heads = query_width // head_dim
    per_kv = heads // kv_local
    here = index_ref[0]

    own = own_slots(facts_ref[:, 1:2], total, rank)
    products, squares, low = project_slices(slices, masks, here, gain_ref, weight_ref)
    inverse = lax.rsqrt((squares_ref[:, :1] + squares) / features + epsilon)
    low = (low_ref[...] + low) * inverse

    def project(columns, up_ref, index):
        spread = spread_over_slots(low[:, index * rank : (index + 1) * rank], own)
        delta = jnp.dot(spread, up_ref[...], preferred_element_type=f32).astype(bf16)
        whole = (products_ref[:, columns] + products[:, columns]) * inverse
        return whole + delta.astype(f32)

    cosine = cosine_ref[step]
    sine = sine_ref[step]
    key = project(slice(query_width, query_width + key_width), key_up, 1)
    value = project(slice(query_width + key_width, None), value_up, 2).astype(bf16)
    for g in range(kv_local):
        columns = slice(g * head_dim, (g + 1) * head_dim)
        key_fresh[g] = norm_and_rotate(key[:, columns], key_gain[...], cosine, sine)
        value_fresh[g] = value[:, columns]
    query = project(slice(0, query_width), query_up, 0)
    query_heads = [
        norm_and_rotate(query[:, h * head_dim : (h + 1) * head_dim], query_gain[...], cosine, sine)
        for h in range(heads)
    ]

    scale = head_dim ** (-0.5)
    fresh_count = (step + 1) * capacity
    lanes = 128 * (-(-fresh_count // 128))
    filler = jnp.zeros((lanes - fresh_count, head_dim), bf16)
    key_place = lax.broadcasted_iota(jnp.int32, (per_kv * capacity, lanes), 1)
    own_row = lax.broadcasted_iota(jnp.int32, (per_kv * capacity, lanes), 0) % capacity
    same_row = (key_place % capacity == own_row) & (key_place < fresh_count)
    def fresh_rows(now, which, g, block):
        return jnp.concatenate(
            [earlier[2 * t + which][g, block, :] for t in range(step)] + [now[g, block, :], filler],
            axis=0,
        )

    together = 4
    for first in range(0, groups, together):
        blocks = [
            (b, slice(b * capacity, (b + 1) * capacity), g)
            for g in range(kv_local)
            for b in range(first, min(first + together, groups))
        ]
        scores = []
        for b, block, g in blocks:
            queries = jnp.concatenate(
                [query_heads[g * per_kv + h][block] for h in range(per_kv)], axis=0
            )
            bias = jnp.concatenate([bias_ref[block, :]] * per_kv, axis=0)
            cached = lax.dot_general(queries, cache[b][g], NT, preferred_element_type=f32)
            fresh = lax.dot_general(
                queries, fresh_rows(key_fresh, 0, g, block), NT, preferred_element_type=f32
            )
            fresh = jnp.where(same_row, fresh * scale, blocked)
            scores.append(jnp.concatenate([cached * scale + bias, fresh], axis=1))
        largest = [jnp.max(score, axis=1, keepdims=True) for score in scores]
        weights = [
            jnp.exp(score - top).astype(bf16) for score, top in zip(scores, largest)
        ]
        mixes = []
        for (b, block, g), weight in zip(blocks, weights):
            values = jnp.concatenate(
                [cache[b][kv_local + g], fresh_rows(value_fresh, 1, g, block)], axis=0
            )
            summing = jnp.concatenate([values, jnp.ones_like(values)], axis=1)
            mixes.append(jnp.dot(weight, summing, preferred_element_type=f32))
        for (b, block, g), mixed in zip(blocks, mixes):
            mixed = (mixed[:, :head_dim] / mixed[:, head_dim:]).astype(bf16)
            for h in range(per_kv):
                head = g * per_kv + h
                attended[block, head * head_dim : (head + 1) * head_dim] = mixed[
                    h * capacity : (h + 1) * capacity
                ]

    attended_rows = attended[...]
    product = jnp.dot(attended_rows, output_down[...], preferred_element_type=f32)
    low_out = pick_slot(product, own).astype(bf16)
    for n in range(parts):
        term = jnp.dot(
            attended_rows,
            output_weight[:, n * width : (n + 1) * width],
            preferred_element_type=f32,
        )
        terms[jnp.bitwise_xor(here, n)] = term.astype(bf16)
    for mask in range(parts):
        outgoing[mask][:, :width] = terms[mask]
        outgoing[mask][:, width:] = low_out


def swap(block, axis, mask):
    return lax.ppermute(block, axis, [(i, i ^ mask) for i in range(lax.axis_size(axis))])


def swap_all(blocks, axis, order):
    return [blocks[0]] + [swap(blocks[mask], axis, mask) for mask in order[1:]]


def shards(
    hidden,
    input_norm_gain,
    query_projection_weight,
    key_projection_weight,
    value_projection_weight,
    query_norm_gain,
    key_norm_gain,
    output_projection_weight,
    stacked_down_factors,
    query_up_factor,
    key_up_factor,
    value_up_factor,
    output_down_factor,
    output_up_factor,
    cached_key_rows,
    cached_value_rows,
    cached_length_rows,
    domain_of_row,
    slot_of_domain,
):
    groups = lax.axis_size("wide")
    parts = lax.axis_size("narrow")
    wide_index = lax.axis_index("wide")
    narrow_index = lax.axis_index("narrow")
    row_group, width = hidden.shape
    capacity = row_group // 4
    rows = groups * capacity
    total = stacked_down_factors.shape[0]
    low_width = stacked_down_factors.shape[1]
    rank = output_up_factor.shape[1]
    _, kv_local, context, head_dim = cached_key_rows.shape
    features = input_norm_gain.shape[0]
    query_width = query_projection_weight.shape[1]

    load_cost = pl.CostEstimate(flops=0, bytes_accessed=20000000, transcendentals=0)
    smem = pl.BlockSpec(memory_space=pltpu.SMEM)
    vmem = pl.BlockSpec(memory_space=pltpu.VMEM)
    hbm = pl.BlockSpec(memory_space=pltpu.HBM)
    outgoing_shape = jax.ShapeDtypeStruct((capacity, width + 128), bf16)
    target, place, *outgoing = pl.pallas_call(
        route_kernel,
        out_shape=[
            jax.ShapeDtypeStruct((row_group,), jnp.int32),
            jax.ShapeDtypeStruct((row_group, rows), bf16),
        ]
        + [outgoing_shape] * groups,
        in_specs=[smem] + [hbm] * 4,
        out_specs=[smem] + [vmem] * (groups + 1),
        scratch_shapes=[
            pltpu.SMEM((groups,), jnp.int32),
            pltpu.VMEM((row_group, rows), f32),
            pltpu.VMEM((row_group, 128), f32),
            pltpu.SMEM(domain_of_row.shape, jnp.int32),
            pltpu.SMEM(slot_of_domain.shape, jnp.int32),
            pltpu.SMEM(cached_length_rows.shape, jnp.int32),
            pltpu.VMEM(hidden.shape, bf16),
            pltpu.SemaphoreType.DMA((4,)),
        ],
        compiler_params=kernel_params(8),
        name="route_rows",
    )(
        wide_index.reshape(1),
        in_hbm(domain_of_row),
        in_hbm(slot_of_domain),
        in_hbm(cached_length_rows),
        in_hbm(hidden),
    )
    by_group = [0] + list(range(groups - 1, 0, -1))
    arrived = swap_all(outgoing, "wide", by_group)
    packed_shape = (2 * kv_local, capacity, context, head_dim)
    kinds = low_width // rank
    *packed, down = pl.pallas_call(
        pack_kernel,
        out_shape=[jax.ShapeDtypeStruct(packed_shape, bf16)] * groups
        + [jax.ShapeDtypeStruct((kinds, total * rank, width), bf16)],
        in_specs=[smem, hbm, hbm, hbm],
        out_specs=[vmem] * (groups + 1),
        scratch_shapes=[
            pltpu.VMEM((groups,) + packed_shape, bf16),
            pltpu.VMEM(cached_key_rows.shape, bf16),
            pltpu.VMEM(cached_value_rows.shape, bf16),
            pltpu.SemaphoreType.DMA((2 + kinds * total,)),
        ],
        compiler_params=kernel_params(16),
        name="pack_cache",
    )(target, in_hbm(cached_key_rows), in_hbm(cached_value_rows), in_hbm(stacked_down_factors))
    cache = swap_all(packed, "wide", by_group)
    cache = [block.reshape(2 * kv_local, capacity * context, head_dim) for block in cache]

    gain_rows = input_norm_gain.reshape(parts, 1, width)
    gain_slice = lax.dynamic_index_in_dim(gain_rows, narrow_index, 0, keepdims=False)
    sent_state = jax.ShapeDtypeStruct((rows, width + low_width), bf16)
    key_width = key_projection_weight.shape[1]
    input_width = query_width + 2 * key_width

    def load_inputs(turn, after, *held):
        return pl.pallas_call(
            functools.partial(load_inputs_kernel, turn),
            out_shape=jax.ShapeDtypeStruct((features, input_width), bf16),
            in_specs=[smem] + [hbm] * 3 + [vmem] * (1 + len(held)),
            out_specs=vmem,
            scratch_shapes=[pltpu.SemaphoreType.DMA((3,))],
            compiler_params=kernel_params(18),
            cost_estimate=load_cost,
            name="load_inputs",
        )(
            lax.rem(wide_index, 2).reshape(1),
            in_hbm(query_projection_weight),
            in_hbm(key_projection_weight),
            in_hbm(value_projection_weight),
            after,
            *held,
        )

    input_weight = load_inputs(1, arrived[-1])
    input_weight, *arrived = lax.optimization_barrier((input_weight, *arrived))
    send, facts_here = pl.pallas_call(
        functools.partial(enter_kernel, total, rank, by_group),
        out_shape=[sent_state, jax.ShapeDtypeStruct((rows, 128), f32)],
        in_specs=[vmem] * (groups + 2),
        out_specs=[vmem] * 2,
        compiler_params=kernel_params(8),
        name="enter",
    )(*arrived, gain_slice, down)

    def load_others(after):
        others = [
            query_up_factor.reshape(total * rank, query_width),
            key_up_factor.reshape(total * rank, key_width),
            value_up_factor.reshape(total * rank, key_width),
            output_projection_weight,
            output_up_factor.reshape(total * rank, width),
        ]
        turned = [
            jax.ShapeDtypeStruct((query_width, total * rank), bf16),
            jax.ShapeDtypeStruct((kinds, width, total * rank), bf16),
        ]
        return pl.pallas_call(
            load_others_kernel,
            out_shape=[jax.ShapeDtypeStruct(array.shape, bf16) for array in others] + turned,
            in_specs=[hbm] * (len(others) + 1) + [vmem] * 2,
            out_specs=[vmem] * (len(others) + 2),
            scratch_shapes=[
                pltpu.VMEM((total * rank, query_width), bf16),
                pltpu.SemaphoreType.DMA((len(others) + 1,)),
            ],
            compiler_params=kernel_params(20),
            cost_estimate=load_cost,
            name="load_others",
        )(
            *[in_hbm(array) for array in others],
            in_hbm(output_down_factor.reshape(total * rank, query_width)),
            down,
            after,
        )

    lengths = facts_here[:, 0]
    frequency = rope_base ** (-(jnp.arange(head_dim // 2, dtype=f32) * 2.0) / head_dim)
    positions = lengths[None, :] + jnp.arange(STEPS, dtype=f32)[:, None]
    angles = positions[:, :, None] * frequency
    cosine = jnp.cos(angles)
    sine = jnp.sin(angles)
    cosine = jnp.concatenate([cosine, cosine], axis=-1)
    sine = jnp.concatenate([-sine, sine], axis=-1)
    key_index = jnp.arange(capacity * context)[None, :]
    visible = (key_index // context == (jnp.arange(rows) % capacity)[:, None]) & (
        (key_index % context).astype(f32) < lengths[:, None]
    )
    bias = jnp.where(visible, 0.0, blocked).astype(f32)

    query_gain = query_norm_gain.reshape(1, head_dim)
    key_gain = key_norm_gain.reshape(1, head_dim)
    index_here = narrow_index.reshape(1)
    sent_terms = jax.ShapeDtypeStruct((rows, width + rank), bf16)
    fresh = jax.ShapeDtypeStruct((kv_local, rows, head_dim), bf16)
    far = [mask for mask in range(2, parts) if mask % 2 == 0]
    early = [0, 1] + far
    late = [mask ^ 1 for mask in far]

    earlier = []
    for step in range(STEPS):
        from_far = [swap(send, "narrow", mask) for mask in far]
        from_near = swap(send, "narrow", 1)
        if step == 0:
            input_weight = load_inputs(0, facts_here, input_weight)
            input_weight, *from_far = lax.optimization_barrier((input_weight, *from_far))
        passed_on = [swap(piece, "narrow", 1) for piece in from_far]
        if step == 0:
            *others, output_down, down_across = load_others(from_far[0])
            query_up, key_up, value_up, output_weight, output_up = others
        sums = pl.pallas_call(
            functools.partial(early_kernel, early),
            out_shape=[
                jax.ShapeDtypeStruct((rows, input_width), f32),
                jax.ShapeDtypeStruct((rows, 128), f32),
                jax.ShapeDtypeStruct((rows, low_width), f32),
            ],
            in_specs=[vmem] * len(early) + [smem] + [vmem] * 2,
            out_specs=[vmem] * 3,
            compiler_params=kernel_params(16),
            cost_estimate=pl.CostEstimate(
                flops=2 * rows * features * input_width,
                bytes_accessed=10000000,
                transcendentals=0,
            ),
            name="project_early",
        )(send, from_near, *from_far, index_here, gain_rows, input_weight)
        *terms, key_fresh, value_fresh = pl.pallas_call(
            functools.partial(step_kernel, total, rank, step, parts, late, by_group),
            out_shape=[sent_terms] * parts + [fresh] * 2,
            in_specs=[vmem] * len(late) + [smem] + [vmem] * (16 + groups + 2 * step),
            out_specs=[vmem] * (parts + 2),
            scratch_shapes=[
                pltpu.VMEM((rows, query_width), bf16),
                pltpu.VMEM((parts, rows, width), bf16),
            ],
            compiler_params=kernel_params(24),
            name="attend_step",
        )(
            *passed_on,
            index_here,
            *sums,
            facts_here,
            gain_rows,
            input_weight,
            query_up,
            key_up,
            value_up,
            query_gain,
            key_gain,
            cosine,
            sine,
            bias,
            *cache,
            *earlier,
            output_weight,
            output_down,
        )
        earlier += [key_fresh, value_fresh]
        received = swap_all(
            terms, "narrow", [0] + far + [mask + 1 for mask in far] + [1]
        )
        if step < STEPS - 1:
            send = pl.pallas_call(
                functools.partial(between_kernel, total, rank, parts),
                out_shape=sent_state,
                in_specs=[vmem] * (parts + 5),
                out_specs=vmem,
                compiler_params=kernel_params(8),
                name="between",
            )(*received, send, facts_here, output_up, gain_slice, down_across)
        else:
            leaving = pl.pallas_call(
                functools.partial(leave_kernel, total, rank, parts),
                out_shape=[jax.ShapeDtypeStruct((capacity, width), bf16)] * groups,
                in_specs=[vmem] * (parts + 3),
                out_specs=[vmem] * groups,
                compiler_params=kernel_params(8),
                name="leave",
            )(*received, send, facts_here, output_up)

    back = swap_all(leaving, "wide", by_group)
    return pl.pallas_call(
        functools.partial(restore_kernel, by_group),
        out_shape=jax.ShapeDtypeStruct((row_group, width), bf16),
        in_specs=[vmem] * (groups + 1),
        out_specs=vmem,
        compiler_params=kernel_params(8),
        name="restore",
    )(place, *back)


def solution(mesh):
    placed = (
        P(("parts", "wide"), "narrow"),
        P(),
        P(None, "narrow"),
        P(None, "narrow"),
        P(None, "narrow"),
        P(),
        P(),
        P("narrow", None),
        P(("parts", "wide"), None, "narrow"),
        P(("parts", "wide"), None, "narrow"),
        P(("parts", "wide"), None, "narrow"),
        P(("parts", "wide"), None, "narrow"),
        P(("parts", "wide"), None, "narrow"),
        P(("parts", "wide"), None, "narrow"),
        P(("parts", "wide"), "narrow", None, None),
        P(("parts", "wide"), "narrow", None, None),
        P(("parts", "wide")),
        P("parts"),
        P("parts"),
    )
    return jax.shard_map(
        shards,
        mesh=mesh,
        in_specs=placed,
        out_specs=P(("parts", "wide"), "narrow"),
        check_vma=False,
    )
```

```python
import functools

import jax
import jax.numpy as jnp
from jax import lax
from jax.experimental import pallas as pl
from jax.experimental.pallas import tpu as pltpu
from jax.sharding import PartitionSpec as P

STEPS = 4

epsilon = 1e-06
rope_base = 1000000.0
blocked = -1e30
f32 = jnp.float32
bf16 = jnp.bfloat16

NT = (((1,), (1,)), ((), ()))
NN = (((1,), (0,)), ((), ()))


def kernel_params(mib):
    return pltpu.CompilerParams(vmem_limit_bytes=mib * 1024 * 1024)


def in_hbm(array):
    return pltpu.with_memory_space_constraint(array, pltpu.HBM)


def in_order(refs, order):
    return [refs[order.index(block)] for block in range(len(order))]


def copy_all(pairs, sems, first=0):
    copies = [
        pltpu.make_async_copy(source, target, sems.at[index])
        for index, (source, target) in enumerate(pairs, first)
    ]
    for copy in copies:
        copy.start()
    return copies


def route_kernel(
    group_ref,
    domain_hbm,
    slot_hbm,
    length_hbm,
    hidden_hbm,
    key_hbm,
    value_hbm,
    down_hbm,
    target_ref,
    place_ref,
    key_ref,
    value_ref,
    down_ref,
    *refs,
):
    groups = len(refs) - 8
    outgoing = refs[:groups]
    count, place, facts, domain_ref, slot_ref, length_ref, hidden_ref, sems = refs[groups:]
    kinds = down_ref.shape[0]
    total = down_hbm.shape[0]
    rank = down_hbm.shape[1] // kinds
    rows, width = hidden_ref.shape
    capacity = outgoing[0].shape[0]
    per_group = slot_ref.shape[0] // groups
    here = group_ref[0]
    *tables, hidden_copy = copy_all(
        [
            (domain_hbm, domain_ref),
            (slot_hbm, slot_ref),
            (length_hbm, length_ref),
            (hidden_hbm, hidden_ref),
        ],
        sems,
    )
    pairs = [(key_hbm, key_ref), (value_hbm, value_ref)]
    for kind in range(kinds):
        for d in range(total):
            pairs.append(
                (
                    down_hbm.at[d, kind * rank : (kind + 1) * rank, :],
                    down_ref.at[kind, d * rank : (d + 1) * rank, :],
                )
            )
    later = copy_all(pairs, sems, 4)
    for group in range(groups):
        count[group] = 0
    places = lax.broadcasted_iota(jnp.int32, (1, groups * capacity), 1)
    columns = lax.broadcasted_iota(jnp.int32, (1, facts.shape[1]), 1)
    for copy in tables:
        copy.wait()

    def put(row, carry):
        slot = slot_ref[domain_ref[here * rows + row]]
        dest = lax.div(slot, per_group)
        position = jnp.minimum(count[dest], capacity - 1)
        count[dest] = position + 1
        target = jnp.bitwise_xor(dest, here) * capacity + position
        target_ref[row] = target
        place[pl.ds(row, 1), :] = jnp.where(places == target, 1.0, 0.0)
        length = length_ref[row].astype(f32)
        local = (slot - dest * per_group).astype(f32)
        facts[pl.ds(row, 1), :] = jnp.where(
            columns == 0, length, jnp.where(columns == 1, local, 0.0)
        )
        return carry

    lax.fori_loop(0, rows, put, 0, unroll=8)
    chosen = place[...].astype(bf16)
    place_ref[...] = chosen
    across = (((0,), (0,)), ((), ()))
    known = lax.dot_general(
        chosen, facts[...].astype(bf16), across, preferred_element_type=f32
    ).astype(bf16)
    hidden_copy.wait()
    state = lax.dot_general(
        chosen, hidden_ref[...], across, preferred_element_type=f32
    ).astype(bf16)
    for s in range(groups):
        block = slice(s * capacity, (s + 1) * capacity)
        outgoing[s][:, :width] = state[block]
        outgoing[s][:, width:] = known[block]
    for copy in later:
        copy.wait()


def pack_kernel(target_ref, key_ref, value_ref, *refs):
    groups = len(refs) - 1
    outgoing, packed = refs[:groups], refs[groups]
    rows, kv_local = key_ref.shape[:2]
    capacity = packed.shape[2]
    if groups * capacity > rows:
        packed[...] = jnp.zeros_like(packed)

    def put(row, carry):
        target = target_ref[row]
        block = lax.div(target, capacity)
        position = target - block * capacity
        for g in range(kv_local):
            packed[block, g, position] = key_ref[row, g]
            packed[block, kv_local + g, position] = value_ref[row, g]
        return carry

    lax.fori_loop(0, rows, put, 0, unroll=4)
    for s in range(groups):
        outgoing[s][...] = packed[s]


def load_inputs_kernel(turn, turn_ref, query, key, value, after, *refs):
    inputs, sems = refs[-2:]

    @pl.when(turn_ref[0] == turn)
    def _():
        pairs = []
        column = 0
        for weight in (query, key, value):
            width = weight.shape[1]
            pairs.append((weight, inputs.at[:, column : column + width]))
            column += width
        for copy in copy_all(pairs, sems):
            copy.wait()

    for held in refs[:-2]:

        @pl.when(turn_ref[0] != turn)
        def _():
            copy = pltpu.make_async_copy(held, inputs, sems.at[0])
            copy.start()
            copy.wait()


def load_others_kernel(*refs):
    count = (len(refs) - 4) // 2 - 1
    sources, output_down, down, _ = refs[:count], *refs[count : count + 3]
    targets = refs[count + 3 : 2 * count + 3]
    output_down_across, down_across, held, sems = refs[2 * count + 3 :]
    copies = copy_all([(output_down, held), *zip(sources, targets)], sems)
    for kind in range(down.shape[0]):
        down_across[kind] = down[kind].T
    copies[0].wait()
    output_down_across[...] = held[...].T
    for copy in copies[1:]:
        copy.wait()


def own_slots(slot, total, rank):
    lane = lax.broadcasted_iota(jnp.int32, (1, 2 * rank), 1)
    second = (lane >= rank).astype(f32)
    return [slot == 2.0 * j + second for j in range(total // 2)]


def spread_over_slots(factor, own):
    twice = jnp.concatenate([factor, factor], axis=1)
    return jnp.concatenate([jnp.where(mask, twice, 0.0).astype(bf16) for mask in own], axis=1)


def pick_slot(product, own):
    wide = own[0].shape[1]
    picked = jnp.where(own[0], product[:, :wide], 0.0)
    for j in range(1, len(own)):
        picked = picked + jnp.where(own[j], product[:, j * wide : (j + 1) * wide], 0.0)
    return picked[:, : wide // 2] + picked[:, wide // 2 :]


def partial_low(state, gain, own, down_ref, form):
    scaled = (state * gain).astype(bf16)
    picked = []
    for kind in range(down_ref.shape[0]):
        product = lax.dot_general(scaled, down_ref[kind], form, preferred_element_type=f32)
        picked.append(pick_slot(product, own).astype(bf16))
    return jnp.concatenate(picked, axis=1)


def enter_kernel(total, rank, order, *refs):
    groups = len(order)
    blocks = in_order(refs[:groups], order)
    gain_ref, down_ref, send_ref, facts_ref = refs[groups:]
    width = down_ref.shape[2]
    everything = jnp.concatenate([block[...] for block in blocks], axis=0)
    facts = everything[:, width:].astype(f32)
    own = own_slots(facts[:, 1:2], total, rank)
    facts_ref[...] = facts
    send_ref[:, :width] = everything[:, :width]
    send_ref[:, width:] = partial_low(
        everything[:, :width].astype(f32), gain_ref[...], own, down_ref, NT
    )


def new_state(own, received, state, up_ref):
    width = state.shape[1]
    low_out = received[0][:, width:].astype(f32)
    projected = received[0][:, :width].astype(f32)
    for part in received[1:]:
        low_out = low_out + part[:, width:].astype(f32)
        projected = projected + part[:, :width].astype(f32)
    spread = spread_over_slots(low_out, own)
    delta = jnp.dot(spread, up_ref[...], preferred_element_type=f32).astype(bf16)
    return (state.astype(f32) + projected + delta.astype(f32)).astype(bf16)


def between_kernel(total, rank, parts, *refs):
    received = refs[:parts]
    state_ref, facts_ref, up_ref, gain_ref, down_ref, send_ref = refs[parts:]
    width = down_ref.shape[1]
    own = own_slots(facts_ref[:, 1:2], total, rank)
    state = new_state(own, received, state_ref[:, :width], up_ref)
    send_ref[:, :width] = state
    send_ref[:, width:] = partial_low(state.astype(f32), gain_ref[...], own, down_ref, NN)


def leave_kernel(total, rank, parts, *refs):
    received = refs[:parts]
    state_ref, facts_ref, up_ref = refs[parts : parts + 3]
    outgoing = refs[parts + 3 :]
    width = up_ref.shape[1]
    capacity = outgoing[0].shape[0]
    own = own_slots(facts_ref[:, 1:2], total, rank)
    state = new_state(own, received, state_ref[:, :width], up_ref)
    for s in range(len(outgoing)):
        outgoing[s][...] = state[s * capacity : (s + 1) * capacity]


def restore_kernel(order, place_ref, *refs):
    blocks, out_ref = in_order(refs[:-1], order), refs[-1]
    back = jnp.concatenate([block[...] for block in blocks], axis=0)
    out_ref[...] = jnp.dot(place_ref[...], back, preferred_element_type=f32).astype(bf16)


def norm_and_rotate(vector, gain, cosine, sine):
    head_dim = vector.shape[1]
    mean = jnp.mean(vector * vector, axis=1, keepdims=True)
    scaled = vector * lax.rsqrt(mean + epsilon) * gain
    return (scaled * cosine + pltpu.roll(scaled, head_dim // 2, 1) * sine).astype(bf16)


def project_slices(slices, masks, here, gain_ref, weight_ref):
    width = gain_ref.shape[2]
    products, squares, low = None, None, None
    for piece, mask in zip(slices, masks):
        source = jnp.bitwise_xor(here, mask)
        state = piece[:, :width].astype(f32)
        scaled = (state * gain_ref[source]).astype(bf16)
        features_there = pl.ds(pl.multiple_of(source * width, 64), width)
        product = jnp.dot(scaled, weight_ref[features_there, :], preferred_element_type=f32)
        square = jnp.sum(state * state, axis=1, keepdims=True)
        part = piece[:, width:].astype(f32)
        products = product if products is None else products + product
        squares = square if squares is None else squares + square
        low = part if low is None else low + part
    return products, squares, low


def early_kernel(masks, *refs):
    slices = refs[: len(masks)]
    index_ref, gain_ref, weight_ref, products_ref, squares_ref, low_ref = refs[len(masks) :]
    products, squares, low = project_slices(slices, masks, index_ref[0], gain_ref, weight_ref)
    products_ref[...] = products
    squares_ref[...] = jnp.broadcast_to(squares, squares_ref.shape)
    low_ref[...] = low


def step_kernel(total, rank, step, parts, masks, order, *refs):
    groups = len(order)
    refs = list(refs)

    def take(count):
        taken = refs[:count]
        del refs[:count]
        return taken

    slices = take(len(masks))
    (
        index_ref,
        products_ref,
        squares_ref,
        low_ref,
        facts_ref,
        gain_ref,
        weight_ref,
        query_up,
        key_up,
        value_up,
        query_gain,
        key_gain,
        cosine_ref,
        sine_ref,
        bias_ref,
    ) = take(15)
    cache = in_order(take(groups), order)
    earlier = take(2 * step)
    output_weight, output_down = take(2)
    outgoing = take(parts)
    key_fresh, value_fresh, attended, terms = refs
    features = weight_ref.shape[0]
    width = features // parts
    rows = products_ref.shape[0]
    head_dim = cache[0].shape[2]
    kv_local = cache[0].shape[0] // 2
    capacity = rows // groups
    query_width = query_up.shape[1]
    key_width = key_up.shape[1]
    heads = query_width // head_dim
    per_kv = heads // kv_local
    here = index_ref[0]

    own = own_slots(facts_ref[:, 1:2], total, rank)
    products, squares, low = project_slices(slices, masks, here, gain_ref, weight_ref)
    inverse = lax.rsqrt((squares_ref[:, :1] + squares) / features + epsilon)
    low = (low_ref[...] + low) * inverse

    def project(columns, up_ref, index):
        spread = spread_over_slots(low[:, index * rank : (index + 1) * rank], own)
        delta = jnp.dot(spread, up_ref[...], preferred_element_type=f32).astype(bf16)
        whole = (products_ref[:, columns] + products[:, columns]) * inverse
        return whole + delta.astype(f32)

    cosine = cosine_ref[step]
    sine = sine_ref[step]
    key = project(slice(query_width, query_width + key_width), key_up, 1)
    value = project(slice(query_width + key_width, None), value_up, 2).astype(bf16)
    for g in range(kv_local):
        columns = slice(g * head_dim, (g + 1) * head_dim)
        key_fresh[g] = norm_and_rotate(key[:, columns], key_gain[...], cosine, sine)
        value_fresh[g] = value[:, columns]
    query = project(slice(0, query_width), query_up, 0)
    query_heads = [
        norm_and_rotate(query[:, h * head_dim : (h + 1) * head_dim], query_gain[...], cosine, sine)
        for h in range(heads)
    ]

    scale = head_dim ** (-0.5)
    fresh_count = (step + 1) * capacity
    lanes = 128 * (-(-fresh_count // 128))
    filler = jnp.zeros((lanes - fresh_count, head_dim), bf16)
    key_place = lax.broadcasted_iota(jnp.int32, (per_kv * capacity, lanes), 1)
    own_row = lax.broadcasted_iota(jnp.int32, (per_kv * capacity, lanes), 0) % capacity
    same_row = (key_place % capacity == own_row) & (key_place < fresh_count)
    def fresh_rows(now, which, g, block):
        return jnp.concatenate(
            [earlier[2 * t + which][g, block, :] for t in range(step)] + [now[g, block, :], filler],
            axis=0,
        )

    together = 4
    for first in range(0, groups, together):
        blocks = [
            (b, slice(b * capacity, (b + 1) * capacity), g)
            for g in range(kv_local)
            for b in range(first, min(first + together, groups))
        ]
        scores = []
        for b, block, g in blocks:
            queries = jnp.concatenate(
                [query_heads[g * per_kv + h][block] for h in range(per_kv)], axis=0
            )
            bias = jnp.concatenate([bias_ref[block, :]] * per_kv, axis=0)
            cached = lax.dot_general(queries, cache[b][g], NT, preferred_element_type=f32)
            fresh = lax.dot_general(
                queries, fresh_rows(key_fresh, 0, g, block), NT, preferred_element_type=f32
            )
            fresh = jnp.where(same_row, fresh * scale, blocked)
            scores.append(jnp.concatenate([cached * scale + bias, fresh], axis=1))
        largest = [jnp.max(score, axis=1, keepdims=True) for score in scores]
        weights = [
            jnp.exp(score - top).astype(bf16) for score, top in zip(scores, largest)
        ]
        mixes = []
        for (b, block, g), weight in zip(blocks, weights):
            values = jnp.concatenate(
                [cache[b][kv_local + g], fresh_rows(value_fresh, 1, g, block)], axis=0
            )
            summing = jnp.concatenate([values, jnp.ones_like(values)], axis=1)
            mixes.append(jnp.dot(weight, summing, preferred_element_type=f32))
        for (b, block, g), mixed in zip(blocks, mixes):
            mixed = (mixed[:, :head_dim] / mixed[:, head_dim:]).astype(bf16)
            for h in range(per_kv):
                head = g * per_kv + h
                attended[block, head * head_dim : (head + 1) * head_dim] = mixed[
                    h * capacity : (h + 1) * capacity
                ]

    attended_rows = attended[...]
    product = jnp.dot(attended_rows, output_down[...], preferred_element_type=f32)
    low_out = pick_slot(product, own).astype(bf16)
    for n in range(parts):
        term = jnp.dot(
            attended_rows,
            output_weight[:, n * width : (n + 1) * width],
            preferred_element_type=f32,
        )
        terms[jnp.bitwise_xor(here, n)] = term.astype(bf16)
    for mask in range(parts):
        outgoing[mask][:, :width] = terms[mask]
        outgoing[mask][:, width:] = low_out


def swap(block, axis, mask):
    return lax.ppermute(block, axis, [(i, i ^ mask) for i in range(lax.axis_size(axis))])


def swap_all(blocks, axis, order):
    return [blocks[0]] + [swap(blocks[mask], axis, mask) for mask in order[1:]]


def shards(
    hidden,
    input_norm_gain,
    query_projection_weight,
    key_projection_weight,
    value_projection_weight,
    query_norm_gain,
    key_norm_gain,
    output_projection_weight,
    stacked_down_factors,
    query_up_factor,
    key_up_factor,
    value_up_factor,
    output_down_factor,
    output_up_factor,
    cached_key_rows,
    cached_value_rows,
    cached_length_rows,
    domain_of_row,
    slot_of_domain,
):
    groups = lax.axis_size("wide")
    parts = lax.axis_size("narrow")
    wide_index = lax.axis_index("wide")
    narrow_index = lax.axis_index("narrow")
    row_group, width = hidden.shape
    capacity = row_group // 4
    rows = groups * capacity
    total = stacked_down_factors.shape[0]
    low_width = stacked_down_factors.shape[1]
    rank = output_up_factor.shape[1]
    _, kv_local, context, head_dim = cached_key_rows.shape
    features = input_norm_gain.shape[0]
    query_width = query_projection_weight.shape[1]

    load_cost = pl.CostEstimate(flops=0, bytes_accessed=20000000, transcendentals=0)
    smem = pl.BlockSpec(memory_space=pltpu.SMEM)
    vmem = pl.BlockSpec(memory_space=pltpu.VMEM)
    hbm = pl.BlockSpec(memory_space=pltpu.HBM)
    outgoing_shape = jax.ShapeDtypeStruct((capacity, width + 128), bf16)
    kinds = low_width // rank
    target, place, keys, values, down, *outgoing = pl.pallas_call(
        route_kernel,
        out_shape=[
            jax.ShapeDtypeStruct((row_group,), jnp.int32),
            jax.ShapeDtypeStruct((row_group, rows), bf16),
            jax.ShapeDtypeStruct(cached_key_rows.shape, bf16),
            jax.ShapeDtypeStruct(cached_value_rows.shape, bf16),
            jax.ShapeDtypeStruct((kinds, total * rank, width), bf16),
        ]
        + [outgoing_shape] * groups,
        in_specs=[smem] + [hbm] * 7,
        out_specs=[smem] + [vmem] * (groups + 4),
        scratch_shapes=[
            pltpu.SMEM((groups,), jnp.int32),
            pltpu.VMEM((row_group, rows), f32),
            pltpu.VMEM((row_group, 128), f32),
            pltpu.SMEM(domain_of_row.shape, jnp.int32),
            pltpu.SMEM(slot_of_domain.shape, jnp.int32),
            pltpu.SMEM(cached_length_rows.shape, jnp.int32),
            pltpu.VMEM(hidden.shape, bf16),
            pltpu.SemaphoreType.DMA((6 + kinds * total,)),
        ],
        compiler_params=kernel_params(16),
        name="route_rows",
    )(
        wide_index.reshape(1),
        in_hbm(domain_of_row),
        in_hbm(slot_of_domain),
        in_hbm(cached_length_rows),
        in_hbm(hidden),
        in_hbm(cached_key_rows),
        in_hbm(cached_value_rows),
        in_hbm(stacked_down_factors),
    )
    by_group = [0] + list(range(groups - 1, 0, -1))
    arrived = swap_all(outgoing, "wide", by_group)
    packed_shape = (2 * kv_local, capacity, context, head_dim)
    packed = pl.pallas_call(
        pack_kernel,
        out_shape=[jax.ShapeDtypeStruct(packed_shape, bf16)] * groups,
        in_specs=[smem, vmem, vmem],
        out_specs=[vmem] * groups,
        scratch_shapes=[pltpu.VMEM((groups,) + packed_shape, bf16)],
        compiler_params=kernel_params(16),
        name="pack_cache",
    )(target, keys, values)
    cache = swap_all(packed, "wide", by_group)
    cache = [block.reshape(2 * kv_local, capacity * context, head_dim) for block in cache]

    gain_rows = input_norm_gain.reshape(parts, 1, width)
    gain_slice = lax.dynamic_index_in_dim(gain_rows, narrow_index, 0, keepdims=False)
    sent_state = jax.ShapeDtypeStruct((rows, width + low_width), bf16)
    key_width = key_projection_weight.shape[1]
    input_width = query_width + 2 * key_width

    def load_inputs(turn, after, *held):
        return pl.pallas_call(
            functools.partial(load_inputs_kernel, turn),
            out_shape=jax.ShapeDtypeStruct((features, input_width), bf16),
            in_specs=[smem] + [hbm] * 3 + [vmem] * (1 + len(held)),
            out_specs=vmem,
            scratch_shapes=[pltpu.SemaphoreType.DMA((3,))],
            compiler_params=kernel_params(18),
            cost_estimate=load_cost,
            name="load_inputs",
        )(
            lax.rem(wide_index, 2).reshape(1),
            in_hbm(query_projection_weight),
            in_hbm(key_projection_weight),
            in_hbm(value_projection_weight),
            after,
            *held,
        )

    input_weight = load_inputs(1, arrived[-1])
    input_weight, *arrived = lax.optimization_barrier((input_weight, *arrived))
    send, facts_here = pl.pallas_call(
        functools.partial(enter_kernel, total, rank, by_group),
        out_shape=[sent_state, jax.ShapeDtypeStruct((rows, 128), f32)],
        in_specs=[vmem] * (groups + 2),
        out_specs=[vmem] * 2,
        compiler_params=kernel_params(8),
        name="enter",
    )(*arrived, gain_slice, down)

    def load_others(after):
        others = [
            query_up_factor.reshape(total * rank, query_width),
            key_up_factor.reshape(total * rank, key_width),
            value_up_factor.reshape(total * rank, key_width),
            output_projection_weight,
            output_up_factor.reshape(total * rank, width),
        ]
        turned = [
            jax.ShapeDtypeStruct((query_width, total * rank), bf16),
            jax.ShapeDtypeStruct((kinds, width, total * rank), bf16),
        ]
        return pl.pallas_call(
            load_others_kernel,
            out_shape=[jax.ShapeDtypeStruct(array.shape, bf16) for array in others] + turned,
            in_specs=[hbm] * (len(others) + 1) + [vmem] * 2,
            out_specs=[vmem] * (len(others) + 2),
            scratch_shapes=[
                pltpu.VMEM((total * rank, query_width), bf16),
                pltpu.SemaphoreType.DMA((len(others) + 1,)),
            ],
            compiler_params=kernel_params(20),
            cost_estimate=load_cost,
            name="load_others",
        )(
            *[in_hbm(array) for array in others],
            in_hbm(output_down_factor.reshape(total * rank, query_width)),
            down,
            after,
        )

    lengths = facts_here[:, 0]
    frequency = rope_base ** (-(jnp.arange(head_dim // 2, dtype=f32) * 2.0) / head_dim)
    positions = lengths[None, :] + jnp.arange(STEPS, dtype=f32)[:, None]
    angles = positions[:, :, None] * frequency
    cosine = jnp.cos(angles)
    sine = jnp.sin(angles)
    cosine = jnp.concatenate([cosine, cosine], axis=-1)
    sine = jnp.concatenate([-sine, sine], axis=-1)
    key_index = jnp.arange(capacity * context)[None, :]
    visible = (key_index // context == (jnp.arange(rows) % capacity)[:, None]) & (
        (key_index % context).astype(f32) < lengths[:, None]
    )
    bias = jnp.where(visible, 0.0, blocked).astype(f32)

    query_gain = query_norm_gain.reshape(1, head_dim)
    key_gain = key_norm_gain.reshape(1, head_dim)
    index_here = narrow_index.reshape(1)
    sent_terms = jax.ShapeDtypeStruct((rows, width + rank), bf16)
    fresh = jax.ShapeDtypeStruct((kv_local, rows, head_dim), bf16)
    far = [mask for mask in range(2, parts) if mask % 2 == 0]
    early = [0, 1] + far
    late = [mask ^ 1 for mask in far]

    earlier = []
    for step in range(STEPS):
        from_far = [swap(send, "narrow", mask) for mask in far]
        from_near = swap(send, "narrow", 1)
        if step == 0:
            input_weight = load_inputs(0, facts_here, input_weight)
            input_weight, *from_far = lax.optimization_barrier((input_weight, *from_far))
        passed_on = [swap(piece, "narrow", 1) for piece in from_far]
        if step == 0:
            *others, output_down, down_across = load_others(from_far[0])
            query_up, key_up, value_up, output_weight, output_up = others
        sums = pl.pallas_call(
            functools.partial(early_kernel, early),
            out_shape=[
                jax.ShapeDtypeStruct((rows, input_width), f32),
                jax.ShapeDtypeStruct((rows, 128), f32),
                jax.ShapeDtypeStruct((rows, low_width), f32),
            ],
            in_specs=[vmem] * len(early) + [smem] + [vmem] * 2,
            out_specs=[vmem] * 3,
            compiler_params=kernel_params(16),
            cost_estimate=pl.CostEstimate(
                flops=2 * rows * features * input_width,
                bytes_accessed=10000000,
                transcendentals=0,
            ),
            name="project_early",
        )(send, from_near, *from_far, index_here, gain_rows, input_weight)
        *terms, key_fresh, value_fresh = pl.pallas_call(
            functools.partial(step_kernel, total, rank, step, parts, late, by_group),
            out_shape=[sent_terms] * parts + [fresh] * 2,
            in_specs=[vmem] * len(late) + [smem] + [vmem] * (16 + groups + 2 * step),
            out_specs=[vmem] * (parts + 2),
            scratch_shapes=[
                pltpu.VMEM((rows, query_width), bf16),
                pltpu.VMEM((parts, rows, width), bf16),
            ],
            compiler_params=kernel_params(24),
            name="attend_step",
        )(
            *passed_on,
            index_here,
            *sums,
            facts_here,
            gain_rows,
            input_weight,
            query_up,
            key_up,
            value_up,
            query_gain,
            key_gain,
            cosine,
            sine,
            bias,
            *cache,
            *earlier,
            output_weight,
            output_down,
        )
        earlier += [key_fresh, value_fresh]
        received = swap_all(
            terms, "narrow", [0] + far + [mask + 1 for mask in far] + [1]
        )
        if step < STEPS - 1:
            send = pl.pallas_call(
                functools.partial(between_kernel, total, rank, parts),
                out_shape=sent_state,
                in_specs=[vmem] * (parts + 5),
                out_specs=vmem,
                compiler_params=kernel_params(8),
                name="between",
            )(*received, send, facts_here, output_up, gain_slice, down_across)
        else:
            leaving = pl.pallas_call(
                functools.partial(leave_kernel, total, rank, parts),
                out_shape=[jax.ShapeDtypeStruct((capacity, width), bf16)] * groups,
                in_specs=[vmem] * (parts + 3),
                out_specs=[vmem] * groups,
                compiler_params=kernel_params(8),
                name="leave",
            )(*received, send, facts_here, output_up)

    back = swap_all(leaving, "wide", by_group)
    return pl.pallas_call(
        functools.partial(restore_kernel, by_group),
        out_shape=jax.ShapeDtypeStruct((row_group, width), bf16),
        in_specs=[vmem] * (groups + 1),
        out_specs=vmem,
        compiler_params=kernel_params(8),
        name="restore",
    )(place, *back)


def solution(mesh):
    placed = (
        P(("parts", "wide"), "narrow"),
        P(),
        P(None, "narrow"),
        P(None, "narrow"),
        P(None, "narrow"),
        P(),
        P(),
        P("narrow", None),
        P(("parts", "wide"), None, "narrow"),
        P(("parts", "wide"), None, "narrow"),
        P(("parts", "wide"), None, "narrow"),
        P(("parts", "wide"), None, "narrow"),
        P(("parts", "wide"), None, "narrow"),
        P(("parts", "wide"), None, "narrow"),
        P(("parts", "wide"), "narrow", None, None),
        P(("parts", "wide"), "narrow", None, None),
        P(("parts", "wide")),
        P("parts"),
        P("parts"),
    )
    return jax.shard_map(
        shards,
        mesh=mesh,
        in_specs=placed,
        out_specs=P(("parts", "wide"), "narrow"),
        check_vma=False,
    )
```

```python
import functools

import jax
import jax.numpy as jnp
from jax import lax
from jax.experimental import pallas as pl
from jax.experimental.pallas import tpu as pltpu
from jax.sharding import PartitionSpec as P

STEPS = 4

epsilon = 1e-06
rope_base = 1000000.0
blocked = -1e30
f32 = jnp.float32
bf16 = jnp.bfloat16

NT = (((1,), (1,)), ((), ()))
NN = (((1,), (0,)), ((), ()))


def kernel_params(mib):
    return pltpu.CompilerParams(vmem_limit_bytes=mib * 1024 * 1024)


def in_hbm(array):
    return pltpu.with_memory_space_constraint(array, pltpu.HBM)


def in_order(refs, order):
    return [refs[order.index(block)] for block in range(len(order))]


def copy_all(pairs, sems, first=0):
    copies = [
        pltpu.make_async_copy(source, target, sems.at[index])
        for index, (source, target) in enumerate(pairs, first)
    ]
    for copy in copies:
        copy.start()
    return copies


def route_kernel(
    group_ref,
    domain_hbm,
    slot_hbm,
    length_hbm,
    hidden_hbm,
    key_hbm,
    value_hbm,
    down_hbm,
    target_ref,
    place_ref,
    key_ref,
    value_ref,
    down_ref,
    *refs,
):
    groups = len(refs) - 8
    outgoing = refs[:groups]
    count, place, facts, domain_ref, slot_ref, length_ref, hidden_ref, sems = refs[groups:]
    kinds = down_ref.shape[0]
    total = down_hbm.shape[0]
    rank = down_hbm.shape[1] // kinds
    rows, width = hidden_ref.shape
    capacity = outgoing[0].shape[0]
    per_group = slot_ref.shape[0] // groups
    here = group_ref[0]
    *tables, hidden_copy = copy_all(
        [
            (domain_hbm, domain_ref),
            (slot_hbm, slot_ref),
            (length_hbm, length_ref),
            (hidden_hbm, hidden_ref),
        ],
        sems,
    )
    pairs = [(key_hbm, key_ref), (value_hbm, value_ref)]
    for kind in range(kinds):
        for d in range(total):
            pairs.append(
                (
                    down_hbm.at[d, kind * rank : (kind + 1) * rank, :],
                    down_ref.at[kind, d * rank : (d + 1) * rank, :],
                )
            )
    later = copy_all(pairs, sems, 4)
    for group in range(groups):
        count[group] = 0
    places = lax.broadcasted_iota(jnp.int32, (1, groups * capacity), 1)
    columns = lax.broadcasted_iota(jnp.int32, (1, facts.shape[1]), 1)
    for copy in tables:
        copy.wait()

    def put(row, carry):
        slot = slot_ref[domain_ref[here * rows + row]]
        dest = lax.div(slot, per_group)
        position = jnp.minimum(count[dest], capacity - 1)
        count[dest] = position + 1
        target = jnp.bitwise_xor(dest, here) * capacity + position
        target_ref[row] = target
        place[pl.ds(row, 1), :] = jnp.where(places == target, 1.0, 0.0)
        length = length_ref[row].astype(f32)
        local = (slot - dest * per_group).astype(f32)
        facts[pl.ds(row, 1), :] = jnp.where(
            columns == 0, length, jnp.where(columns == 1, local, 0.0)
        )
        return carry

    lax.fori_loop(0, rows, put, 0, unroll=8)
    chosen = place[...].astype(bf16)
    place_ref[...] = chosen
    across = (((0,), (0,)), ((), ()))
    known = lax.dot_general(
        chosen, facts[...].astype(bf16), across, preferred_element_type=f32
    ).astype(bf16)
    hidden_copy.wait()
    state = lax.dot_general(
        chosen, hidden_ref[...], across, preferred_element_type=f32
    ).astype(bf16)
    for s in range(groups):
        block = slice(s * capacity, (s + 1) * capacity)
        outgoing[s][:, :width] = state[block]
        outgoing[s][:, width:] = known[block]
    for copy in later:
        copy.wait()


def pack_kernel(target_ref, key_ref, value_ref, *refs):
    groups = len(refs) - 1
    outgoing, packed = refs[:groups], refs[groups]
    rows, kv_local = key_ref.shape[:2]
    capacity = packed.shape[2]
    if groups * capacity > rows:
        packed[...] = jnp.zeros_like(packed)

    def put(row, carry):
        target = target_ref[row]
        block = lax.div(target, capacity)
        position = target - block * capacity
        for g in range(kv_local):
            packed[block, g, position] = key_ref[row, g]
            packed[block, kv_local + g, position] = value_ref[row, g]
        return carry

    lax.fori_loop(0, rows, put, 0, unroll=4)
    for s in range(groups):
        outgoing[s][...] = packed[s]


def load_inputs_kernel(turn, turn_ref, query, key, value, after, *refs):
    inputs, sems = refs[-2:]

    @pl.when(turn_ref[0] == turn)
    def _():
        pairs = []
        column = 0
        for weight in (query, key, value):
            width = weight.shape[1]
            pairs.append((weight, inputs.at[:, column : column + width]))
            column += width
        for copy in copy_all(pairs, sems):
            copy.wait()

    for held in refs[:-2]:

        @pl.when(turn_ref[0] != turn)
        def _():
            copy = pltpu.make_async_copy(held, inputs, sems.at[0])
            copy.start()
            copy.wait()


def load_others_kernel(*refs):
    count = (len(refs) - 4) // 2 - 1
    sources, output_down, down, _ = refs[:count], *refs[count : count + 3]
    targets = refs[count + 3 : 2 * count + 3]
    output_down_across, down_across, held, sems = refs[2 * count + 3 :]
    copies = copy_all([(output_down, held), *zip(sources, targets)], sems)
    for kind in range(down.shape[0]):
        down_across[kind] = down[kind].T
    copies[0].wait()
    output_down_across[...] = held[...].T
    for copy in copies[1:]:
        copy.wait()


def own_slots(slot, total, rank):
    lane = lax.broadcasted_iota(jnp.int32, (1, 2 * rank), 1)
    second = (lane >= rank).astype(f32)
    return [slot == 2.0 * j + second for j in range(total // 2)]


def spread_over_slots(factor, own):
    twice = jnp.concatenate([factor, factor], axis=1)
    return jnp.concatenate([jnp.where(mask, twice, 0.0).astype(bf16) for mask in own], axis=1)


def pick_slot(product, own):
    wide = own[0].shape[1]
    picked = jnp.where(own[0], product[:, :wide], 0.0)
    for j in range(1, len(own)):
        picked = picked + jnp.where(own[j], product[:, j * wide : (j + 1) * wide], 0.0)
    return picked[:, : wide // 2] + picked[:, wide // 2 :]


def partial_low(state, gain, own, down_ref, form):
    scaled = (state * gain).astype(bf16)
    picked = []
    for kind in range(down_ref.shape[0]):
        product = lax.dot_general(scaled, down_ref[kind], form, preferred_element_type=f32)
        picked.append(pick_slot(product, own).astype(bf16))
    return jnp.concatenate(picked, axis=1)


def enter_kernel(total, rank, order, *refs):
    groups = len(order)
    blocks = in_order(refs[:groups], order)
    gain_ref, down_ref, send_ref, facts_ref = refs[groups:]
    width = down_ref.shape[2]
    everything = jnp.concatenate([block[...] for block in blocks], axis=0)
    facts = everything[:, width:].astype(f32)
    own = own_slots(facts[:, 1:2], total, rank)
    facts_ref[...] = facts
    send_ref[:, :width] = everything[:, :width]
    send_ref[:, width:] = partial_low(
        everything[:, :width].astype(f32), gain_ref[...], own, down_ref, NT
    )


def new_state(own, received, state, up_ref):
    width = state.shape[1]
    low_out = received[0][:, width:].astype(f32)
    projected = received[0][:, :width].astype(f32)
    for part in received[1:]:
        low_out = low_out + part[:, width:].astype(f32)
        projected = projected + part[:, :width].astype(f32)
    spread = spread_over_slots(low_out, own)
    delta = jnp.dot(spread, up_ref[...], preferred_element_type=f32).astype(bf16)
    return (state.astype(f32) + projected + delta.astype(f32)).astype(bf16)


def between_kernel(total, rank, parts, *refs):
    received = refs[:parts]
    state_ref, facts_ref, up_ref, gain_ref, down_ref, send_ref = refs[parts:]
    width = down_ref.shape[1]
    own = own_slots(facts_ref[:, 1:2], total, rank)
    state = new_state(own, received, state_ref[:, :width], up_ref)
    send_ref[:, :width] = state
    send_ref[:, width:] = partial_low(state.astype(f32), gain_ref[...], own, down_ref, NN)


def leave_kernel(total, rank, parts, *refs):
    received = refs[:parts]
    state_ref, facts_ref, up_ref = refs[parts : parts + 3]
    outgoing = refs[parts + 3 :]
    width = up_ref.shape[1]
    capacity = outgoing[0].shape[0]
    own = own_slots(facts_ref[:, 1:2], total, rank)
    state = new_state(own, received, state_ref[:, :width], up_ref)
    for s in range(len(outgoing)):
        outgoing[s][...] = state[s * capacity : (s + 1) * capacity]


def restore_kernel(order, place_ref, *refs):
    blocks, out_ref = in_order(refs[:-1], order), refs[-1]
    back = jnp.concatenate([block[...] for block in blocks], axis=0)
    out_ref[...] = jnp.dot(place_ref[...], back, preferred_element_type=f32).astype(bf16)


def norm_and_rotate(vector, gain, cosine, sine):
    head_dim = vector.shape[1]
    mean = jnp.mean(vector * vector, axis=1, keepdims=True)
    scaled = vector * lax.rsqrt(mean + epsilon) * gain
    return (scaled * cosine + pltpu.roll(scaled, head_dim // 2, 1) * sine).astype(bf16)


def project_slices(slices, masks, here, gain_ref, weight_ref):
    width = gain_ref.shape[2]
    products, squares, low = None, None, None
    for piece, mask in zip(slices, masks):
        source = jnp.bitwise_xor(here, mask)
        state = piece[:, :width].astype(f32)
        scaled = (state * gain_ref[source]).astype(bf16)
        features_there = pl.ds(pl.multiple_of(source * width, 64), width)
        product = jnp.dot(scaled, weight_ref[features_there, :], preferred_element_type=f32)
        square = jnp.sum(state * state, axis=1, keepdims=True)
        part = piece[:, width:].astype(f32)
        products = product if products is None else products + product
        squares = square if squares is None else squares + square
        low = part if low is None else low + part
    return products, squares, low


def early_kernel(masks, *refs):
    slices = refs[: len(masks)]
    index_ref, gain_ref, weight_ref, products_ref, squares_ref, low_ref = refs[len(masks) :]
    products, squares, low = project_slices(slices, masks, index_ref[0], gain_ref, weight_ref)
    products_ref[...] = products
    squares_ref[...] = jnp.broadcast_to(squares, squares_ref.shape)
    low_ref[...] = low


def step_kernel(total, rank, step, parts, masks, order, *refs):
    groups = len(order)
    refs = list(refs)

    def take(count):
        taken = refs[:count]
        del refs[:count]
        return taken

    slices = take(len(masks))
    (
        index_ref,
        products_ref,
        squares_ref,
        low_ref,
        facts_ref,
        gain_ref,
        weight_ref,
        query_up,
        key_up,
        value_up,
        query_gain,
        key_gain,
        cosine_ref,
        sine_ref,
        bias_ref,
    ) = take(15)
    cache = in_order(take(groups), order)
    earlier = take(2 * step)
    output_weight, output_down = take(2)
    outgoing = take(parts)
    key_fresh, value_fresh, attended, terms = refs
    features = weight_ref.shape[0]
    width = features // parts
    rows = products_ref.shape[0]
    head_dim = cache[0].shape[2]
    kv_local = cache[0].shape[0] // 2
    capacity = rows // groups
    query_width = query_up.shape[1]
    key_width = key_up.shape[1]
    heads = query_width // head_dim
    per_kv = heads // kv_local
    here = index_ref[0]

    own = own_slots(facts_ref[:, 1:2], total, rank)
    products, squares, low = project_slices(slices, masks, here, gain_ref, weight_ref)
    inverse = lax.rsqrt((squares_ref[:, :1] + squares) / features + epsilon)
    low = (low_ref[...] + low) * inverse

    def project(columns, up_ref, index):
        spread = spread_over_slots(low[:, index * rank : (index + 1) * rank], own)
        delta = jnp.dot(spread, up_ref[...], preferred_element_type=f32).astype(bf16)
        whole = (products_ref[:, columns] + products[:, columns]) * inverse
        return whole + delta.astype(f32)

    cosine = cosine_ref[step]
    sine = sine_ref[step]
    key = project(slice(query_width, query_width + key_width), key_up, 1)
    value = project(slice(query_width + key_width, None), value_up, 2).astype(bf16)
    for g in range(kv_local):
        columns = slice(g * head_dim, (g + 1) * head_dim)
        key_fresh[g] = norm_and_rotate(key[:, columns], key_gain[...], cosine, sine)
        value_fresh[g] = value[:, columns]
    query = project(slice(0, query_width), query_up, 0)
    query_heads = [
        norm_and_rotate(query[:, h * head_dim : (h + 1) * head_dim], query_gain[...], cosine, sine)
        for h in range(heads)
    ]

    scale = head_dim ** (-0.5)
    fresh_count = (step + 1) * capacity
    lanes = 128 * (-(-fresh_count // 128))
    filler = jnp.zeros((lanes - fresh_count, head_dim), bf16)
    key_place = lax.broadcasted_iota(jnp.int32, (per_kv * capacity, lanes), 1)
    own_row = lax.broadcasted_iota(jnp.int32, (per_kv * capacity, lanes), 0) % capacity
    same_row = (key_place % capacity == own_row) & (key_place < fresh_count)
    def fresh_rows(now, which, g, block):
        return jnp.concatenate(
            [earlier[2 * t + which][g, block, :] for t in range(step)] + [now[g, block, :], filler],
            axis=0,
        )

    together = 4
    for first in range(0, groups, together):
        blocks = [
            (b, slice(b * capacity, (b + 1) * capacity), g)
            for g in range(kv_local)
            for b in range(first, min(first + together, groups))
        ]
        scores = []
        for b, block, g in blocks:
            queries = jnp.concatenate(
                [query_heads[g * per_kv + h][block] for h in range(per_kv)], axis=0
            )
            bias = jnp.concatenate([bias_ref[block, :]] * per_kv, axis=0)
            cached = lax.dot_general(queries, cache[b][g], NT, preferred_element_type=f32)
            fresh = lax.dot_general(
                queries, fresh_rows(key_fresh, 0, g, block), NT, preferred_element_type=f32
            )
            fresh = jnp.where(same_row, fresh * scale, blocked)
            scores.append(jnp.concatenate([cached * scale + bias, fresh], axis=1))
        largest = [jnp.max(score, axis=1, keepdims=True) for score in scores]
        weights = [
            jnp.exp(score - top).astype(bf16) for score, top in zip(scores, largest)
        ]
        mixes = []
        for (b, block, g), weight in zip(blocks, weights):
            values = jnp.concatenate(
                [cache[b][kv_local + g], fresh_rows(value_fresh, 1, g, block)], axis=0
            )
            summing = jnp.concatenate([values, jnp.ones_like(values)], axis=1)
            mixes.append(jnp.dot(weight, summing, preferred_element_type=f32))
        for (b, block, g), mixed in zip(blocks, mixes):
            mixed = (mixed[:, :head_dim] / mixed[:, head_dim:]).astype(bf16)
            for h in range(per_kv):
                head = g * per_kv + h
                attended[block, head * head_dim : (head + 1) * head_dim] = mixed[
                    h * capacity : (h + 1) * capacity
                ]

    attended_rows = attended[...]
    product = jnp.dot(attended_rows, output_down[...], preferred_element_type=f32)
    low_out = pick_slot(product, own).astype(bf16)
    for n in range(parts):
        term = jnp.dot(
            attended_rows,
            output_weight[:, n * width : (n + 1) * width],
            preferred_element_type=f32,
        )
        terms[jnp.bitwise_xor(here, n)] = term.astype(bf16)
    for mask in range(parts):
        outgoing[mask][:, :width] = terms[mask]
        outgoing[mask][:, width:] = low_out


def swap(block, axis, mask):
    return lax.ppermute(block, axis, [(i, i ^ mask) for i in range(lax.axis_size(axis))])


def swap_all(blocks, axis, order):
    return [blocks[0]] + [swap(blocks[mask], axis, mask) for mask in order[1:]]


def shards(
    hidden,
    input_norm_gain,
    query_projection_weight,
    key_projection_weight,
    value_projection_weight,
    query_norm_gain,
    key_norm_gain,
    output_projection_weight,
    stacked_down_factors,
    query_up_factor,
    key_up_factor,
    value_up_factor,
    output_down_factor,
    output_up_factor,
    cached_key_rows,
    cached_value_rows,
    cached_length_rows,
    domain_of_row,
    slot_of_domain,
):
    groups = lax.axis_size("wide")
    parts = lax.axis_size("narrow")
    wide_index = lax.axis_index("wide")
    narrow_index = lax.axis_index("narrow")
    row_group, width = hidden.shape
    capacity = row_group // 4
    rows = groups * capacity
    total = stacked_down_factors.shape[0]
    low_width = stacked_down_factors.shape[1]
    rank = output_up_factor.shape[1]
    _, kv_local, context, head_dim = cached_key_rows.shape
    features = input_norm_gain.shape[0]
    query_width = query_projection_weight.shape[1]

    load_cost = pl.CostEstimate(flops=0, bytes_accessed=20000000, transcendentals=0)
    smem = pl.BlockSpec(memory_space=pltpu.SMEM)
    vmem = pl.BlockSpec(memory_space=pltpu.VMEM)
    hbm = pl.BlockSpec(memory_space=pltpu.HBM)
    outgoing_shape = jax.ShapeDtypeStruct((capacity, width + 128), bf16)
    kinds = low_width // rank
    target, place, keys, values, down, *outgoing = pl.pallas_call(
        route_kernel,
        out_shape=[
            jax.ShapeDtypeStruct((row_group,), jnp.int32),
            jax.ShapeDtypeStruct((row_group, rows), bf16),
            jax.ShapeDtypeStruct(cached_key_rows.shape, bf16),
            jax.ShapeDtypeStruct(cached_value_rows.shape, bf16),
            jax.ShapeDtypeStruct((kinds, total * rank, width), bf16),
        ]
        + [outgoing_shape] * groups,
        in_specs=[smem] + [hbm] * 7,
        out_specs=[smem] + [vmem] * (groups + 4),
        scratch_shapes=[
            pltpu.SMEM((groups,), jnp.int32),
            pltpu.VMEM((row_group, rows), f32),
            pltpu.VMEM((row_group, 128), f32),
            pltpu.SMEM(domain_of_row.shape, jnp.int32),
            pltpu.SMEM(slot_of_domain.shape, jnp.int32),
            pltpu.SMEM(cached_length_rows.shape, jnp.int32),
            pltpu.VMEM(hidden.shape, bf16),
            pltpu.SemaphoreType.DMA((6 + kinds * total,)),
        ],
        compiler_params=kernel_params(16),
        name="route_rows",
    )(
        wide_index.reshape(1),
        in_hbm(domain_of_row),
        in_hbm(slot_of_domain),
        in_hbm(cached_length_rows),
        in_hbm(hidden),
        in_hbm(cached_key_rows),
        in_hbm(cached_value_rows),
        in_hbm(stacked_down_factors),
    )
    by_group = [0] + list(range(groups - 1, 0, -1))
    arrived = swap_all(outgoing, "wide", by_group)
    packed_shape = (2 * kv_local, capacity, context, head_dim)
    packed = pl.pallas_call(
        pack_kernel,
        out_shape=[jax.ShapeDtypeStruct(packed_shape, bf16)] * groups,
        in_specs=[smem, vmem, vmem],
        out_specs=[vmem] * groups,
        scratch_shapes=[pltpu.VMEM((groups,) + packed_shape, bf16)],
        compiler_params=kernel_params(16),
        name="pack_cache",
    )(target, keys, values)
    cache = swap_all(packed, "wide", by_group)
    cache = [block.reshape(2 * kv_local, capacity * context, head_dim) for block in cache]

    gain_rows = input_norm_gain.reshape(parts, 1, width)
    gain_slice = lax.dynamic_index_in_dim(gain_rows, narrow_index, 0, keepdims=False)
    sent_state = jax.ShapeDtypeStruct((rows, width + low_width), bf16)
    key_width = key_projection_weight.shape[1]
    input_width = query_width + 2 * key_width

    def load_inputs(turn, after, *held):
        return pl.pallas_call(
            functools.partial(load_inputs_kernel, turn),
            out_shape=jax.ShapeDtypeStruct((features, input_width), bf16),
            in_specs=[smem] + [hbm] * 3 + [vmem] * (1 + len(held)),
            out_specs=vmem,
            scratch_shapes=[pltpu.SemaphoreType.DMA((3,))],
            compiler_params=kernel_params(18),
            cost_estimate=load_cost,
            name="load_inputs",
        )(
            lax.rem(wide_index, 2).reshape(1),
            in_hbm(query_projection_weight),
            in_hbm(key_projection_weight),
            in_hbm(value_projection_weight),
            after,
            *held,
        )

    input_weight = load_inputs(1, packed[0])
    input_weight, *arrived = lax.optimization_barrier((input_weight, *arrived))
    send, facts_here = pl.pallas_call(
        functools.partial(enter_kernel, total, rank, by_group),
        out_shape=[sent_state, jax.ShapeDtypeStruct((rows, 128), f32)],
        in_specs=[vmem] * (groups + 2),
        out_specs=[vmem] * 2,
        compiler_params=kernel_params(8),
        name="enter",
    )(*arrived, gain_slice, down)

    def load_others(after):
        others = [
            query_up_factor.reshape(total * rank, query_width),
            key_up_factor.reshape(total * rank, key_width),
            value_up_factor.reshape(total * rank, key_width),
            output_projection_weight,
            output_up_factor.reshape(total * rank, width),
        ]
        turned = [
            jax.ShapeDtypeStruct((query_width, total * rank), bf16),
            jax.ShapeDtypeStruct((kinds, width, total * rank), bf16),
        ]
        return pl.pallas_call(
            load_others_kernel,
            out_shape=[jax.ShapeDtypeStruct(array.shape, bf16) for array in others] + turned,
            in_specs=[hbm] * (len(others) + 1) + [vmem] * 2,
            out_specs=[vmem] * (len(others) + 2),
            scratch_shapes=[
                pltpu.VMEM((total * rank, query_width), bf16),
                pltpu.SemaphoreType.DMA((len(others) + 1,)),
            ],
            compiler_params=kernel_params(20),
            cost_estimate=load_cost,
            name="load_others",
        )(
            *[in_hbm(array) for array in others],
            in_hbm(output_down_factor.reshape(total * rank, query_width)),
            down,
            after,
        )

    lengths = facts_here[:, 0]
    frequency = rope_base ** (-(jnp.arange(head_dim // 2, dtype=f32) * 2.0) / head_dim)
    positions = lengths[None, :] + jnp.arange(STEPS, dtype=f32)[:, None]
    angles = positions[:, :, None] * frequency
    cosine = jnp.cos(angles)
    sine = jnp.sin(angles)
    cosine = jnp.concatenate([cosine, cosine], axis=-1)
    sine = jnp.concatenate([-sine, sine], axis=-1)
    key_index = jnp.arange(capacity * context)[None, :]
    visible = (key_index // context == (jnp.arange(rows) % capacity)[:, None]) & (
        (key_index % context).astype(f32) < lengths[:, None]
    )
    bias = jnp.where(visible, 0.0, blocked).astype(f32)

    query_gain = query_norm_gain.reshape(1, head_dim)
    key_gain = key_norm_gain.reshape(1, head_dim)
    index_here = narrow_index.reshape(1)
    sent_terms = jax.ShapeDtypeStruct((rows, width + rank), bf16)
    fresh = jax.ShapeDtypeStruct((kv_local, rows, head_dim), bf16)
    far = [mask for mask in range(2, parts) if mask % 2 == 0]
    early = [0, 1] + far
    late = [mask ^ 1 for mask in far]

    earlier = []
    for step in range(STEPS):
        from_far = [swap(send, "narrow", mask) for mask in far]
        from_near = swap(send, "narrow", 1)
        if step == 0:
            input_weight = load_inputs(0, facts_here, input_weight)
            input_weight, *from_far = lax.optimization_barrier((input_weight, *from_far))
        passed_on = [swap(piece, "narrow", 1) for piece in from_far]
        if step == 0:
            *others, output_down, down_across = load_others(from_far[0])
            query_up, key_up, value_up, output_weight, output_up = others
        sums = pl.pallas_call(
            functools.partial(early_kernel, early),
            out_shape=[
                jax.ShapeDtypeStruct((rows, input_width), f32),
                jax.ShapeDtypeStruct((rows, 128), f32),
                jax.ShapeDtypeStruct((rows, low_width), f32),
            ],
            in_specs=[vmem] * len(early) + [smem] + [vmem] * 2,
            out_specs=[vmem] * 3,
            compiler_params=kernel_params(16),
            cost_estimate=pl.CostEstimate(
                flops=2 * rows * features * input_width,
                bytes_accessed=10000000,
                transcendentals=0,
            ),
            name="project_early",
        )(send, from_near, *from_far, index_here, gain_rows, input_weight)
        *terms, key_fresh, value_fresh = pl.pallas_call(
            functools.partial(step_kernel, total, rank, step, parts, late, by_group),
            out_shape=[sent_terms] * parts + [fresh] * 2,
            in_specs=[vmem] * len(late) + [smem] + [vmem] * (16 + groups + 2 * step),
            out_specs=[vmem] * (parts + 2),
            scratch_shapes=[
                pltpu.VMEM((rows, query_width), bf16),
                pltpu.VMEM((parts, rows, width), bf16),
            ],
            compiler_params=kernel_params(24),
            name="attend_step",
        )(
            *passed_on,
            index_here,
            *sums,
            facts_here,
            gain_rows,
            input_weight,
            query_up,
            key_up,
            value_up,
            query_gain,
            key_gain,
            cosine,
            sine,
            bias,
            *cache,
            *earlier,
            output_weight,
            output_down,
        )
        earlier += [key_fresh, value_fresh]
        received = swap_all(
            terms, "narrow", [0] + far + [mask + 1 for mask in far] + [1]
        )
        if step < STEPS - 1:
            send = pl.pallas_call(
                functools.partial(between_kernel, total, rank, parts),
                out_shape=sent_state,
                in_specs=[vmem] * (parts + 5),
                out_specs=vmem,
                compiler_params=kernel_params(8),
                name="between",
            )(*received, send, facts_here, output_up, gain_slice, down_across)
        else:
            leaving = pl.pallas_call(
                functools.partial(leave_kernel, total, rank, parts),
                out_shape=[jax.ShapeDtypeStruct((capacity, width), bf16)] * groups,
                in_specs=[vmem] * (parts + 3),
                out_specs=[vmem] * groups,
                compiler_params=kernel_params(8),
                name="leave",
            )(*received, send, facts_here, output_up)

    back = swap_all(leaving, "wide", by_group)
    return pl.pallas_call(
        functools.partial(restore_kernel, by_group),
        out_shape=jax.ShapeDtypeStruct((row_group, width), bf16),
        in_specs=[vmem] * (groups + 1),
        out_specs=vmem,
        compiler_params=kernel_params(8),
        name="restore",
    )(place, *back)


def solution(mesh):
    placed = (
        P(("parts", "wide"), "narrow"),
        P(),
        P(None, "narrow"),
        P(None, "narrow"),
        P(None, "narrow"),
        P(),
        P(),
        P("narrow", None),
        P(("parts", "wide"), None, "narrow"),
        P(("parts", "wide"), None, "narrow"),
        P(("parts", "wide"), None, "narrow"),
        P(("parts", "wide"), None, "narrow"),
        P(("parts", "wide"), None, "narrow"),
        P(("parts", "wide"), None, "narrow"),
        P(("parts", "wide"), "narrow", None, None),
        P(("parts", "wide"), "narrow", None, None),
        P(("parts", "wide")),
        P("parts"),
        P("parts"),
    )
    return jax.shard_map(
        shards,
        mesh=mesh,
        in_specs=placed,
        out_specs=P(("parts", "wide"), "narrow"),
        check_vma=False,
    )
```
